32 devices in a mesh: dp: 16 (over z, x, core), tensor: 2 (over y).
Axes of the slice: x: 2, y: 2, z: 4, core: 2. Of those that a mesh axis runs over, the one named last changes fastest.
Arguments:
- tokens: bfloat16 [16384, 1024], P(('dp', 'tensor')), may hold values from -6 to 6
- cotangent: bfloat16 [16384, 1024], P(('dp', 'tensor')), may hold values from -6 to 6
- sequence_lengths: int32 [64], replicated, may hold values from 0 to 1024, as said below
- sequence_group: int32 [64], replicated, may hold values from 0 to 15
- sequence_offset: int32 [64], replicated, may hold values from 0 to 15, as said below
- mixer_gain: bfloat16 [1024], replicated, may hold values from 0.5 to 1.5
- query_weight: bfloat16 [1024, 512], P('dp', 'tensor'), may hold values from -0.1875 to 0.1875
- key_weight: bfloat16 [1024, 512], P('dp', 'tensor'), may hold values from -0.1875 to 0.1875
- value_weight: bfloat16 [1024, 1024], P('dp', 'tensor'), may hold values from -0.1875 to 0.1875
- output_gate: bfloat16 [1024, 1024], P('dp', 'tensor'), may hold values from -0.1875 to 0.1875
- output_weight: bfloat16 [1024, 1024], P('dp', 'tensor'), may hold values from -0.375 to 0.375
- decay_down: bfloat16 [1024, 16], replicated, may hold values from -0.1875 to 0.1875
- decay_up: bfloat16 [16, 512], replicated, may hold values from -1.5 to 1.5
- decay_bias: bfloat16 [512], replicated, may hold values from -2 to 6
- head_gain: bfloat16 [256], replicated, may hold values from 0.5 to 1.5
- feed_gain: bfloat16 [1024], replicated, may hold values from 0.5 to 1.5
- feed_gate: bfloat16 [1024, 2816], P('dp', 'tensor'), may hold values from -0.1875 to 0.1875
- feed_up: bfloat16 [1024, 2816], P('dp', 'tensor'), may hold values from -0.1875 to 0.1875
- feed_down: bfloat16 [1024, 2816], P('dp', 'tensor'), may hold values from -0.15625 to 0.15625
Outputs:
- output: bfloat16 [16384, 1024], P(('dp', 'tensor'))
- input_grad: float32 [16384, 1024], P(('dp', 'tensor'))
- mixer_gain_grad: float32 [1024], replicated
- query_weight_grad: float32 [1024, 512], P('dp', 'tensor')
- key_weight_grad: float32 [1024, 512], P('dp', 'tensor')
- value_weight_grad: float32 [1024, 1024], P('dp', 'tensor')
- output_gate_grad: float32 [1024, 1024], P('dp', 'tensor')
- output_weight_grad: float32 [1024, 1024], P('dp', 'tensor')
- decay_down_grad: float32 [1024, 16], replicated
- decay_up_grad: float32 [16, 512], replicated
- decay_bias_grad: float32 [512], replicated
- head_gain_grad: float32 [256], replicated
- feed_gain_grad: float32 [1024], replicated
- feed_gate_grad: float32 [1024, 2816], P('dp', 'tensor')
- feed_up_grad: float32 [1024, 2816], P('dp', 'tensor')
- feed_down_grad: float32 [1024, 2816], P('dp', 'tensor')
The draws below stay inside these ranges and needn't reach their ends.
Inputs may be any that keep to these rules, and one draw needn't show every extreme that they name: Record i is one sequence of sequence_lengths[i] tokens, held by index sequence_group[i] along dp and starting at span sequence_offset[i] of 64 tokens within that index's 1024 slots; a length of 0 marks an unused record. Each index along dp has 4 records and at least one live sequence; its live sequences, each rounded up to whole spans, are disjoint and lie within its 1024 slots, and one of them starts at span 0. Some index holds a single sequence of 1024 tokens. `sequence_offset`: an unused record has offset 0. Some index has a sequence that starts at its last span.
All inputs are finite; a program needn't handle non-finite values.
Results may differ from the reference program's by a relative error of at most 0.015.
Values may be sent and summed in bfloat16 or wider, within the bound.
No kernel may reach another device: no remote copies, remote signals or barrier semaphores. Data moves between devices by JAX's collectives and lax.ppermute only.
A program may use at most 192 MiB of HBM per device.

```python
import jax
import jax.numpy as jnp
from jax import lax

D = 1024
HEADS = 4
KDIM = 128
VDIM = 256
FF = 2816
LOWRANK = 16
SPAN = 64
SEQ_GRP = 4
GRP = 1024
KD = 512
VD = 1024
TOKENS = 16384
SEQS = 64


def sequence_layout(key):
    group_count = SEQS // SEQ_GRP
    span_count = GRP // SPAN
    middle = span_count // 2
    keys = jax.random.split(key, 6)
    live_count = jax.random.randint(keys[0], (group_count,), 1, SEQ_GRP + 1, dtype=jnp.int32)
    used = jax.random.randint(keys[1], (group_count,), middle + 1, span_count + 1, dtype=jnp.int32)
    shares = jax.random.randint(keys[2], (group_count, SEQ_GRP), 1, 9, dtype=jnp.int32)
    tails = jax.random.randint(keys[3], (group_count, SEQ_GRP), 1, SPAN + 1, dtype=jnp.int32)
    longest = jax.random.randint(keys[4], (), 0, group_count, dtype=jnp.int32)
    group_ids = jnp.arange(group_count, dtype=jnp.int32)
    special = group_ids == longest
    second = group_ids == (longest + 1) % group_count
    live_count = jnp.where(special, 1, live_count).astype(jnp.int32)
    used = jnp.where(special, span_count, used).astype(jnp.int32)
    tails = jnp.where(special[:, None], SPAN, tails).astype(jnp.int32)
    slots = jnp.arange(SEQ_GRP, dtype=jnp.int32)[None, :]
    active = slots < live_count[:, None]
    shares = jnp.where(active, shares, 0).astype(jnp.int32)
    total_share = jnp.sum(shares, axis=1, keepdims=True)
    after = jnp.cumsum(shares, axis=1).astype(jnp.int32)
    before = after - shares
    spare = (used - 1 - live_count)[:, None]
    start_compact = slots + spare * before // total_share
    end_compact = slots + 1 + spare * after // total_share
    start_span = start_compact + (start_compact >= middle).astype(jnp.int32)
    end_span = end_compact + (end_compact >= middle).astype(jnp.int32)
    lengths = jnp.where(active, (end_span - start_span - 1) * SPAN + tails, 0).astype(jnp.int32)
    offsets = jnp.where(active, start_span, 0).astype(jnp.int32)
    second_lengths = jnp.where(slots == 0, (span_count - 2) * SPAN + tails, jnp.where(slots == 1, tails, 0))
    second_offsets = jnp.where(slots == 1, span_count - 1, 0)
    lengths = jnp.where(second[:, None], second_lengths, lengths).astype(jnp.int32)
    offsets = jnp.where(second[:, None], second_offsets, offsets).astype(jnp.int32)
    owners = jnp.broadcast_to(group_ids[:, None], (group_count, SEQ_GRP))
    order = jax.random.permutation(keys[5], SEQS)
    return (lengths.reshape(SEQS)[order].astype(jnp.int32), owners.reshape(SEQS)[order].astype(jnp.int32), offsets.reshape(SEQS)[order].astype(jnp.int32))


def draw_sequence_lengths(key, part):
    layout = sequence_layout(key)
    return layout[0]


def draw_sequence_group(key, part):
    layout = sequence_layout(key)
    return layout[1]


def draw_sequence_offset(key, part):
    layout = sequence_layout(key)
    return layout[2]


def levels(stream_key, extent, cuts, low, high):
    def one(axis_at, parts):
        heights = jax.random.uniform(jax.random.fold_in(jax.random.fold_in(stream_key, 6), axis_at), (parts,), jnp.float32, low / len(cuts), high / len(cuts))
        return jnp.repeat(jnp.exp(heights), extent[axis_at] // parts).reshape((-1,) + (1,) * (len(extent) - axis_at - 1))

    loudness = one(*cuts[0])
    for cut in cuts[1:]:
        loudness = loudness * one(*cut)
    return loudness


def gaussian(stream_key, shape, scale, reach, cuts=(), kind=jnp.bfloat16):
    gain = levels(stream_key, shape, cuts, -0.22, 0.18) if cuts else 1.0
    result = jax.random.normal(stream_key, shape, jnp.float32) * scale * gain
    return jnp.minimum(jnp.maximum(result, -reach), reach).astype(kind)


def setup_inputs(seed: int = 0) -> dict:
    arg_keys = jax.random.split(jax.random.key(seed), 20)
    return {
        "tokens": gaussian(arg_keys[0], (TOKENS, D), 1.0, 6.0, ((0, 32),)),
        "cotangent": gaussian(arg_keys[1], (TOKENS, D), 1.0, 6.0, ((0, 32),)),
        "sequence_lengths": draw_sequence_lengths(jax.random.fold_in(arg_keys[19], 71), 0),
        "sequence_group": draw_sequence_group(jax.random.fold_in(arg_keys[19], 71), 0),
        "sequence_offset": draw_sequence_offset(jax.random.fold_in(arg_keys[19], 71), 0),
        "mixer_gain": jnp.clip(1.0 + 0.1 * jax.random.normal(arg_keys[5], (D,), jnp.float32), 0.5, 1.5).astype(jnp.bfloat16),
        "query_weight": gaussian(arg_keys[6], (D, KD), D ** -0.5, 0.1875, ((0, 16), (1, 2))),
        "key_weight": gaussian(arg_keys[7], (D, KD), D ** -0.5, 0.1875, ((0, 16), (1, 2))),
        "value_weight": gaussian(arg_keys[8], (D, VD), D ** -0.5, 0.1875, ((0, 16), (1, 2))),
        "output_gate": gaussian(arg_keys[9], (D, VD), D ** -0.5, 0.1875, ((0, 16), (1, 2))),
        "output_weight": gaussian(arg_keys[10], (D, VD), (VD // 4) ** -0.5, 0.375, ((0, 16), (1, 2))),
        "decay_down": gaussian(arg_keys[11], (D, LOWRANK), D ** -0.5, 0.1875),
        "decay_up": gaussian(arg_keys[12], (LOWRANK, KD), LOWRANK ** -0.5, 1.5),
        "decay_bias": jnp.clip(jax.random.uniform(arg_keys[13], (KD,), jnp.float32, -2.0, 6.0), -2.0, 6.0).astype(jnp.bfloat16),
        "head_gain": jnp.clip(1.0 + 0.1 * jax.random.normal(arg_keys[14], (VDIM,), jnp.float32), 0.5, 1.5).astype(jnp.bfloat16),
        "feed_gain": jnp.clip(1.0 + 0.1 * jax.random.normal(arg_keys[15], (D,), jnp.float32), 0.5, 1.5).astype(jnp.bfloat16),
        "feed_gate": gaussian(arg_keys[16], (D, FF), D ** -0.5, 0.1875, ((0, 16), (1, 2))),
        "feed_up": gaussian(arg_keys[17], (D, FF), D ** -0.5, 0.1875, ((0, 16), (1, 2))),
        "feed_down": gaussian(arg_keys[18], (D, FF), (FF // 2) ** -0.5, 0.15625, ((0, 16), (1, 2))),
    }


@jax.custom_vjp
def low(v):
    return lax.optimization_barrier(v.astype(jnp.bfloat16)).astype(jnp.float32)

@jax.custom_vjp
def low_back(v):
    return v

def low_keep(v):
    return (low(v), None)

def low_pass(kept, grad):
    return (grad,)

def back_keep(v):
    return (v, None)

def back_low(kept, grad):
    return (low(grad),)
low.defvjp(low_keep, low_pass)
low_back.defvjp(back_keep, back_low)
epsilon = 1e-06
head_epsilon = 1.0
gate_scale = 16.0
highest = lax.Precision.HIGHEST

def product(left, right):
    return jnp.dot(left, right, precision=highest, preferred_element_type=jnp.float32)

def rms_norm(values, norm_gain, floor_value=epsilon):
    inverse = lax.rsqrt(lax.optimization_barrier(jnp.mean(values * values, axis=-1, keepdims=True)) + floor_value)
    return values * inverse * norm_gain

def group_layout(sequence_lengths, sequence_group, sequence_offset, which_group, group_rows):
    span_count = group_rows // SPAN
    live_record = (sequence_group == which_group) & (sequence_lengths > 0)
    start_row = sequence_offset * SPAN
    places = jnp.arange(group_rows, dtype=jnp.int32)[:, None]
    covered = live_record[None, :] & (places >= start_row[None, :]) & (places < (start_row + sequence_lengths)[None, :])
    live_mask = jnp.any(covered, axis=1).astype(jnp.float32)
    span_ids = jnp.arange(span_count, dtype=jnp.int32)[:, None]
    restart = jnp.any(live_record[None, :] & (span_ids == sequence_offset[None, :]), axis=1).astype(jnp.float32)
    return (live_mask, restart)

def span_mixer(queries, key_rows, values, decays, restart):
    length, head_count, key_size = queries.shape
    value_size = values.shape[2]
    spans = restart.shape[0]
    span_rows = length // spans
    block_shape = (spans, span_rows, head_count, key_size)
    query_blocks = queries.reshape(block_shape)
    key_blocks = key_rows.reshape(block_shape)
    value_blocks = values.reshape((spans, span_rows, head_count, value_size))
    within = jnp.cumsum(decays.reshape(block_shape), axis=1)
    last_sum = within[:, -1]
    span_add = jnp.einsum('nchk,nchv->nhkv', key_blocks * jnp.exp(last_sum[:, None] - within), value_blocks, precision=highest)

    def advance(memory, entries):
        fading, addend, keep_flag = entries
        entering = memory * keep_flag
        return (fading[:, :, None] * entering + addend, entering)
    start_memory = jnp.zeros((head_count, key_size, value_size), jnp.float32)
    _, entering = lax.scan(advance, start_memory, (jnp.exp(last_sum), span_add, 1.0 - restart))
    carried = jnp.einsum('nchk,nhkv->nchv', query_blocks * jnp.exp(within), entering, precision=highest)
    causal_grid = jnp.arange(span_rows, dtype=jnp.int32)[:, None] >= jnp.arange(span_rows, dtype=jnp.int32)[None, :]

    def local_block(entries):
        block_query, block_key, block_value, block_decay = entries
        spread = block_decay[:, :, None] - block_decay[:, None, :]
        causal = causal_grid[None, :, :, None, None]
        fading = jnp.where(causal, jnp.exp(jnp.where(causal, spread, 0.0)), 0.0)
        scores = jnp.einsum('bihk,bjhk,bijhk->bhij', block_query, block_key, fading, precision=highest)
        return jnp.einsum('bhij,bjhv->bihv', scores, block_value, precision=highest)
    pair_count = spans // 2
    pair_shape = (pair_count, 2) + block_shape[1:]
    inside = lax.map(jax.checkpoint(local_block), (query_blocks.reshape(pair_shape), key_blocks.reshape(pair_shape), value_blocks.reshape((pair_count, 2, span_rows, head_count, value_size)), within.reshape(pair_shape)))
    combined = carried + inside.reshape((spans, span_rows, head_count, value_size))
    return combined.reshape((length, head_count, value_size))

def group_forward(params, group_tokens, live_mask, restart):
    mixer_gain, query_weight, key_weight, value_weight, output_gate, output_weight, decay_down, decay_up, decay_bias, head_gain, feed_gain, feed_gate, feed_up, feed_down = params
    row_total = group_tokens.shape[0]
    normed = low(rms_norm(group_tokens, mixer_gain))
    queries = low_back(product(normed, query_weight))
    key_rows = low_back(product(normed, key_weight))
    values = low_back(product(normed, value_weight))
    gating = low_back(product(normed, output_gate))
    latent = product(normed, decay_down)
    decays = jax.nn.log_sigmoid(product(latent, decay_up) + decay_bias) / gate_scale
    mixture = span_mixer(queries.reshape(row_total, HEADS, KDIM), key_rows.reshape(row_total, HEADS, KDIM), values.reshape(row_total, HEADS, VDIM), decays.reshape(row_total, HEADS, KDIM), restart)
    head_out = rms_norm(mixture, head_gain, head_epsilon).reshape(row_total, HEADS * VDIM)
    gated = low(head_out * jax.nn.silu(gating) * live_mask[:, None])
    attended = low_back(product(gated, output_weight.T))
    middle = group_tokens + attended
    normed_mid = low(rms_norm(middle, feed_gain))
    gate_part = low_back(product(normed_mid, feed_gate))
    up_part = low_back(product(normed_mid, feed_up))
    hidden = low(jax.nn.silu(gate_part) * up_part)
    fed = low_back(product(hidden, feed_down.T))
    return middle + fed

def reference(tokens, cotangent, sequence_lengths, sequence_group, sequence_offset, mixer_gain, query_weight, key_weight, value_weight, output_gate, output_weight, decay_down, decay_up, decay_bias, head_gain, feed_gain, feed_gate, feed_up, feed_down):
    params = tuple((weight_arg.astype(jnp.float32) for weight_arg in (mixer_gain, query_weight, key_weight, value_weight, output_gate, output_weight, decay_down, decay_up, decay_bias, head_gain, feed_gain, feed_gate, feed_up, feed_down)))
    group_count = tokens.shape[0] // GRP
    token_values = tokens.astype(jnp.float32).reshape(group_count, GRP, D)
    upstream = cotangent.astype(jnp.float32).reshape(group_count, GRP, D)
    group_numbers = jnp.arange(group_count, dtype=jnp.int32)

    def layer(weights, inputs):

        def one_group(carry, entries):
            group_tokens, which_group = entries
            live_mask, restart = group_layout(sequence_lengths, sequence_group, sequence_offset, which_group, GRP)
            return (carry, group_forward(weights, group_tokens, live_mask, restart))
        _, results = lax.scan(jax.checkpoint(one_group), jnp.zeros((), jnp.float32), (inputs, group_numbers))
        return results
    results, layer_back = jax.vjp(layer, params, token_values)
    weight_grads, token_grads = layer_back(upstream)
    grad_mixer_gain, grad_query, grad_key, grad_value, grad_gate, grad_output, grad_down, grad_up, grad_bias, grad_head, grad_feed_gain, grad_feed_gate, grad_feed_up, grad_feed_down = weight_grads
    output = results.reshape(tokens.shape).astype(jnp.bfloat16)
    input_grad = token_grads.reshape(tokens.shape)
    return (output, input_grad, grad_mixer_gain, grad_query, grad_key, grad_value, grad_gate, grad_output, grad_down, grad_up, grad_bias, grad_head, grad_feed_gain, grad_feed_gate, grad_feed_up, grad_feed_down)
```

```python
import functools

import jax
import jax.numpy as jnp
import numpy as np
from jax import lax
from jax.experimental import pallas as pl
from jax.experimental.pallas import tpu as pltpu
from jax.sharding import PartitionSpec as P

KDIM = 128
VDIM = 256
SPAN = 64
LEVELS = 6
KINDS = LEVELS + 2
STEP_SPANS = 2

epsilon = 1e-06
head_epsilon = 1.0
gate_scale = 16.0
highest = lax.Precision.HIGHEST
f32 = jnp.float32
bf16 = jnp.bfloat16


def rms_forward(values, norm_gain, floor_value=epsilon):
    inverse = lax.rsqrt(jnp.mean(values * values, axis=-1, keepdims=True) + floor_value)
    return (values * inverse * norm_gain, inverse)


def rms_backward(values, inverse, norm_gain, upstream):
    scaled = upstream * norm_gain
    inner = jnp.mean(scaled * values, axis=-1, keepdims=True)
    grad_values = inverse * scaled - values * (inverse * inverse * inverse) * inner
    grad_gain = jnp.sum(upstream * values * inverse, axis=0)
    return (grad_values, grad_gain)


def group_layout(sequence_lengths, sequence_group, sequence_offset, which_group, places, span_count):
    live_record = (sequence_group == which_group) & (sequence_lengths > 0)
    start_row = sequence_offset * SPAN
    covered = (
        live_record[None, :]
        & (places >= start_row[None, :])
        & (places < (start_row + sequence_lengths)[None, :])
    )
    live_mask = jnp.any(covered, axis=1).astype(f32)
    span_ids = jnp.arange(span_count, dtype=jnp.int32)[:, None]
    restart = jnp.any(live_record[None, :] & (span_ids == sequence_offset[None, :]), axis=1)
    return (live_mask, restart.astype(jnp.int32))


def nn(left, right):
    return lax.dot_general(left, right, (((1,), (0,)), ((), ())), preferred_element_type=f32)


def nt(left, right):
    return lax.dot_general(left, right, (((1,), (1,)), ((), ())), preferred_element_type=f32)


def tn(left, right):
    return lax.dot_general(left, right, (((0,), (0,)), ((), ())), preferred_element_type=f32)


def decay_sums():
    rows = np.arange(SPAN)[:, None]
    cols = np.arange(SPAN)[None, :]
    blocks = [cols <= rows]
    for level in range(LEVELS):
        half = 1 << level
        edge = (rows // (2 * half)) * (2 * half) + half
        right = rows >= edge
        blocks.append(np.where(right, (cols >= edge) & (cols <= rows), (cols > rows) & (cols < edge)))
    blocks.append(cols > rows)
    return np.concatenate(blocks, axis=0).astype(np.float32)


def pair_levels():
    rows = lax.broadcasted_iota(jnp.int32, (SPAN, SPAN), 0)
    cols = lax.broadcasted_iota(jnp.int32, (SPAN, SPAN), 1)
    apart = rows ^ cols
    later = rows > cols
    masks = [later & (lax.shift_right_logical(apart, level) == 1) for level in range(LEVELS)]
    return masks, rows == cols


def span_factors(z_part, sums):
    decays = (jnp.minimum(z_part, 0.0) - jnp.log1p(jnp.exp(-jnp.abs(z_part)))) * (1.0 / gate_scale)
    high = decays.astype(bf16)
    low = (decays - high.astype(f32)).astype(bf16)
    return jnp.exp(nn(sums, jnp.concatenate([high, low], axis=0)))


def span_scores(queries, keys, factors, masks, diagonal):
    scores = jnp.where(diagonal, nt(queries.astype(bf16), keys.astype(bf16)), 0.0)
    query_levels = []
    key_levels = []
    for level in range(LEVELS):
        factor = factors[(level + 1) * SPAN : (level + 2) * SPAN]
        query_level = (queries * factor).astype(bf16)
        key_level = (keys * factor).astype(bf16)
        scores = jnp.where(masks[level], nt(query_level, key_level), scores)
        query_levels.append(query_level)
        key_levels.append(key_level)
    return scores, query_levels, key_levels


def forward_kernel(heads, scal, projected, z, live, gain, sums, gated, mixture, states, state):
    step = pl.program_id(0)
    key_width = heads * KDIM
    value_width = heads * VDIM

    @pl.when(step == 0)
    def _():
        state[...] = jnp.zeros_like(state)

    masks, diagonal = pair_levels()
    head_gain = gain[...]
    for part in range(STEP_SPANS):
        rows = slice(part * SPAN, (part + 1) * SPAN)
        factors_all = span_factors(z[rows, :], sums[...])
        keep = jnp.where(scal[1 + step * STEP_SPANS + part] == 0, 1.0, 0.0)
        for head in range(heads):
            keys_at = slice(head * KDIM, (head + 1) * KDIM)
            queries = projected[rows, keys_at]
            keys = projected[rows, key_width + head * KDIM : key_width + (head + 1) * KDIM]
            value_at = 2 * key_width + head * VDIM
            values = projected[rows, value_at : value_at + VDIM].astype(bf16)
            gating = projected[rows, value_at + value_width : value_at + value_width + VDIM]
            factors = factors_all[:, keys_at]
            scores, _, _ = span_scores(queries, keys, factors, masks, diagonal)
            entering = state[head] * keep
            entering_low = entering.astype(bf16)
            states[part, head] = entering_low
            whole = factors[:SPAN]
            after = factors[(KINDS - 1) * SPAN :]
            mixed = nn(scores.astype(bf16), values) + nt(
                (queries * whole).astype(bf16), entering_low
            )
            state[head] = entering * whole[SPAN - 1 :] + tn(values, (keys * after).astype(bf16))
            value_cols = slice(head * VDIM, (head + 1) * VDIM)
            mixture[rows, value_cols] = mixed
            inverse = lax.rsqrt(jnp.mean(mixed * mixed, axis=-1, keepdims=True) + head_epsilon)
            silu = gating * jax.nn.sigmoid(gating)
            gated[rows, value_cols] = (mixed * inverse * head_gain * silu * live[rows, :]).astype(bf16)


def backward_kernel(
    heads,
    scal,
    projected,
    z,
    live,
    gain,
    sums,
    mixture,
    states,
    grad_gated,
    grad_projected,
    grad_z,
    grad_gain,
    grad_state,
):
    step = pl.program_id(0)
    natural = pl.num_programs(0) - 1 - step
    key_width = heads * KDIM
    value_width = heads * VDIM

    @pl.when(step == 0)
    def _():
        grad_state[...] = jnp.zeros_like(grad_state)
        grad_gain[...] = jnp.zeros_like(grad_gain)

    masks, diagonal = pair_levels()
    head_gain = gain[...]
    last_row = lax.broadcasted_iota(jnp.int32, (SPAN, KDIM), 0) == SPAN - 1
    for part in reversed(range(STEP_SPANS)):
        rows = slice(part * SPAN, (part + 1) * SPAN)
        z_part = z[rows, :]
        factors_all = span_factors(z_part, sums[...])
        keep = jnp.where(scal[1 + natural * STEP_SPANS + part] == 0, 1.0, 0.0)
        live_part = live[rows, :]
        exponents = []
        for head in range(heads):
            keys_at = slice(head * KDIM, (head + 1) * KDIM)
            key_cols = slice(key_width + head * KDIM, key_width + (head + 1) * KDIM)
            value_at = 2 * key_width + head * VDIM
            value_cols = slice(value_at, value_at + VDIM)
            gate_cols = slice(value_at + value_width, value_at + value_width + VDIM)
            mixed_cols = slice(head * VDIM, (head + 1) * VDIM)
            queries = projected[rows, keys_at]
            keys = projected[rows, key_cols]
            values = projected[rows, value_cols].astype(bf16)
            gating = projected[rows, gate_cols]
            factors = factors_all[:, keys_at]
            scores, query_levels, key_levels = span_scores(queries, keys, factors, masks, diagonal)
            scores_low = scores.astype(bf16)
            whole = factors[:SPAN]
            after = factors[(KINDS - 1) * SPAN :]

            mixed = mixture[rows, mixed_cols]
            inverse = lax.rsqrt(jnp.mean(mixed * mixed, axis=-1, keepdims=True) + head_epsilon)
            unit = mixed * inverse
            sigmoid = jax.nn.sigmoid(gating)
            silu = gating * sigmoid
            upstream = grad_gated[rows, mixed_cols] * live_part
            grad_projected[rows, gate_cols] = (
                upstream * unit * head_gain * (sigmoid + silu * (1.0 - sigmoid))
            ).astype(bf16)
            normed_back = upstream * silu
            gain_part = normed_back * unit
            grad_gain[...] += jnp.sum(gain_part.reshape(SPAN // 8, 8, VDIM), axis=0)
            scaled = normed_back * head_gain
            inner = jnp.mean(scaled * unit, axis=-1, keepdims=True)
            grad_mixed = (inverse * (scaled - unit * inner)).astype(bf16)

            entering = states[part, head]
            leaving = grad_state[head]
            leaving_low = leaving.astype(bf16)
            grad_scores = nt(grad_mixed, values)
            after_keys = (keys * after).astype(bf16)
            whole_queries = (queries * whole).astype(bf16)
            grad_projected[rows, value_cols] = (
                tn(scores_low, grad_mixed) + nt(after_keys, leaving_low)
            ).astype(bf16)
            grad_queries = whole * nn(grad_mixed, entering)
            grad_keys = after * nn(values, leaving_low)
            fading = whole[SPAN - 1 :]
            last_sum = fading * jnp.sum(entering.astype(f32) * leaving, axis=0, keepdims=True)
            exponents_head = [queries * grad_queries + jnp.where(last_row, last_sum, 0.0)]
            last_exponent = keys * grad_keys
            for level in range(LEVELS):
                factor = factors[(level + 1) * SPAN : (level + 2) * SPAN]
                level_back = jnp.where(masks[level], grad_scores, 0.0).astype(bf16)
                query_part = factor * nn(level_back, key_levels[level])
                key_part = factor * tn(level_back, query_levels[level])
                grad_queries += query_part
                grad_keys += key_part
                exponents_head.append(queries * query_part + keys * key_part)
            exponents_head.append(last_exponent)
            same = jnp.sum(jnp.where(diagonal, grad_scores, 0.0), axis=1, keepdims=True)
            grad_projected[rows, keys_at] = (grad_queries + same * keys).astype(bf16)
            grad_projected[rows, key_cols] = (grad_keys + same * queries).astype(bf16)
            exponents.append(jnp.concatenate(exponents_head, axis=0).astype(bf16))
            grad_state[head] = keep * (leaving * fading + tn(grad_mixed, whole_queries))
        grad_decays = tn(sums[:, :SPAN], jnp.concatenate(exponents, axis=1))
        grad_z[rows, :] = grad_decays * jax.nn.sigmoid(-z_part) * (1.0 / gate_scale)


def mixer_specs(length, projected_width, key_width, value_width, reverse):
    steps = length // (SPAN * STEP_SPANS)
    step_rows = SPAN * STEP_SPANS
    heads = key_width // KDIM

    def natural(step):
        return steps - 1 - step if reverse else step

    def by_rows(step, scal):
        return (lax.rem(natural(step) + scal[0] * (steps // 2), steps), 0)

    def whole(step, scal):
        return (0, 0)

    return dict(
        steps=steps,
        projected=pl.BlockSpec((step_rows, projected_width), by_rows),
        z=pl.BlockSpec((step_rows, key_width), by_rows),
        live=pl.BlockSpec((step_rows, 1), by_rows),
        gain=pl.BlockSpec((1, VDIM), whole),
        sums=pl.BlockSpec((KINDS * SPAN, 2 * SPAN), whole),
        values=pl.BlockSpec((step_rows, value_width), by_rows),
        states=pl.BlockSpec(
            (STEP_SPANS, heads, VDIM, KDIM), lambda step, scal: (natural(step), 0, 0, 0)
        ),
        gain_grad=pl.BlockSpec((8, VDIM), whole),
    )


def mixer_forward(scal, projected, z, live, gain, sums):
    length, projected_width = projected.shape
    key_width = z.shape[1]
    heads = key_width // KDIM
    value_width = heads * VDIM
    spans = length // SPAN
    specs = mixer_specs(length, projected_width, key_width, value_width, False)
    return pl.pallas_call(
        functools.partial(forward_kernel, heads),
        grid_spec=pltpu.PrefetchScalarGridSpec(
            num_scalar_prefetch=1,
            grid=(specs["steps"],),
            in_specs=[specs[name] for name in ("projected", "z", "live", "gain", "sums")],
            out_specs=[specs[name] for name in ("values", "values", "states")],
            scratch_shapes=[pltpu.VMEM((heads, VDIM, KDIM), f32)],
        ),
        out_shape=[
            jax.ShapeDtypeStruct((length, value_width), bf16),
            jax.ShapeDtypeStruct((length, value_width), f32),
            jax.ShapeDtypeStruct((spans, heads, VDIM, KDIM), bf16),
        ],
        compiler_params=pltpu.CompilerParams(vmem_limit_bytes=40 * 1024 * 1024),
        cost_estimate=pl.CostEstimate(
            flops=10**10, bytes_accessed=15 * 10**6, transcendentals=4 * 10**6
        ),
        name="mixer_forward",
    )(scal, projected, z, live, gain, sums)


def mixer_backward(scal, projected, z, live, gain, sums, mixture, states, grad_gated):
    length, projected_width = projected.shape
    key_width = z.shape[1]
    heads = key_width // KDIM
    value_width = heads * VDIM
    specs = mixer_specs(length, projected_width, key_width, value_width, True)
    names = ("projected", "z", "live", "gain", "sums", "values", "states", "values")
    return pl.pallas_call(
        functools.partial(backward_kernel, heads),
        grid_spec=pltpu.PrefetchScalarGridSpec(
            num_scalar_prefetch=1,
            grid=(specs["steps"],),
            in_specs=[specs[name] for name in names],
            out_specs=[specs[name] for name in ("projected", "z", "gain_grad")],
            scratch_shapes=[pltpu.VMEM((heads, VDIM, KDIM), f32)],
        ),
        out_shape=[
            jax.ShapeDtypeStruct((length, projected_width), bf16),
            jax.ShapeDtypeStruct((length, key_width), f32),
            jax.ShapeDtypeStruct((8, VDIM), f32),
        ],
        compiler_params=pltpu.CompilerParams(vmem_limit_bytes=40 * 1024 * 1024),
        cost_estimate=pl.CostEstimate(
            flops=25 * 10**9, bytes_accessed=20 * 10**6, transcendentals=4 * 10**6
        ),
        name="mixer_backward",
    )(scal, projected, z, live, gain, sums, mixture, states, grad_gated)


def swap_tensor(values):
    return lax.ppermute(values, "tensor", [(0, 1), (1, 0)])


def butterfly_sum(values):
    total = values + swap_tensor(values)
    count = lax.axis_size("dp")
    reach = 1
    while reach < count:
        total = total + lax.ppermute(total, "dp", [(i, i ^ reach) for i in range(count)])
        reach *= 2
    return total


def on_device(
    tokens,
    cotangent,
    sequence_lengths,
    sequence_group,
    sequence_offset,
    mixer_gain,
    query_weight,
    key_weight,
    value_weight,
    output_gate,
    output_weight,
    decay_down,
    decay_up,
    decay_bias,
    head_gain,
    feed_gain,
    feed_gate,
    feed_up,
    feed_down,
):
    which_group = lax.axis_index("dp")
    half_index = lax.axis_index("tensor")
    own = tokens.shape[0]
    group_rows = own * 2
    key_width = query_weight.shape[1]
    value_width = value_weight.shape[1]
    feed_width = feed_gate.shape[1]
    places = (jnp.arange(group_rows, dtype=jnp.int32) + half_index * own) % group_rows
    live_mask, restart = group_layout(
        sequence_lengths,
        sequence_group,
        sequence_offset,
        which_group,
        places[:, None],
        group_rows // SPAN,
    )
    live = live_mask[:, None]
    scal = jnp.concatenate([half_index.astype(jnp.int32)[None], restart])
    sums = jnp.asarray(np.tile(decay_sums(), (1, 2)), bf16)
    gain_head = head_gain.astype(f32)[None, :]

    joined = lax.all_gather(
        jnp.concatenate([query_weight, key_weight, value_weight, output_gate], axis=1),
        "dp",
        axis=0,
        tiled=True,
    )
    feed_all = lax.all_gather(
        jnp.concatenate([feed_gate, feed_up, feed_down, output_weight], axis=1),
        "dp",
        axis=0,
        tiled=True,
    )
    gate_up_full = feed_all[:, : 2 * feed_width]
    feed_down_full = feed_all[:, 2 * feed_width : 3 * feed_width]
    output_full = feed_all[:, 3 * feed_width :]

    gain_in = mixer_gain.astype(f32)
    token_values = tokens.astype(f32)
    normed_in, inverse_in = rms_forward(token_values, gain_in)
    normed_low = normed_in.astype(bf16)
    normed_all = jnp.concatenate([normed_low, swap_tensor(normed_low)], axis=0)
    cotangent_all = jnp.concatenate([cotangent, swap_tensor(cotangent)], axis=0)
    projected = nn(normed_all, joined)
    latent = nn(normed_all, decay_down)
    up_local = lax.dynamic_slice_in_dim(decay_up, half_index * key_width, key_width, 1).astype(f32)
    bias_local = lax.dynamic_slice_in_dim(decay_bias, half_index * key_width, key_width, 0)
    z = jnp.dot(latent, up_local, precision=highest) + bias_local.astype(f32)
    gated, mixture, states = mixer_forward(scal, projected, z, live, gain_head, sums)

    partial = nt(gated, output_full).astype(bf16)
    attended = partial[:own].astype(f32) + swap_tensor(partial[own:]).astype(f32)
    middle = token_values + attended
    gain_mid = feed_gain.astype(f32)
    normed_mid, inverse_mid = rms_forward(middle, gain_mid)
    mid_low = normed_mid.astype(bf16)
    mid_all = jnp.concatenate([mid_low, swap_tensor(mid_low)], axis=0)
    both = nn(mid_all, gate_up_full)
    gate_part = both[:, :feed_width]
    up_part = both[:, feed_width:]
    sigmoid_gate = jax.nn.sigmoid(gate_part)
    silu_gate = gate_part * sigmoid_gate
    hidden_low = (silu_gate * up_part).astype(bf16)
    fed_part = nt(hidden_low, feed_down_full).astype(bf16)
    fed = fed_part[:own].astype(f32) + swap_tensor(fed_part[own:]).astype(f32)
    output = (middle + fed).astype(bf16)

    upstream = cotangent.astype(f32)
    grad_hidden = nn(cotangent_all, feed_down_full)
    grad_gate_low = (
        grad_hidden * up_part * (sigmoid_gate + silu_gate * (1.0 - sigmoid_gate))
    ).astype(bf16)
    grad_up_low = (grad_hidden * silu_gate).astype(bf16)
    grad_both = jnp.concatenate([grad_gate_low, grad_up_low], axis=1)
    mid_part = nt(grad_both, gate_up_full).astype(bf16)
    grad_normed_mid = mid_part[:own].astype(f32) + swap_tensor(mid_part[own:]).astype(f32)
    grad_mid_in, grad_feed_gain = rms_backward(middle, inverse_mid, gain_mid, grad_normed_mid)
    grad_middle = upstream + grad_mid_in
    attended_low = grad_middle.astype(bf16)
    attended_all = jnp.concatenate([attended_low, swap_tensor(attended_low)], axis=0)
    feed_grads = jnp.concatenate(
        [
            tn(mid_all, grad_both).astype(bf16),
            tn(cotangent_all, hidden_low).astype(bf16),
            tn(attended_all, gated).astype(bf16),
        ],
        axis=1,
    )
    grad_gated = nn(attended_all, output_full)
    grad_gated, feed_grads = lax.optimization_barrier((grad_gated, feed_grads))
    grad_projected, grad_z, grad_gain_rows = mixer_backward(
        scal, projected, z, live, gain_head, sums, mixture, states, grad_gated
    )
    feed_sum = lax.psum_scatter(feed_grads, "dp", scatter_dimension=0, tiled=True).astype(f32)
    grad_joined = tn(normed_all, grad_projected).astype(bf16)
    joined_sum = lax.psum_scatter(grad_joined, "dp", scatter_dimension=0, tiled=True).astype(f32)

    grad_latent = lax.dot_general(
        grad_z, up_local, (((1,), (1,)), ((), ())), precision=highest, preferred_element_type=f32
    )
    grad_up_local = lax.dot_general(
        latent, grad_z, (((0,), (0,)), ((), ())), precision=highest, preferred_element_type=f32
    )
    grad_bias_local = jnp.sum(grad_z, axis=0)
    latent_high = grad_latent.astype(bf16)
    latent_rest = (grad_latent - latent_high.astype(f32)).astype(bf16)
    grad_down_parts = tn(normed_all, jnp.concatenate([latent_high, latent_rest], axis=1))
    low_rank = decay_down.shape[1]
    grad_decay_down = grad_down_parts[:, :low_rank] + grad_down_parts[:, low_rank:]
    from_latent = nt(latent_high, decay_down) + nt(latent_rest, decay_down)
    normed_part = (nt(grad_projected, joined) + from_latent).astype(bf16)
    grad_normed = normed_part[:own].astype(f32) + swap_tensor(normed_part[own:]).astype(f32)
    grad_in_part, grad_mixer_gain = rms_backward(token_values, inverse_in, gain_in, grad_normed)
    input_grad = grad_middle + grad_in_part

    up_full = lax.dynamic_update_slice_in_dim(
        jnp.zeros(decay_up.shape, f32), grad_up_local, half_index * key_width, 1
    )
    bias_full = lax.dynamic_update_slice_in_dim(
        jnp.zeros(decay_bias.shape, f32), grad_bias_local, half_index * key_width, 0
    )
    small = (
        grad_mixer_gain,
        grad_decay_down,
        up_full,
        bias_full,
        jnp.sum(grad_gain_rows, axis=0),
        grad_feed_gain,
    )
    flat = butterfly_sum(jnp.concatenate([part.reshape(-1, 128) for part in small], axis=0))
    small_sums = []
    row = 0
    for part in small:
        taken = part.size // 128
        small_sums.append(flat[row : row + taken].reshape(part.shape))
        row += taken
    return (
        output,
        input_grad,
        small_sums[0],
        joined_sum[:, :key_width],
        joined_sum[:, key_width : 2 * key_width],
        joined_sum[:, 2 * key_width : 2 * key_width + value_width],
        joined_sum[:, 2 * key_width + value_width :],
        feed_sum[:, 3 * feed_width :],
        small_sums[1],
        small_sums[2],
        small_sums[3],
        small_sums[4],
        small_sums[5],
        feed_sum[:, :feed_width],
        feed_sum[:, feed_width : 2 * feed_width],
        feed_sum[:, 2 * feed_width : 3 * feed_width],
    )


def solution(mesh):
    rows = P(("dp", "tensor"), None)
    weight = P("dp", "tensor")
    return jax.shard_map(
        on_device,
        mesh=mesh,
        in_specs=(rows, rows, P(), P(), P(), P())
        + (weight,) * 5
        + (P(), P(), P(), P(), P())
        + (weight,) * 3,
        out_specs=(rows, rows, P()) + (weight,) * 5 + (P(),) * 5 + (weight,) * 3,
        check_vma=False,
    )
```

```python
import functools

import jax
import jax.numpy as jnp
import numpy as np
from jax import lax
from jax.experimental import pallas as pl
from jax.experimental.pallas import tpu as pltpu
from jax.sharding import PartitionSpec as P

KDIM = 128
VDIM = 256
SPAN = 64
LEVELS = 6
KINDS = LEVELS + 2
STEP_SPANS = 2

epsilon = 1e-06
head_epsilon = 1.0
gate_scale = 16.0
highest = lax.Precision.HIGHEST
f32 = jnp.float32
bf16 = jnp.bfloat16


def rms_forward(values, norm_gain, floor_value=epsilon):
    inverse = lax.rsqrt(jnp.mean(values * values, axis=-1, keepdims=True) + floor_value)
    return (values * inverse * norm_gain, inverse)


def rms_backward(values, inverse, norm_gain, upstream):
    scaled = upstream * norm_gain
    inner = jnp.mean(scaled * values, axis=-1, keepdims=True)
    grad_values = inverse * scaled - values * (inverse * inverse * inverse) * inner
    grad_gain = jnp.sum(upstream * values * inverse, axis=0)
    return (grad_values, grad_gain)


def group_layout(sequence_lengths, sequence_group, sequence_offset, which_group, places, span_count):
    live_record = (sequence_group == which_group) & (sequence_lengths > 0)
    start_row = sequence_offset * SPAN
    covered = (
        live_record[None, :]
        & (places >= start_row[None, :])
        & (places < (start_row + sequence_lengths)[None, :])
    )
    live_mask = jnp.any(covered, axis=1).astype(f32)
    span_ids = jnp.arange(span_count, dtype=jnp.int32)[:, None]
    restart = jnp.any(live_record[None, :] & (span_ids == sequence_offset[None, :]), axis=1)
    return (live_mask, restart.astype(jnp.int32))


def nn(left, right):
    return lax.dot_general(left, right, (((1,), (0,)), ((), ())), preferred_element_type=f32)


def nt(left, right):
    return lax.dot_general(left, right, (((1,), (1,)), ((), ())), preferred_element_type=f32)


def tn(left, right):
    return lax.dot_general(left, right, (((0,), (0,)), ((), ())), preferred_element_type=f32)


def decay_sums():
    rows = np.arange(SPAN)[:, None]
    cols = np.arange(SPAN)[None, :]
    blocks = [cols <= rows]
    for level in range(LEVELS):
        half = 1 << level
        edge = (rows // (2 * half)) * (2 * half) + half
        right = rows >= edge
        blocks.append(np.where(right, (cols >= edge) & (cols <= rows), (cols > rows) & (cols < edge)))
    blocks.append(cols > rows)
    return np.concatenate(blocks, axis=0).astype(np.float32)


def pair_levels():
    rows = lax.broadcasted_iota(jnp.int32, (SPAN, SPAN), 0)
    cols = lax.broadcasted_iota(jnp.int32, (SPAN, SPAN), 1)
    apart = rows ^ cols
    later = rows > cols
    masks = [later & (lax.shift_right_logical(apart, level) == 1) for level in range(LEVELS)]
    return masks, rows == cols


def span_factors(z_part, sums):
    decays = (jnp.minimum(z_part, 0.0) - jnp.log1p(jnp.exp(-jnp.abs(z_part)))) * (1.0 / gate_scale)
    high = decays.astype(bf16)
    low = (decays - high.astype(f32)).astype(bf16)
    return jnp.exp(nn(sums, jnp.concatenate([high, low], axis=0)))


def span_scores(queries, keys, factors, masks, diagonal):
    scores = jnp.where(diagonal, nt(queries.astype(bf16), keys.astype(bf16)), 0.0)
    query_levels = []
    key_levels = []
    for level in range(LEVELS):
        factor = factors[(level + 1) * SPAN : (level + 2) * SPAN]
        query_level = (queries * factor).astype(bf16)
        key_level = (keys * factor).astype(bf16)
        scores = jnp.where(masks[level], nt(query_level, key_level), scores)
        query_levels.append(query_level)
        key_levels.append(key_level)
    return scores, query_levels, key_levels


def forward_kernel(heads, scal, projected, z, live, gain, sums, gated, mixture, states, state):
    step = pl.program_id(0)
    key_width = heads * KDIM
    value_width = heads * VDIM

    @pl.when(step == 0)
    def _():
        state[...] = jnp.zeros_like(state)

    masks, diagonal = pair_levels()
    head_gain = gain[...]
    for part in range(STEP_SPANS):
        rows = slice(part * SPAN, (part + 1) * SPAN)
        factors_all = span_factors(z[rows, :], sums[...])
        keep = jnp.where(scal[1 + step * STEP_SPANS + part] == 0, 1.0, 0.0)
        for head in range(heads):
            keys_at = slice(head * KDIM, (head + 1) * KDIM)
            queries = projected[rows, keys_at].astype(f32)
            keys = projected[rows, key_width + head * KDIM : key_width + (head + 1) * KDIM].astype(f32)
            value_at = 2 * key_width + head * VDIM
            values = projected[rows, value_at : value_at + VDIM]
            gating = projected[rows, value_at + value_width : value_at + value_width + VDIM].astype(f32)
            factors = factors_all[:, keys_at]
            scores, _, _ = span_scores(queries, keys, factors, masks, diagonal)
            entering = state[head] * keep
            entering_low = entering.astype(bf16)
            states[part, head] = entering_low
            whole = factors[:SPAN]
            after = factors[(KINDS - 1) * SPAN :]
            mixed = nn(scores.astype(bf16), values) + nt(
                (queries * whole).astype(bf16), entering_low
            )
            state[head] = entering * whole[SPAN - 1 :] + tn(values, (keys * after).astype(bf16))
            value_cols = slice(head * VDIM, (head + 1) * VDIM)
            mixture[rows, value_cols] = mixed.astype(bf16)
            inverse = lax.rsqrt(jnp.mean(mixed * mixed, axis=-1, keepdims=True) + head_epsilon)
            silu = gating * jax.nn.sigmoid(gating)
            gated[rows, value_cols] = (mixed * inverse * head_gain * silu * live[rows, :]).astype(bf16)


def backward_kernel(
    heads,
    scal,
    projected,
    z,
    live,
    gain,
    sums,
    mixture,
    states,
    grad_gated,
    grad_projected,
    grad_z,
    grad_gain,
    grad_state,
):
    step = pl.program_id(0)
    natural = pl.num_programs(0) - 1 - step
    key_width = heads * KDIM
    value_width = heads * VDIM

    @pl.when(step == 0)
    def _():
        grad_state[...] = jnp.zeros_like(grad_state)
        grad_gain[...] = jnp.zeros_like(grad_gain)

    masks, diagonal = pair_levels()
    head_gain = gain[...]
    last_row = lax.broadcasted_iota(jnp.int32, (SPAN, KDIM), 0) == SPAN - 1
    for part in reversed(range(STEP_SPANS)):
        rows = slice(part * SPAN, (part + 1) * SPAN)
        z_part = z[rows, :]
        factors_all = span_factors(z_part, sums[...])
        keep = jnp.where(scal[1 + natural * STEP_SPANS + part] == 0, 1.0, 0.0)
        live_part = live[rows, :]
        exponents = []
        for head in range(heads):
            keys_at = slice(head * KDIM, (head + 1) * KDIM)
            key_cols = slice(key_width + head * KDIM, key_width + (head + 1) * KDIM)
            value_at = 2 * key_width + head * VDIM
            value_cols = slice(value_at, value_at + VDIM)
            gate_cols = slice(value_at + value_width, value_at + value_width + VDIM)
            mixed_cols = slice(head * VDIM, (head + 1) * VDIM)
            queries = projected[rows, keys_at].astype(f32)
            keys = projected[rows, key_cols].astype(f32)
            values = projected[rows, value_cols]
            gating = projected[rows, gate_cols].astype(f32)
            factors = factors_all[:, keys_at]
            scores, query_levels, key_levels = span_scores(queries, keys, factors, masks, diagonal)
            scores_low = scores.astype(bf16)
            whole = factors[:SPAN]
            after = factors[(KINDS - 1) * SPAN :]

            mixed = mixture[rows, mixed_cols].astype(f32)
            inverse = lax.rsqrt(jnp.mean(mixed * mixed, axis=-1, keepdims=True) + head_epsilon)
            unit = mixed * inverse
            sigmoid = jax.nn.sigmoid(gating)
            silu = gating * sigmoid
            upstream = grad_gated[rows, mixed_cols].astype(f32) * live_part
            grad_projected[rows, gate_cols] = (
                upstream * unit * head_gain * (sigmoid + silu * (1.0 - sigmoid))
            ).astype(bf16)
            normed_back = upstream * silu
            gain_part = normed_back * unit
            grad_gain[...] += jnp.sum(gain_part.reshape(SPAN // 8, 8, VDIM), axis=0)
            scaled = normed_back * head_gain
            inner = jnp.mean(scaled * unit, axis=-1, keepdims=True)
            grad_mixed = (inverse * (scaled - unit * inner)).astype(bf16)

            entering = states[part, head]
            leaving = grad_state[head]
            leaving_low = leaving.astype(bf16)
            grad_scores = nt(grad_mixed, values)
            after_keys = (keys * after).astype(bf16)
            whole_queries = (queries * whole).astype(bf16)
            grad_projected[rows, value_cols] = (
                tn(scores_low, grad_mixed) + nt(after_keys, leaving_low)
            ).astype(bf16)
            grad_queries = whole * nn(grad_mixed, entering)
            grad_keys = after * nn(values, leaving_low)
            fading = whole[SPAN - 1 :]
            last_sum = fading * jnp.sum(entering.astype(f32) * leaving, axis=0, keepdims=True)
            exponents_head = [queries * grad_queries + jnp.where(last_row, last_sum, 0.0)]
            last_exponent = keys * grad_keys
            for level in range(LEVELS):
                factor = factors[(level + 1) * SPAN : (level + 2) * SPAN]
                level_back = jnp.where(masks[level], grad_scores, 0.0).astype(bf16)
                query_part = factor * nn(level_back, key_levels[level])
                key_part = factor * tn(level_back, query_levels[level])
                grad_queries += query_part
                grad_keys += key_part
                exponents_head.append(queries * query_part + keys * key_part)
            exponents_head.append(last_exponent)
            same = jnp.sum(jnp.where(diagonal, grad_scores, 0.0), axis=1, keepdims=True)
            grad_projected[rows, keys_at] = (grad_queries + same * keys).astype(bf16)
            grad_projected[rows, key_cols] = (grad_keys + same * queries).astype(bf16)
            exponents.append(jnp.concatenate(exponents_head, axis=0).astype(bf16))
            grad_state[head] = keep * (leaving * fading + tn(grad_mixed, whole_queries))
        grad_decays = tn(sums[:, :SPAN], jnp.concatenate(exponents, axis=1))
        grad_z[rows, :] = grad_decays * jax.nn.sigmoid(-z_part) * (1.0 / gate_scale)


def mixer_specs(length, projected_width, key_width, value_width, reverse):
    steps = length // (SPAN * STEP_SPANS)
    step_rows = SPAN * STEP_SPANS
    heads = key_width // KDIM

    def natural(step):
        return steps - 1 - step if reverse else step

    def by_rows(step, scal):
        return (lax.rem(natural(step) + scal[0] * (steps // 2), steps), 0)

    def whole(step, scal):
        return (0, 0)

    return dict(
        steps=steps,
        projected=pl.BlockSpec((step_rows, projected_width), by_rows),
        z=pl.BlockSpec((step_rows, key_width), by_rows),
        live=pl.BlockSpec((step_rows, 1), by_rows),
        gain=pl.BlockSpec((1, VDIM), whole),
        sums=pl.BlockSpec((KINDS * SPAN, 2 * SPAN), whole),
        values=pl.BlockSpec((step_rows, value_width), by_rows),
        states=pl.BlockSpec(
            (STEP_SPANS, heads, VDIM, KDIM), lambda step, scal: (natural(step), 0, 0, 0)
        ),
        gain_grad=pl.BlockSpec((8, VDIM), whole),
    )


def mixer_forward(scal, projected, z, live, gain, sums):
    length, projected_width = projected.shape
    key_width = z.shape[1]
    heads = key_width // KDIM
    value_width = heads * VDIM
    spans = length // SPAN
    specs = mixer_specs(length, projected_width, key_width, value_width, False)
    return pl.pallas_call(
        functools.partial(forward_kernel, heads),
        grid_spec=pltpu.PrefetchScalarGridSpec(
            num_scalar_prefetch=1,
            grid=(specs["steps"],),
            in_specs=[specs[name] for name in ("projected", "z", "live", "gain", "sums")],
            out_specs=[specs[name] for name in ("values", "values", "states")],
            scratch_shapes=[pltpu.VMEM((heads, VDIM, KDIM), f32)],
        ),
        out_shape=[
            jax.ShapeDtypeStruct((length, value_width), bf16),
            jax.ShapeDtypeStruct((length, value_width), bf16),
            jax.ShapeDtypeStruct((spans, heads, VDIM, KDIM), bf16),
        ],
        compiler_params=pltpu.CompilerParams(vmem_limit_bytes=40 * 1024 * 1024),
        cost_estimate=pl.CostEstimate(
            flops=10**10, bytes_accessed=15 * 10**6, transcendentals=4 * 10**6
        ),
        name="mixer_forward",
    )(scal, projected, z, live, gain, sums)


def mixer_backward(scal, projected, z, live, gain, sums, mixture, states, grad_gated):
    length, projected_width = projected.shape
    key_width = z.shape[1]
    heads = key_width // KDIM
    value_width = heads * VDIM
    specs = mixer_specs(length, projected_width, key_width, value_width, True)
    names = ("projected", "z", "live", "gain", "sums", "values", "states", "values")
    return pl.pallas_call(
        functools.partial(backward_kernel, heads),
        grid_spec=pltpu.PrefetchScalarGridSpec(
            num_scalar_prefetch=1,
            grid=(specs["steps"],),
            in_specs=[specs[name] for name in names],
            out_specs=[specs[name] for name in ("projected", "z", "gain_grad")],
            scratch_shapes=[pltpu.VMEM((heads, VDIM, KDIM), f32)],
        ),
        out_shape=[
            jax.ShapeDtypeStruct((length, projected_width), bf16),
            jax.ShapeDtypeStruct((length, key_width), f32),
            jax.ShapeDtypeStruct((8, VDIM), f32),
        ],
        compiler_params=pltpu.CompilerParams(vmem_limit_bytes=40 * 1024 * 1024),
        cost_estimate=pl.CostEstimate(
            flops=25 * 10**9, bytes_accessed=20 * 10**6, transcendentals=4 * 10**6
        ),
        name="mixer_backward",
    )(scal, projected, z, live, gain, sums, mixture, states, grad_gated)


def swap_tensor(values):
    return lax.ppermute(values, "tensor", [(0, 1), (1, 0)])


def chip_sum(values):
    count = lax.axis_size("dp")
    parity = lax.axis_index("dp") % 2
    blocks = values.reshape(count // 2, 2, values.shape[0] // count, values.shape[1])
    kept = lax.dynamic_index_in_dim(blocks, parity, 1, keepdims=False)
    sent = lax.dynamic_index_in_dim(blocks, 1 - parity, 1, keepdims=False)
    arrived = lax.ppermute(sent, "dp", [(i, i ^ 1) for i in range(count)])
    total = (kept.astype(f32) + arrived.astype(f32)).astype(bf16)
    return total.reshape(values.shape[0] // 2, values.shape[1])


def chips_scatter(values):
    count = lax.axis_size("dp")
    groups = [list(range(parity, count, 2)) for parity in range(2)]
    return lax.psum_scatter(
        values, "dp", scatter_dimension=0, axis_index_groups=groups, tiled=True
    )


def butterfly_sum(values):
    total = values + swap_tensor(values)
    count = lax.axis_size("dp")
    reach = 1
    while reach < count:
        total = total + lax.ppermute(total, "dp", [(i, i ^ reach) for i in range(count)])
        reach *= 2
    return total


def on_device(
    tokens,
    cotangent,
    sequence_lengths,
    sequence_group,
    sequence_offset,
    mixer_gain,
    query_weight,
    key_weight,
    value_weight,
    output_gate,
    output_weight,
    decay_down,
    decay_up,
    decay_bias,
    head_gain,
    feed_gain,
    feed_gate,
    feed_up,
    feed_down,
):
    which_group = lax.axis_index("dp")
    half_index = lax.axis_index("tensor")
    own = tokens.shape[0]
    group_rows = own * 2
    key_width = query_weight.shape[1]
    value_width = value_weight.shape[1]
    feed_width = feed_gate.shape[1]
    places = (jnp.arange(group_rows, dtype=jnp.int32) + half_index * own) % group_rows
    live_mask, restart = group_layout(
        sequence_lengths,
        sequence_group,
        sequence_offset,
        which_group,
        places[:, None],
        group_rows // SPAN,
    )
    live = live_mask[:, None]
    scal = jnp.concatenate([half_index.astype(jnp.int32)[None], restart])
    sums = jnp.asarray(np.tile(decay_sums(), (1, 2)), bf16)
    gain_head = head_gain.astype(f32)[None, :]

    joined = lax.all_gather(
        jnp.concatenate(
            [query_weight, key_weight, value_weight, output_gate, output_weight], axis=1
        ),
        "dp",
        axis=0,
        tiled=True,
    )
    feed_all = lax.all_gather(
        jnp.concatenate([feed_gate, feed_up, feed_down], axis=1), "dp", axis=0, tiled=True
    )
    gain_in = mixer_gain.astype(f32)
    token_values = tokens.astype(f32)
    normed_in, inverse_in = rms_forward(token_values, gain_in)
    normed_low = normed_in.astype(bf16)
    normed_other = swap_tensor(normed_low)
    normed_other, cotangent_low = lax.optimization_barrier((normed_other, cotangent))
    cotangent_other = swap_tensor(cotangent_low)
    joined, cotangent_other = lax.optimization_barrier((joined, cotangent_other))
    projected_width = 2 * key_width + 2 * value_width
    joined_in = joined[:, :projected_width]
    output_full = joined[:, projected_width:]
    gate_up_full = feed_all[:, : 2 * feed_width]
    feed_down_full = feed_all[:, 2 * feed_width :]

    normed_all = jnp.concatenate([normed_low, normed_other], axis=0)
    projected = nn(normed_all, joined_in).astype(bf16)
    latent = nn(normed_all, decay_down)
    up_local = lax.dynamic_slice_in_dim(decay_up, half_index * key_width, key_width, 1).astype(f32)
    bias_local = lax.dynamic_slice_in_dim(decay_bias, half_index * key_width, key_width, 0)
    z = jnp.dot(latent, up_local, precision=highest) + bias_local.astype(f32)
    gated, mixture, states = mixer_forward(scal, projected, z, live, gain_head, sums)

    attended_other = swap_tensor(nt(gated[own:], output_full).astype(bf16))
    attended_own = nt(gated[:own], output_full)
    middle = token_values + (attended_own + attended_other.astype(f32))
    gain_mid = feed_gain.astype(f32)
    normed_mid, inverse_mid = rms_forward(middle, gain_mid)
    mid_low = normed_mid.astype(bf16)
    mid_other = swap_tensor(mid_low)

    def feed_rows(mid_rows, cotangent_rows):
        both = nn(mid_rows, gate_up_full)
        gate_part = both[:, :feed_width]
        up_part = both[:, feed_width:]
        sigmoid_gate = jax.nn.sigmoid(gate_part)
        silu_gate = gate_part * sigmoid_gate
        hidden_low = (silu_gate * up_part).astype(bf16)
        grad_hidden = nn(cotangent_rows, feed_down_full)
        grad_gate_low = (
            grad_hidden * up_part * (sigmoid_gate + silu_gate * (1.0 - sigmoid_gate))
        ).astype(bf16)
        grad_up_low = (grad_hidden * silu_gate).astype(bf16)
        grad_both = jnp.concatenate([grad_gate_low, grad_up_low], axis=1)
        return hidden_low, grad_both, nt(grad_both, gate_up_full)

    hidden_own, grad_both_own, mid_back_own = feed_rows(mid_low, cotangent)
    hidden_other, grad_both_other, mid_back_other = feed_rows(mid_other, cotangent_other)
    mid_back = swap_tensor(mid_back_other.astype(bf16))

    upstream = cotangent.astype(f32)
    grad_normed_mid = mid_back_own + mid_back.astype(f32)
    grad_mid_in, grad_feed_gain = rms_backward(middle, inverse_mid, gain_mid, grad_normed_mid)
    grad_middle = upstream + grad_mid_in
    grad_attended = grad_middle.astype(bf16)
    attended_back = swap_tensor(grad_attended)

    mid_all = jnp.concatenate([mid_low, mid_other], axis=0)
    cotangent_all = jnp.concatenate([cotangent, cotangent_other], axis=0)
    hidden_all = jnp.concatenate([hidden_own, hidden_other], axis=0)
    grad_both_all = jnp.concatenate([grad_both_own, grad_both_other], axis=0)
    feed_grads = jnp.concatenate(
        [
            tn(mid_all, grad_both_all).astype(bf16),
            tn(cotangent_all, hidden_all).astype(bf16),
        ],
        axis=1,
    )
    feed_chip = chip_sum(feed_grads)

    attended_all = jnp.concatenate([grad_attended, attended_back], axis=0)
    grad_gated = nn(attended_all, output_full).astype(bf16)
    fed_send = nt(hidden_other, feed_down_full).astype(bf16)
    grad_gated, feed_chip, fed_send = lax.optimization_barrier((grad_gated, feed_chip, fed_send))
    fed = nt(hidden_own, feed_down_full) + swap_tensor(fed_send).astype(f32)
    output = (middle + fed).astype(bf16)
    feed_sum = chips_scatter(feed_chip)
    grad_projected, grad_z, grad_gain_rows = mixer_backward(
        scal, projected, z, live, gain_head, sums, mixture, states, grad_gated
    )
    joined_grads = jnp.concatenate(
        [tn(normed_all, grad_projected).astype(bf16), tn(attended_all, gated).astype(bf16)], axis=1
    )
    joined_chip, feed_sum = lax.optimization_barrier((chip_sum(joined_grads), feed_sum))
    joined_sum = chips_scatter(joined_chip).astype(f32)
    feed_sum = feed_sum.astype(f32)

    grad_latent = lax.dot_general(
        grad_z, up_local, (((1,), (1,)), ((), ())), precision=highest, preferred_element_type=f32
    )
    grad_up_local = lax.dot_general(
        latent, grad_z, (((0,), (0,)), ((), ())), precision=highest, preferred_element_type=f32
    )
    grad_bias_local = jnp.sum(grad_z, axis=0)
    latent_high = grad_latent.astype(bf16)
    latent_rest = (grad_latent - latent_high.astype(f32)).astype(bf16)
    grad_down_parts = tn(normed_all, jnp.concatenate([latent_high, latent_rest], axis=1))
    low_rank = decay_down.shape[1]
    grad_decay_down = grad_down_parts[:, :low_rank] + grad_down_parts[:, low_rank:]
    from_latent = nt(latent_high, decay_down) + nt(latent_rest, decay_down)
    normed_part = (nt(grad_projected, joined_in) + from_latent).astype(bf16)
    grad_normed = normed_part[:own].astype(f32) + swap_tensor(normed_part[own:]).astype(f32)
    grad_in_part, grad_mixer_gain = rms_backward(token_values, inverse_in, gain_in, grad_normed)
    input_grad = grad_middle + grad_in_part

    up_full = lax.dynamic_update_slice_in_dim(
        jnp.zeros(decay_up.shape, f32), grad_up_local, half_index * key_width, 1
    )
    bias_full = lax.dynamic_update_slice_in_dim(
        jnp.zeros(decay_bias.shape, f32), grad_bias_local, half_index * key_width, 0
    )
    small = (
        grad_mixer_gain,
        grad_decay_down,
        up_full,
        bias_full,
        jnp.sum(grad_gain_rows, axis=0),
        grad_feed_gain,
    )
    flat = butterfly_sum(jnp.concatenate([part.reshape(-1, 128) for part in small], axis=0))
    small_sums = []
    row = 0
    for part in small:
        taken = part.size // 128
        small_sums.append(flat[row : row + taken].reshape(part.shape))
        row += taken
    return (
        output,
        input_grad,
        small_sums[0],
        joined_sum[:, :key_width],
        joined_sum[:, key_width : 2 * key_width],
        joined_sum[:, 2 * key_width : 2 * key_width + value_width],
        joined_sum[:, 2 * key_width + value_width : projected_width],
        joined_sum[:, projected_width:],
        small_sums[1],
        small_sums[2],
        small_sums[3],
        small_sums[4],
        small_sums[5],
        feed_sum[:, :feed_width],
        feed_sum[:, feed_width : 2 * feed_width],
        feed_sum[:, 2 * feed_width : 3 * feed_width],
    )


def solution(mesh):
    rows = P(("dp", "tensor"), None)
    weight = P("dp", "tensor")
    return jax.shard_map(
        on_device,
        mesh=mesh,
        in_specs=(rows, rows, P(), P(), P(), P())
        + (weight,) * 5
        + (P(), P(), P(), P(), P())
        + (weight,) * 3,
        out_specs=(rows, rows, P()) + (weight,) * 5 + (P(),) * 5 + (weight,) * 3,
        check_vma=False,
    )
```

```python
import functools

import jax
import jax.numpy as jnp
import numpy as np
from jax import lax
from jax.experimental import pallas as pl
from jax.experimental.pallas import tpu as pltpu
from jax.sharding import PartitionSpec as P

KDIM = 128
VDIM = 256
SPAN = 64
LEVELS = 6
KINDS = LEVELS + 2
STEP_SPANS = 2

epsilon = 1e-06
head_epsilon = 1.0
gate_scale = 16.0
highest = lax.Precision.HIGHEST
f32 = jnp.float32
bf16 = jnp.bfloat16


def rms_forward(values, norm_gain, floor_value=epsilon):
    inverse = lax.rsqrt(jnp.mean(values * values, axis=-1, keepdims=True) + floor_value)
    return (values * inverse * norm_gain, inverse)


def rms_backward(values, inverse, norm_gain, upstream):
    scaled = upstream * norm_gain
    inner = jnp.mean(scaled * values, axis=-1, keepdims=True)
    grad_values = inverse * scaled - values * (inverse * inverse * inverse) * inner
    grad_gain = jnp.sum(upstream * values * inverse, axis=0)
    return (grad_values, grad_gain)


def group_layout(sequence_lengths, sequence_group, sequence_offset, which_group, places, span_count):
    live_record = (sequence_group == which_group) & (sequence_lengths > 0)
    start_row = sequence_offset * SPAN
    covered = (
        live_record[None, :]
        & (places >= start_row[None, :])
        & (places < (start_row + sequence_lengths)[None, :])
    )
    live_mask = jnp.any(covered, axis=1).astype(f32)
    span_ids = jnp.arange(span_count, dtype=jnp.int32)[:, None]
    restart = jnp.any(live_record[None, :] & (span_ids == sequence_offset[None, :]), axis=1)
    return (live_mask, restart.astype(jnp.int32))


def nn(left, right):
    return lax.dot_general(left, right, (((1,), (0,)), ((), ())), preferred_element_type=f32)


def nt(left, right):
    return lax.dot_general(left, right, (((1,), (1,)), ((), ())), preferred_element_type=f32)


def tn(left, right):
    return lax.dot_general(left, right, (((0,), (0,)), ((), ())), preferred_element_type=f32)


def decay_sums():
    rows = np.arange(SPAN)[:, None]
    cols = np.arange(SPAN)[None, :]
    blocks = [cols <= rows]
    for level in range(LEVELS):
        half = 1 << level
        edge = (rows // (2 * half)) * (2 * half) + half
        right = rows >= edge
        blocks.append(np.where(right, (cols >= edge) & (cols <= rows), (cols > rows) & (cols < edge)))
    blocks.append(cols > rows)
    return np.concatenate(blocks, axis=0).astype(np.float32)


def pair_levels():
    rows = lax.broadcasted_iota(jnp.int32, (SPAN, SPAN), 0)
    cols = lax.broadcasted_iota(jnp.int32, (SPAN, SPAN), 1)
    apart = rows ^ cols
    later = rows > cols
    masks = [later & (lax.shift_right_logical(apart, level) == 1) for level in range(LEVELS)]
    return masks, rows == cols


def span_factors(z_part, sums):
    decays = (jnp.minimum(z_part, 0.0) - jnp.log1p(jnp.exp(-jnp.abs(z_part)))) * (1.0 / gate_scale)
    high = decays.astype(bf16)
    low = (decays - high.astype(f32)).astype(bf16)
    return jnp.exp(nn(sums, jnp.concatenate([high, low], axis=0)))


def span_scores(queries, keys, factors, masks, diagonal):
    scores = jnp.where(diagonal, nt(queries.astype(bf16), keys.astype(bf16)), 0.0)
    query_levels = []
    key_levels = []
    for level in range(LEVELS):
        factor = factors[(level + 1) * SPAN : (level + 2) * SPAN]
        query_level = (queries * factor).astype(bf16)
        key_level = (keys * factor).astype(bf16)
        scores = jnp.where(masks[level], nt(query_level, key_level), scores)
        query_levels.append(query_level)
        key_levels.append(key_level)
    return scores, query_levels, key_levels


def forward_kernel(heads, scal, projected, z, live, gain, sums, gated, mixture, states, state):
    step = pl.program_id(0)
    key_width = heads * KDIM
    value_width = heads * VDIM

    @pl.when(step == 0)
    def _():
        state[...] = jnp.zeros_like(state)

    masks, diagonal = pair_levels()
    head_gain = gain[...]
    for part in range(STEP_SPANS):
        rows = slice(part * SPAN, (part + 1) * SPAN)
        factors_all = span_factors(z[rows, :], sums[...])
        keep = jnp.where(scal[1 + step * STEP_SPANS + part] == 0, 1.0, 0.0)
        for head in range(heads):
            keys_at = slice(head * KDIM, (head + 1) * KDIM)
            queries = projected[rows, keys_at].astype(f32)
            keys = projected[rows, key_width + head * KDIM : key_width + (head + 1) * KDIM].astype(f32)
            value_at = 2 * key_width + head * VDIM
            values = projected[rows, value_at : value_at + VDIM]
            gating = projected[rows, value_at + value_width : value_at + value_width + VDIM].astype(f32)
            factors = factors_all[:, keys_at]
            scores, _, _ = span_scores(queries, keys, factors, masks, diagonal)
            entering = state[head] * keep
            entering_low = entering.astype(bf16)
            states[part, head] = entering_low
            whole = factors[:SPAN]
            after = factors[(KINDS - 1) * SPAN :]
            mixed = nn(scores.astype(bf16), values) + nt(
                (queries * whole).astype(bf16), entering_low
            )
            state[head] = entering * whole[SPAN - 1 :] + tn(values, (keys * after).astype(bf16))
            value_cols = slice(head * VDIM, (head + 1) * VDIM)
            mixture[rows, value_cols] = mixed.astype(bf16)
            inverse = lax.rsqrt(jnp.mean(mixed * mixed, axis=-1, keepdims=True) + head_epsilon)
            silu = gating * jax.nn.sigmoid(gating)
            gated[rows, value_cols] = (mixed * inverse * head_gain * silu * live[rows, :]).astype(bf16)


def backward_kernel(
    heads,
    scal,
    projected,
    z,
    live,
    gain,
    sums,
    mixture,
    states,
    grad_gated,
    grad_projected,
    grad_z,
    grad_gain,
    grad_state,
):
    step = pl.program_id(0)
    natural = pl.num_programs(0) - 1 - step
    key_width = heads * KDIM
    value_width = heads * VDIM

    @pl.when(step == 0)
    def _():
        grad_state[...] = jnp.zeros_like(grad_state)
        grad_gain[...] = jnp.zeros_like(grad_gain)

    masks, diagonal = pair_levels()
    head_gain = gain[...]
    last_row = lax.broadcasted_iota(jnp.int32, (SPAN, KDIM), 0) == SPAN - 1
    for part in reversed(range(STEP_SPANS)):
        rows = slice(part * SPAN, (part + 1) * SPAN)
        z_part = z[rows, :]
        factors_all = span_factors(z_part, sums[...])
        keep = jnp.where(scal[1 + natural * STEP_SPANS + part] == 0, 1.0, 0.0)
        live_part = live[rows, :]
        exponents = []
        for head in range(heads):
            keys_at = slice(head * KDIM, (head + 1) * KDIM)
            key_cols = slice(key_width + head * KDIM, key_width + (head + 1) * KDIM)
            value_at = 2 * key_width + head * VDIM
            value_cols = slice(value_at, value_at + VDIM)
            gate_cols = slice(value_at + value_width, value_at + value_width + VDIM)
            mixed_cols = slice(head * VDIM, (head + 1) * VDIM)
            queries = projected[rows, keys_at].astype(f32)
            keys = projected[rows, key_cols].astype(f32)
            values = projected[rows, value_cols]
            gating = projected[rows, gate_cols].astype(f32)
            factors = factors_all[:, keys_at]
            scores, query_levels, key_levels = span_scores(queries, keys, factors, masks, diagonal)
            scores_low = scores.astype(bf16)
            whole = factors[:SPAN]
            after = factors[(KINDS - 1) * SPAN :]

            mixed = mixture[rows, mixed_cols].astype(f32)
            inverse = lax.rsqrt(jnp.mean(mixed * mixed, axis=-1, keepdims=True) + head_epsilon)
            unit = mixed * inverse
            sigmoid = jax.nn.sigmoid(gating)
            silu = gating * sigmoid
            upstream = grad_gated[rows, mixed_cols].astype(f32) * live_part
            grad_projected[rows, gate_cols] = (
                upstream * unit * head_gain * (sigmoid + silu * (1.0 - sigmoid))
            ).astype(bf16)
            normed_back = upstream * silu
            gain_part = normed_back * unit
            grad_gain[...] += jnp.sum(gain_part.reshape(SPAN // 8, 8, VDIM), axis=0)
            scaled = normed_back * head_gain
            inner = jnp.mean(scaled * unit, axis=-1, keepdims=True)
            grad_mixed = (inverse * (scaled - unit * inner)).astype(bf16)

            entering = states[part, head]
            leaving = grad_state[head]
            leaving_low = leaving.astype(bf16)
            grad_scores = nt(grad_mixed, values)
            after_keys = (keys * after).astype(bf16)
            whole_queries = (queries * whole).astype(bf16)
            grad_projected[rows, value_cols] = (
                tn(scores_low, grad_mixed) + nt(after_keys, leaving_low)
            ).astype(bf16)
            grad_queries = whole * nn(grad_mixed, entering)
            grad_keys = after * nn(values, leaving_low)
            fading = whole[SPAN - 1 :]
            last_sum = fading * jnp.sum(entering.astype(f32) * leaving, axis=0, keepdims=True)
            exponents_head = [queries * grad_queries + jnp.where(last_row, last_sum, 0.0)]
            last_exponent = keys * grad_keys
            for level in range(LEVELS):
                factor = factors[(level + 1) * SPAN : (level + 2) * SPAN]
                level_back = jnp.where(masks[level], grad_scores, 0.0).astype(bf16)
                query_part = factor * nn(level_back, key_levels[level])
                key_part = factor * tn(level_back, query_levels[level])
                grad_queries += query_part
                grad_keys += key_part
                exponents_head.append(queries * query_part + keys * key_part)
            exponents_head.append(last_exponent)
            same = jnp.sum(jnp.where(diagonal, grad_scores, 0.0), axis=1, keepdims=True)
            grad_projected[rows, keys_at] = (grad_queries + same * keys).astype(bf16)
            grad_projected[rows, key_cols] = (grad_keys + same * queries).astype(bf16)
            exponents.append(jnp.concatenate(exponents_head, axis=0).astype(bf16))
            grad_state[head] = keep * (leaving * fading + tn(grad_mixed, whole_queries))
        grad_decays = tn(sums[:, :SPAN], jnp.concatenate(exponents, axis=1))
        grad_z[rows, :] = grad_decays * jax.nn.sigmoid(-z_part) * (1.0 / gate_scale)


def mixer_specs(length, projected_width, key_width, value_width, reverse):
    steps = length // (SPAN * STEP_SPANS)
    step_rows = SPAN * STEP_SPANS
    heads = key_width // KDIM

    def natural(step):
        return steps - 1 - step if reverse else step

    def by_rows(step, scal):
        return (lax.rem(natural(step) + scal[0] * (steps // 2), steps), 0)

    def whole(step, scal):
        return (0, 0)

    return dict(
        steps=steps,
        projected=pl.BlockSpec((step_rows, projected_width), by_rows),
        z=pl.BlockSpec((step_rows, key_width), by_rows),
        live=pl.BlockSpec((step_rows, 1), by_rows),
        gain=pl.BlockSpec((1, VDIM), whole),
        sums=pl.BlockSpec((KINDS * SPAN, 2 * SPAN), whole),
        values=pl.BlockSpec((step_rows, value_width), by_rows),
        states=pl.BlockSpec(
            (STEP_SPANS, heads, VDIM, KDIM), lambda step, scal: (natural(step), 0, 0, 0)
        ),
        gain_grad=pl.BlockSpec((8, VDIM), whole),
    )


def mixer_forward(scal, projected, z, live, gain, sums):
    length, projected_width = projected.shape
    key_width = z.shape[1]
    heads = key_width // KDIM
    value_width = heads * VDIM
    spans = length // SPAN
    specs = mixer_specs(length, projected_width, key_width, value_width, False)
    return pl.pallas_call(
        functools.partial(forward_kernel, heads),
        grid_spec=pltpu.PrefetchScalarGridSpec(
            num_scalar_prefetch=1,
            grid=(specs["steps"],),
            in_specs=[specs[name] for name in ("projected", "z", "live", "gain", "sums")],
            out_specs=[specs[name] for name in ("values", "values", "states")],
            scratch_shapes=[pltpu.VMEM((heads, VDIM, KDIM), f32)],
        ),
        out_shape=[
            jax.ShapeDtypeStruct((length, value_width), bf16),
            jax.ShapeDtypeStruct((length, value_width), bf16),
            jax.ShapeDtypeStruct((spans, heads, VDIM, KDIM), bf16),
        ],
        compiler_params=pltpu.CompilerParams(vmem_limit_bytes=40 * 1024 * 1024),
        cost_estimate=pl.CostEstimate(
            flops=10**10, bytes_accessed=15 * 10**6, transcendentals=4 * 10**6
        ),
        name="mixer_forward",
    )(scal, projected, z, live, gain, sums)


def mixer_backward(scal, projected, z, live, gain, sums, mixture, states, grad_gated):
    length, projected_width = projected.shape
    key_width = z.shape[1]
    heads = key_width // KDIM
    value_width = heads * VDIM
    specs = mixer_specs(length, projected_width, key_width, value_width, True)
    names = ("projected", "z", "live", "gain", "sums", "values", "states", "values")
    return pl.pallas_call(
        functools.partial(backward_kernel, heads),
        grid_spec=pltpu.PrefetchScalarGridSpec(
            num_scalar_prefetch=1,
            grid=(specs["steps"],),
            in_specs=[specs[name] for name in names],
            out_specs=[specs[name] for name in ("projected", "z", "gain_grad")],
            scratch_shapes=[pltpu.VMEM((heads, VDIM, KDIM), f32)],
        ),
        out_shape=[
            jax.ShapeDtypeStruct((length, projected_width), bf16),
            jax.ShapeDtypeStruct((length, key_width), f32),
            jax.ShapeDtypeStruct((8, VDIM), f32),
        ],
        compiler_params=pltpu.CompilerParams(vmem_limit_bytes=40 * 1024 * 1024),
        cost_estimate=pl.CostEstimate(
            flops=25 * 10**9, bytes_accessed=20 * 10**6, transcendentals=4 * 10**6
        ),
        name="mixer_backward",
    )(scal, projected, z, live, gain, sums, mixture, states, grad_gated)


def swap_tensor(values):
    return lax.ppermute(values, "tensor", [(0, 1), (1, 0)])


def chip_sum(values):
    count = lax.axis_size("dp")
    parity = lax.axis_index("dp") % 2
    blocks = values.reshape(count // 2, 2, values.shape[0] // count, values.shape[1])
    kept = lax.dynamic_index_in_dim(blocks, parity, 1, keepdims=False)
    sent = lax.dynamic_index_in_dim(blocks, 1 - parity, 1, keepdims=False)
    arrived = lax.ppermute(sent, "dp", [(i, i ^ 1) for i in range(count)])
    total = (kept.astype(f32) + arrived.astype(f32)).astype(bf16)
    return total.reshape(values.shape[0] // 2, values.shape[1])


def halving_stages():
    return (lax.axis_size("dp") // 2).bit_length() - 1


def by_chip(values):
    stages = halving_stages()
    return values.reshape((2,) * stages + (values.shape[0] >> stages, values.shape[1]))


def halving_stage(held, stage):
    count = lax.axis_size("dp")
    stages = halving_stages()
    bit = 2 << stage
    side = (lax.axis_index("dp") // bit) % 2
    axis = stages - 1 - stage
    kept = lax.dynamic_index_in_dim(held, side, axis, keepdims=False)
    sent = lax.dynamic_index_in_dim(held, 1 - side, axis, keepdims=False)
    arrived = lax.ppermute(sent, "dp", [(i, i ^ bit) for i in range(count)])
    total = kept.astype(f32) + arrived.astype(f32)
    return total if stage == stages - 1 else total.astype(bf16)


def halving_rest(held):
    for stage in range(1, halving_stages()):
        held = halving_stage(held, stage)
    return held


def both_ways(side, mine, other, axis):
    first = jnp.where(side == 0, mine, other)
    second = jnp.where(side == 0, other, mine)
    return jnp.stack([first, second], axis=axis)


def gather_doubling(values):
    count = lax.axis_size("dp")
    place = lax.axis_index("dp")
    stages = count.bit_length() - 1
    held = values
    for stage in range(stages):
        bit = count >> (stage + 1)
        arrived = lax.ppermute(held, "dp", [(i, i ^ bit) for i in range(count)])
        held = both_ways((place // bit) % 2, held, arrived, stage)
    return held.reshape(values.shape[0] * count, values.shape[1])


def swap_whole(values):
    count = lax.axis_size("dp")
    parity = lax.axis_index("dp") % 2
    half = values.shape[0] // 2
    mine = swap_tensor(lax.dynamic_slice_in_dim(values, parity * half, half, 0))
    other = lax.ppermute(mine, "dp", [(i, i ^ 1) for i in range(count)])
    return both_ways(parity, mine, other, 0).reshape(values.shape)


def butterfly_sum(values):
    total = values + swap_tensor(values)
    count = lax.axis_size("dp")
    reach = 1
    while reach < count:
        total = total + lax.ppermute(total, "dp", [(i, i ^ reach) for i in range(count)])
        reach *= 2
    return total


def on_device(
    tokens,
    cotangent,
    sequence_lengths,
    sequence_group,
    sequence_offset,
    mixer_gain,
    query_weight,
    key_weight,
    value_weight,
    output_gate,
    output_weight,
    decay_down,
    decay_up,
    decay_bias,
    head_gain,
    feed_gain,
    feed_gate,
    feed_up,
    feed_down,
):
    which_group = lax.axis_index("dp")
    half_index = lax.axis_index("tensor")
    own = tokens.shape[0]
    group_rows = own * 2
    key_width = query_weight.shape[1]
    value_width = value_weight.shape[1]
    feed_width = feed_gate.shape[1]
    places = (jnp.arange(group_rows, dtype=jnp.int32) + half_index * own) % group_rows
    live_mask, restart = group_layout(
        sequence_lengths,
        sequence_group,
        sequence_offset,
        which_group,
        places[:, None],
        group_rows // SPAN,
    )
    live = live_mask[:, None]
    scal = jnp.concatenate([half_index.astype(jnp.int32)[None], restart])
    sums = jnp.asarray(np.tile(decay_sums(), (1, 2)), bf16)
    gain_head = head_gain.astype(f32)[None, :]

    joined = lax.all_gather(
        jnp.concatenate(
            [query_weight, key_weight, value_weight, output_gate, output_weight], axis=1
        ),
        "dp",
        axis=0,
        tiled=True,
    )
    gate_up_full = lax.all_gather(
        jnp.concatenate([feed_gate, feed_up], axis=1), "dp", axis=0, tiled=True
    )
    feed_down_full = gather_doubling(feed_down)
    gain_in = mixer_gain.astype(f32)
    token_values = tokens.astype(f32)
    normed_in, inverse_in = rms_forward(token_values, gain_in)
    normed_low = normed_in.astype(bf16)
    normed_other = swap_tensor(normed_low)
    cotangent_other = swap_tensor(cotangent)
    joined, cotangent_other = lax.optimization_barrier((joined, cotangent_other))
    projected_width = 2 * key_width + 2 * value_width
    joined_in = joined[:, :projected_width]
    output_half = joined[:, projected_width:]
    output_other = swap_whole(output_half)

    normed_all = jnp.concatenate([normed_low, normed_other], axis=0)
    projected = nn(normed_all, joined_in).astype(bf16)
    latent = nn(normed_all, decay_down)
    up_local = lax.dynamic_slice_in_dim(decay_up, half_index * key_width, key_width, 1).astype(f32)
    bias_local = lax.dynamic_slice_in_dim(decay_bias, half_index * key_width, key_width, 0)
    z = jnp.dot(latent, up_local, precision=highest) + bias_local.astype(f32)
    gated, mixture, states = mixer_forward(scal, projected, z, live, gain_head, sums)

    gated_own = gated[:own]
    gated_rest = swap_tensor(gated[own:])
    attended = nt(gated_own, output_half) + nt(gated_rest, output_other)
    middle = token_values + attended
    gain_mid = feed_gain.astype(f32)
    normed_mid, inverse_mid = rms_forward(middle, gain_mid)
    mid_low = normed_mid.astype(bf16)
    mid_other = swap_tensor(mid_low)

    def feed_rows(mid_rows, cotangent_rows):
        both = nn(mid_rows, gate_up_full)
        gate_part = both[:, :feed_width]
        up_part = both[:, feed_width:]
        sigmoid_gate = jax.nn.sigmoid(gate_part)
        silu_gate = gate_part * sigmoid_gate
        hidden_low = (silu_gate * up_part).astype(bf16)
        grad_hidden = nn(cotangent_rows, feed_down_full)
        grad_gate_low = (
            grad_hidden * up_part * (sigmoid_gate + silu_gate * (1.0 - sigmoid_gate))
        ).astype(bf16)
        grad_up_low = (grad_hidden * silu_gate).astype(bf16)
        grad_both = jnp.concatenate([grad_gate_low, grad_up_low], axis=1)
        return hidden_low, grad_both, nt(grad_both, gate_up_full)

    hidden_other, grad_both_other, mid_back_other = feed_rows(mid_other, cotangent_other)
    mid_send, mid_here, cotangent_here = lax.optimization_barrier(
        (mid_back_other.astype(bf16), mid_low, cotangent)
    )
    mid_back = swap_tensor(mid_send)
    hidden_own, grad_both_own, mid_back_own = feed_rows(mid_here, cotangent_here)

    upstream = cotangent.astype(f32)
    grad_normed_mid = mid_back_own + mid_back.astype(f32)
    grad_mid_in, grad_feed_gain = rms_backward(middle, inverse_mid, gain_mid, grad_normed_mid)
    grad_middle = upstream + grad_mid_in
    grad_attended = grad_middle.astype(bf16)
    gated_back = swap_tensor(nn(grad_attended, output_other).astype(bf16))
    grad_gated = jnp.concatenate([nn(grad_attended, output_half).astype(bf16), gated_back], axis=0)

    mid_all = jnp.concatenate([mid_low, mid_other], axis=0)
    cotangent_all = jnp.concatenate([cotangent, cotangent_other], axis=0)
    hidden_all = jnp.concatenate([hidden_own, hidden_other], axis=0)
    grad_both_all = jnp.concatenate([grad_both_own, grad_both_other], axis=0)
    down_sum = by_chip(chip_sum(tn(cotangent_all, hidden_all).astype(bf16)))
    down_sum = halving_stage(down_sum, 0)
    both_chip = chip_sum(tn(mid_all, grad_both_all).astype(bf16))
    fed_send = nt(hidden_other, feed_down_full).astype(bf16)
    grad_gated, down_sum, both_chip, fed_send = lax.optimization_barrier(
        (grad_gated, down_sum, both_chip, fed_send)
    )
    gate_sum = halving_stage(by_chip(both_chip[:, :feed_width]), 0)
    up_sum = halving_stage(by_chip(both_chip[:, feed_width:]), 0)
    fed_back = swap_tensor(fed_send)
    output_chip = chip_sum(
        jnp.concatenate(
            [
                tn(grad_attended, gated_own).astype(bf16),
                tn(grad_attended, gated_rest).astype(bf16),
            ],
            axis=1,
        )
    )
    output_back = swap_tensor(output_chip[:, value_width:])
    grad_projected, grad_z, grad_gain_rows = mixer_backward(
        scal, projected, z, live, gain_head, sums, mixture, states, grad_gated
    )
    grad_projected, gate_sum = lax.optimization_barrier((grad_projected, gate_sum))
    projected_chip = chip_sum(tn(normed_all, grad_projected).astype(bf16))
    output_total = output_chip[:, :value_width].astype(f32) + output_back.astype(f32)
    joined_chip = jnp.concatenate([projected_chip, output_total.astype(bf16)], axis=1)
    joined_chip, up_sum = lax.optimization_barrier((joined_chip, up_sum))
    joined_sums = [
        halving_stage(by_chip(piece), 0) for piece in jnp.split(joined_chip, 2, axis=1)
    ]
    hidden_late, grad_projected = lax.optimization_barrier((hidden_own, grad_projected))
    fed = nt(hidden_late, feed_down_full) + fed_back.astype(f32)
    output = (middle + fed).astype(bf16)

    grad_latent = lax.dot_general(
        grad_z, up_local, (((1,), (1,)), ((), ())), precision=highest, preferred_element_type=f32
    )
    grad_up_local = lax.dot_general(
        latent, grad_z, (((0,), (0,)), ((), ())), precision=highest, preferred_element_type=f32
    )
    grad_bias_local = jnp.sum(grad_z, axis=0)
    latent_high = grad_latent.astype(bf16)
    latent_rest = (grad_latent - latent_high.astype(f32)).astype(bf16)
    grad_down_parts = tn(normed_all, jnp.concatenate([latent_high, latent_rest], axis=1))
    low_rank = decay_down.shape[1]
    grad_decay_down = grad_down_parts[:, :low_rank] + grad_down_parts[:, low_rank:]
    from_latent = nt(latent_high, decay_down) + nt(latent_rest, decay_down)
    normed_part = nt(grad_projected, joined_in) + from_latent
    grad_mixer_gain = jnp.sum(normed_part * normed_all.astype(f32), axis=0) / gain_in
    normed_part = normed_part.astype(bf16)
    normed_back, joined_sums[1] = lax.optimization_barrier(
        (swap_tensor(normed_part[own:]), joined_sums[1])
    )
    grad_normed = normed_part[:own].astype(f32) + normed_back.astype(f32)
    grad_in_part = rms_backward(token_values, inverse_in, gain_in, grad_normed)[0]
    input_grad = grad_middle + grad_in_part

    up_full = lax.dynamic_update_slice_in_dim(
        jnp.zeros(decay_up.shape, f32), grad_up_local, half_index * key_width, 1
    )
    bias_full = lax.dynamic_update_slice_in_dim(
        jnp.zeros(decay_bias.shape, f32), grad_bias_local, half_index * key_width, 0
    )
    small = (
        grad_mixer_gain,
        grad_decay_down,
        up_full,
        bias_full,
        jnp.sum(grad_gain_rows, axis=0),
        grad_feed_gain,
    )
    flat = jnp.concatenate([part.reshape(-1, 128) for part in small], axis=0)
    flat, joined_sums[0] = lax.optimization_barrier((flat, joined_sums[0]))
    flat = butterfly_sum(flat)
    down_sum, gate_sum, up_sum = (halving_rest(held) for held in (down_sum, gate_sum, up_sum))
    joined_sum = jnp.concatenate([halving_rest(held) for held in joined_sums], axis=1)
    small_sums = []
    row = 0
    for part in small:
        taken = part.size // 128
        small_sums.append(flat[row : row + taken].reshape(part.shape))
        row += taken
    return (
        output,
        input_grad,
        small_sums[0],
        joined_sum[:, :key_width],
        joined_sum[:, key_width : 2 * key_width],
        joined_sum[:, 2 * key_width : 2 * key_width + value_width],
        joined_sum[:, 2 * key_width + value_width : projected_width],
        joined_sum[:, projected_width:],
        small_sums[1],
        small_sums[2],
        small_sums[3],
        small_sums[4],
        small_sums[5],
        gate_sum,
        up_sum,
        down_sum,
    )


def solution(mesh):
    rows = P(("dp", "tensor"), None)
    weight = P("dp", "tensor")
    return jax.shard_map(
        on_device,
        mesh=mesh,
        in_specs=(rows, rows, P(), P(), P(), P())
        + (weight,) * 5
        + (P(), P(), P(), P(), P())
        + (weight,) * 3,
        out_specs=(rows, rows, P()) + (weight,) * 5 + (P(),) * 5 + (weight,) * 3,
        check_vma=False,
    )
```

```python
import functools

import jax
import jax.numpy as jnp
import numpy as np
from jax import lax
from jax.experimental import pallas as pl
from jax.experimental.pallas import tpu as pltpu
from jax.sharding import PartitionSpec as P

KDIM = 128
VDIM = 256
SPAN = 64
LEVELS = 6
KINDS = LEVELS + 2
STEP_SPANS = 2
LANES = 128
UNPACK_FLOPS = 3 * 10**10

epsilon = 1e-06
head_epsilon = 1.0
gate_scale = 16.0
highest = lax.Precision.HIGHEST
f32 = jnp.float32
bf16 = jnp.bfloat16


def rms_forward(values, norm_gain, floor_value=epsilon):
    inverse = lax.rsqrt(jnp.mean(values * values, axis=-1, keepdims=True) + floor_value)
    return (values * inverse * norm_gain, inverse)


def rms_backward(values, inverse, norm_gain, upstream):
    scaled = upstream * norm_gain
    inner = jnp.mean(scaled * values, axis=-1, keepdims=True)
    grad_values = inverse * scaled - values * (inverse * inverse * inverse) * inner
    grad_gain = jnp.sum(upstream * values * inverse, axis=0)
    return (grad_values, grad_gain)


def group_layout(sequence_lengths, sequence_group, sequence_offset, which_group, places, span_count):
    live_record = (sequence_group == which_group) & (sequence_lengths > 0)
    start_row = sequence_offset * SPAN
    covered = (
        live_record[None, :]
        & (places >= start_row[None, :])
        & (places < (start_row + sequence_lengths)[None, :])
    )
    live_mask = jnp.any(covered, axis=1).astype(f32)
    span_ids = jnp.arange(span_count, dtype=jnp.int32)[:, None]
    restart = jnp.any(live_record[None, :] & (span_ids == sequence_offset[None, :]), axis=1)
    return (live_mask, restart.astype(jnp.int32))


def nn(left, right):
    return lax.dot_general(left, right, (((1,), (0,)), ((), ())), preferred_element_type=f32)


def nt(left, right):
    return lax.dot_general(left, right, (((1,), (1,)), ((), ())), preferred_element_type=f32)


def tn(left, right):
    return lax.dot_general(left, right, (((0,), (0,)), ((), ())), preferred_element_type=f32)


def decay_sums():
    rows = np.arange(SPAN)[:, None]
    cols = np.arange(SPAN)[None, :]
    blocks = [cols <= rows]
    for level in range(LEVELS):
        half = 1 << level
        edge = (rows // (2 * half)) * (2 * half) + half
        right = rows >= edge
        blocks.append(np.where(right, (cols >= edge) & (cols <= rows), (cols > rows) & (cols < edge)))
    blocks.append(cols > rows)
    return np.concatenate(blocks, axis=0).astype(np.float32)


def pair_levels():
    rows = lax.broadcasted_iota(jnp.int32, (SPAN, SPAN), 0)
    cols = lax.broadcasted_iota(jnp.int32, (SPAN, SPAN), 1)
    apart = rows ^ cols
    later = rows > cols
    masks = [later & (lax.shift_right_logical(apart, level) == 1) for level in range(LEVELS)]
    return masks, rows == cols


def span_factors(z_part, sums):
    decays = (jnp.minimum(z_part, 0.0) - jnp.log1p(jnp.exp(-jnp.abs(z_part)))) * (1.0 / gate_scale)
    high = decays.astype(bf16)
    low = (decays - high.astype(f32)).astype(bf16)
    return jnp.exp(nn(sums, jnp.concatenate([high, low], axis=0)))


def span_scores(queries, keys, factors, masks, diagonal):
    scores = jnp.where(diagonal, nt(queries.astype(bf16), keys.astype(bf16)), 0.0)
    query_levels = []
    key_levels = []
    for level in range(LEVELS):
        factor = factors[(level + 1) * SPAN : (level + 2) * SPAN]
        query_level = (queries * factor).astype(bf16)
        key_level = (keys * factor).astype(bf16)
        scores = jnp.where(masks[level], nt(query_level, key_level), scores)
        query_levels.append(query_level)
        key_levels.append(key_level)
    return scores, query_levels, key_levels


def forward_kernel(heads, scal, projected, z, live, gain, sums, gated, mixture, states, state):
    step = pl.program_id(0)
    key_width = heads * KDIM
    value_width = heads * VDIM

    @pl.when(step == 0)
    def _():
        state[...] = jnp.zeros_like(state)

    masks, diagonal = pair_levels()
    head_gain = gain[...]
    for part in range(STEP_SPANS):
        rows = slice(part * SPAN, (part + 1) * SPAN)
        factors_all = span_factors(z[rows, :], sums[...])
        keep = jnp.where(scal[1 + step * STEP_SPANS + part] == 0, 1.0, 0.0)
        for head in range(heads):
            keys_at = slice(head * KDIM, (head + 1) * KDIM)
            queries = projected[rows, keys_at].astype(f32)
            keys = projected[rows, key_width + head * KDIM : key_width + (head + 1) * KDIM].astype(f32)
            value_at = 2 * key_width + head * VDIM
            values = projected[rows, value_at : value_at + VDIM]
            gating = projected[rows, value_at + value_width : value_at + value_width + VDIM].astype(f32)
            factors = factors_all[:, keys_at]
            scores, _, _ = span_scores(queries, keys, factors, masks, diagonal)
            entering = state[head] * keep
            entering_low = entering.astype(bf16)
            states[part, head] = entering_low
            whole = factors[:SPAN]
            after = factors[(KINDS - 1) * SPAN :]
            mixed = nn(scores.astype(bf16), values) + nt(
                (queries * whole).astype(bf16), entering_low
            )
            state[head] = entering * whole[SPAN - 1 :] + tn(values, (keys * after).astype(bf16))
            value_cols = slice(head * VDIM, (head + 1) * VDIM)
            mixture[rows, value_cols] = mixed.astype(bf16)
            inverse = lax.rsqrt(jnp.mean(mixed * mixed, axis=-1, keepdims=True) + head_epsilon)
            silu = gating * jax.nn.sigmoid(gating)
            gated[rows, value_cols] = (mixed * inverse * head_gain * silu * live[rows, :]).astype(bf16)


def backward_kernel(
    heads,
    scal,
    projected,
    z,
    live,
    gain,
    sums,
    mixture,
    states,
    grad_gated,
    latent,
    up,
    grad_projected,
    grad_gain,
    grad_up,
    grad_bias,
    grad_state,
):
    step = pl.program_id(0)
    natural = pl.num_programs(0) - 1 - step
    key_width = heads * KDIM
    value_width = heads * VDIM

    @pl.when(step == 0)
    def _():
        grad_state[...] = jnp.zeros_like(grad_state)
        grad_gain[...] = jnp.zeros_like(grad_gain)
        grad_up[...] = jnp.zeros_like(grad_up)
        grad_bias[...] = jnp.zeros_like(grad_bias)

    masks, diagonal = pair_levels()
    head_gain = gain[...]
    last_row = lax.broadcasted_iota(jnp.int32, (SPAN, KDIM), 0) == SPAN - 1
    for part in reversed(range(STEP_SPANS)):
        rows = slice(part * SPAN, (part + 1) * SPAN)
        z_part = z[rows, :]
        factors_all = span_factors(z_part, sums[...])
        keep = jnp.where(scal[1 + natural * STEP_SPANS + part] == 0, 1.0, 0.0)
        live_part = live[rows, :]
        exponents = []
        for head in range(heads):
            keys_at = slice(head * KDIM, (head + 1) * KDIM)
            key_cols = slice(key_width + head * KDIM, key_width + (head + 1) * KDIM)
            value_at = 2 * key_width + head * VDIM
            value_cols = slice(value_at, value_at + VDIM)
            gate_cols = slice(value_at + value_width, value_at + value_width + VDIM)
            mixed_cols = slice(head * VDIM, (head + 1) * VDIM)
            queries = projected[rows, keys_at].astype(f32)
            keys = projected[rows, key_cols].astype(f32)
            values = projected[rows, value_cols]
            gating = projected[rows, gate_cols].astype(f32)
            factors = factors_all[:, keys_at]
            scores, query_levels, key_levels = span_scores(queries, keys, factors, masks, diagonal)
            scores_low = scores.astype(bf16)
            whole = factors[:SPAN]
            after = factors[(KINDS - 1) * SPAN :]

            mixed = mixture[rows, mixed_cols].astype(f32)
            inverse = lax.rsqrt(jnp.mean(mixed * mixed, axis=-1, keepdims=True) + head_epsilon)
            unit = mixed * inverse
            sigmoid = jax.nn.sigmoid(gating)
            silu = gating * sigmoid
            upstream = grad_gated[rows, mixed_cols].astype(f32) * live_part
            grad_projected[rows, gate_cols] = (
                upstream * unit * head_gain * (sigmoid + silu * (1.0 - sigmoid))
            ).astype(bf16)
            normed_back = upstream * silu
            gain_part = normed_back * unit
            grad_gain[...] += jnp.sum(gain_part.reshape(SPAN // 8, 8, VDIM), axis=0)
            scaled = normed_back * head_gain
            inner = jnp.mean(scaled * unit, axis=-1, keepdims=True)
            grad_mixed = (inverse * (scaled - unit * inner)).astype(bf16)

            entering = states[part, head]
            leaving = grad_state[head]
            leaving_low = leaving.astype(bf16)
            grad_scores = nt(grad_mixed, values)
            after_keys = (keys * after).astype(bf16)
            whole_queries = (queries * whole).astype(bf16)
            grad_projected[rows, value_cols] = (
                tn(scores_low, grad_mixed) + nt(after_keys, leaving_low)
            ).astype(bf16)
            grad_queries = whole * nn(grad_mixed, entering)
            grad_keys = after * nn(values, leaving_low)
            fading = whole[SPAN - 1 :]
            last_sum = fading * jnp.sum(entering.astype(f32) * leaving, axis=0, keepdims=True)
            exponents_head = [queries * grad_queries + jnp.where(last_row, last_sum, 0.0)]
            last_exponent = keys * grad_keys
            for level in range(LEVELS):
                factor = factors[(level + 1) * SPAN : (level + 2) * SPAN]
                level_back = jnp.where(masks[level], grad_scores, 0.0).astype(bf16)
                query_part = factor * nn(level_back, key_levels[level])
                key_part = factor * tn(level_back, query_levels[level])
                grad_queries += query_part
                grad_keys += key_part
                exponents_head.append(queries * query_part + keys * key_part)
            exponents_head.append(last_exponent)
            same = jnp.sum(jnp.where(diagonal, grad_scores, 0.0), axis=1, keepdims=True)
            grad_projected[rows, keys_at] = (grad_queries + same * keys).astype(bf16)
            grad_projected[rows, key_cols] = (grad_keys + same * queries).astype(bf16)
            exponents.append(jnp.concatenate(exponents_head, axis=0).astype(bf16))
            grad_state[head] = keep * (leaving * fading + tn(grad_mixed, whole_queries))
        grad_decays = tn(sums[:, :SPAN], jnp.concatenate(exponents, axis=1))
        grad_z = grad_decays * jax.nn.sigmoid(-z_part) * (1.0 / gate_scale)
        grad_bias[...] += jnp.sum(grad_z.reshape(SPAN // 8, 8, key_width), axis=0)
        grad_z_low = grad_z.astype(bf16)
        grad_up[...] += tn(latent[rows, :], grad_z_low)
        latent_cols = slice(2 * key_width + 2 * value_width, grad_projected.shape[1])
        grad_projected[rows, latent_cols] = nt(grad_z_low, up[...]).astype(bf16)


def mixer_specs(length, projected_width, key_width, value_width, reverse):
    steps = length // (SPAN * STEP_SPANS)
    step_rows = SPAN * STEP_SPANS
    heads = key_width // KDIM

    def natural(step):
        return steps - 1 - step if reverse else step

    def by_rows(step, scal):
        return (lax.rem(natural(step) + scal[0] * (steps // 2), steps), 0)

    def whole(step, scal):
        return (0, 0)

    return dict(
        steps=steps,
        projected=pl.BlockSpec((step_rows, projected_width), by_rows),
        z=pl.BlockSpec((step_rows, key_width), by_rows),
        live=pl.BlockSpec((step_rows, 1), by_rows),
        gain=pl.BlockSpec((1, VDIM), whole),
        sums=pl.BlockSpec((KINDS * SPAN, 2 * SPAN), whole),
        values=pl.BlockSpec((step_rows, value_width), by_rows),
        states=pl.BlockSpec(
            (STEP_SPANS, heads, VDIM, KDIM), lambda step, scal: (natural(step), 0, 0, 0)
        ),
        gain_grad=pl.BlockSpec((8, VDIM), whole),
        latent=pl.BlockSpec((step_rows, LANES), by_rows),
        up=pl.BlockSpec((LANES, key_width), whole),
        extended=pl.BlockSpec((step_rows, projected_width + LANES), by_rows),
        bias_grad=pl.BlockSpec((8, key_width), whole),
    )


def mixer_forward(scal, projected, z, live, gain, sums):
    length, projected_width = projected.shape
    key_width = z.shape[1]
    heads = key_width // KDIM
    value_width = heads * VDIM
    spans = length // SPAN
    specs = mixer_specs(length, projected_width, key_width, value_width, False)
    return pl.pallas_call(
        functools.partial(forward_kernel, heads),
        grid_spec=pltpu.PrefetchScalarGridSpec(
            num_scalar_prefetch=1,
            grid=(specs["steps"],),
            in_specs=[specs[name] for name in ("projected", "z", "live", "gain", "sums")],
            out_specs=[specs[name] for name in ("values", "values", "states")],
            scratch_shapes=[pltpu.VMEM((heads, VDIM, KDIM), f32)],
        ),
        out_shape=[
            jax.ShapeDtypeStruct((length, value_width), bf16),
            jax.ShapeDtypeStruct((length, value_width), bf16),
            jax.ShapeDtypeStruct((spans, heads, VDIM, KDIM), bf16),
        ],
        compiler_params=pltpu.CompilerParams(vmem_limit_bytes=40 * 1024 * 1024),
        cost_estimate=pl.CostEstimate(
            flops=10**10, bytes_accessed=15 * 10**6, transcendentals=4 * 10**6
        ),
        name="mixer_forward",
    )(scal, projected, z, live, gain, sums)


def mixer_backward(
    scal, projected, z, live, gain, sums, mixture, states, grad_gated, latent, up
):
    length, projected_width = projected.shape
    key_width = z.shape[1]
    heads = key_width // KDIM
    value_width = heads * VDIM
    specs = mixer_specs(length, projected_width, key_width, value_width, True)
    names = ("projected", "z", "live", "gain", "sums", "values", "states", "values")
    names += ("latent", "up")
    return pl.pallas_call(
        functools.partial(backward_kernel, heads),
        grid_spec=pltpu.PrefetchScalarGridSpec(
            num_scalar_prefetch=1,
            grid=(specs["steps"],),
            in_specs=[specs[name] for name in names],
            out_specs=[specs[name] for name in ("extended", "gain_grad", "up", "bias_grad")],
            scratch_shapes=[pltpu.VMEM((heads, VDIM, KDIM), f32)],
        ),
        out_shape=[
            jax.ShapeDtypeStruct((length, projected_width + LANES), bf16),
            jax.ShapeDtypeStruct((8, VDIM), f32),
            jax.ShapeDtypeStruct((LANES, key_width), f32),
            jax.ShapeDtypeStruct((8, key_width), f32),
        ],
        compiler_params=pltpu.CompilerParams(vmem_limit_bytes=40 * 1024 * 1024),
        cost_estimate=pl.CostEstimate(
            flops=25 * 10**9, bytes_accessed=20 * 10**6, transcendentals=4 * 10**6
        ),
        name="mixer_backward",
    )(scal, projected, z, live, gain, sums, mixture, states, grad_gated, latent, up)


def unpack_kernel(packed, *parts):
    width = parts[0].shape[1]
    for index, part in enumerate(parts):
        part[...] = packed[:, index * width : (index + 1) * width].astype(f32)


def unpack_thirds(packed):
    rows, width = packed.shape[0], packed.shape[1] // 3
    return pl.pallas_call(
        unpack_kernel,
        out_shape=[jax.ShapeDtypeStruct((rows, width), f32)] * 3,
        compiler_params=pltpu.CompilerParams(vmem_limit_bytes=8 * 1024 * 1024),
        cost_estimate=pl.CostEstimate(
            flops=UNPACK_FLOPS, bytes_accessed=3 * 10**6, transcendentals=0
        ),
        name="unpack_thirds",
    )(packed)


def lane_pad(values, axis):
    widths = [(0, 0), (0, 0)]
    widths[axis] = (0, LANES - values.shape[axis])
    return jnp.pad(values, widths)


def swap_tensor(values):
    return lax.ppermute(values, "tensor", [(0, 1), (1, 0)])


def chip_sum(values):
    count = lax.axis_size("dp")
    parity = lax.axis_index("dp") % 2
    blocks = values.reshape(count // 2, 2, values.shape[0] // count, values.shape[1])
    kept = lax.dynamic_index_in_dim(blocks, parity, 1, keepdims=False)
    sent = lax.dynamic_index_in_dim(blocks, 1 - parity, 1, keepdims=False)
    arrived = lax.ppermute(sent, "dp", [(i, i ^ 1) for i in range(count)])
    total = (kept.astype(f32) + arrived.astype(f32)).astype(bf16)
    return total.reshape(values.shape[0] // 2, values.shape[1])


def halving_stages():
    return (lax.axis_size("dp") // 2).bit_length() - 1


def by_chip(values):
    stages = halving_stages()
    return values.reshape((2,) * stages + (values.shape[0] >> stages, values.shape[1]))


def halving_stage(held, stage):
    count = lax.axis_size("dp")
    stages = halving_stages()
    bit = 2 << stage
    side = (lax.axis_index("dp") // bit) % 2
    axis = stages - 1 - stage
    kept = lax.dynamic_index_in_dim(held, side, axis, keepdims=False)
    sent = lax.dynamic_index_in_dim(held, 1 - side, axis, keepdims=False)
    arrived = lax.ppermute(sent, "dp", [(i, i ^ bit) for i in range(count)])
    total = kept.astype(f32) + arrived.astype(f32)
    return total if stage == stages - 1 else total.astype(bf16)


def halving_rest(held):
    for stage in range(1, halving_stages()):
        held = halving_stage(held, stage)
    return held


def both_ways(side, mine, other, axis):
    first = jnp.where(side == 0, mine, other)
    second = jnp.where(side == 0, other, mine)
    return jnp.stack([first, second], axis=axis)


def swap_half(values):
    half = values.shape[0] // 2
    parity = lax.axis_index("dp") % 2
    return swap_tensor(lax.dynamic_slice_in_dim(values, parity * half, half, 0))


def join_halves(mine):
    count = lax.axis_size("dp")
    parity = lax.axis_index("dp") % 2
    other = lax.ppermute(mine, "dp", [(i, i ^ 1) for i in range(count)])
    return both_ways(parity, mine, other, 0).reshape(mine.shape[0] * 2, mine.shape[1])


def butterfly_sum(values):
    total = values + swap_tensor(values)
    count = lax.axis_size("dp")
    reach = 1
    while reach < count:
        total = total + lax.ppermute(total, "dp", [(i, i ^ reach) for i in range(count)])
        reach *= 2
    return total


def on_device(
    tokens,
    cotangent,
    sequence_lengths,
    sequence_group,
    sequence_offset,
    mixer_gain,
    query_weight,
    key_weight,
    value_weight,
    output_gate,
    output_weight,
    decay_down,
    decay_up,
    decay_bias,
    head_gain,
    feed_gain,
    feed_gate,
    feed_up,
    feed_down,
):
    which_group = lax.axis_index("dp")
    half_index = lax.axis_index("tensor")
    own = tokens.shape[0]
    group_rows = own * 2
    key_width = query_weight.shape[1]
    value_width = value_weight.shape[1]
    feed_width = feed_gate.shape[1]
    places = (jnp.arange(group_rows, dtype=jnp.int32) + half_index * own) % group_rows
    live_mask, restart = group_layout(
        sequence_lengths,
        sequence_group,
        sequence_offset,
        which_group,
        places[:, None],
        group_rows // SPAN,
    )
    live = live_mask[:, None]
    scal = jnp.concatenate([half_index.astype(jnp.int32)[None], restart])
    sums = jnp.asarray(np.tile(decay_sums(), (1, 2)), bf16)
    gain_head = head_gain.astype(f32)[None, :]

    joined = lax.all_gather(
        jnp.concatenate(
            [query_weight, key_weight, value_weight, output_gate, output_weight], axis=1
        ),
        "dp",
        axis=0,
        tiled=True,
    )
    feed_all = lax.all_gather(
        jnp.concatenate([feed_gate, feed_up, feed_down], axis=1), "dp", axis=0, tiled=True
    )
    gate_up_full = feed_all[:, : 2 * feed_width]
    feed_down_full = feed_all[:, 2 * feed_width :]
    gain_in = mixer_gain.astype(f32)
    token_values = tokens.astype(f32)
    normed_in, inverse_in = rms_forward(token_values, gain_in)
    normed_low = normed_in.astype(bf16)
    normed_other = swap_tensor(normed_low)
    cotangent_other = swap_tensor(cotangent)
    joined, cotangent_other = lax.optimization_barrier((joined, cotangent_other))
    projected_width = 2 * key_width + 2 * value_width
    joined_in = joined[:, :projected_width]
    output_half = joined[:, projected_width:]
    output_piece = swap_half(output_half)

    normed_all = jnp.concatenate([normed_low, normed_other], axis=0)
    projected = nn(normed_all, joined_in).astype(bf16)
    latent = nn(normed_all, decay_down)
    up_local = lax.dynamic_slice_in_dim(decay_up, half_index * key_width, key_width, 1).astype(f32)
    bias_local = lax.dynamic_slice_in_dim(decay_bias, half_index * key_width, key_width, 0)
    z = jnp.dot(latent, up_local, precision=highest) + bias_local.astype(f32)
    gated, mixture, states = mixer_forward(scal, projected, z, live, gain_head, sums)

    gated, output_piece = lax.optimization_barrier((gated, output_piece))
    output_other = join_halves(output_piece)
    gated_own = gated[:own]
    gated_rest = swap_tensor(gated[own:])
    attended = nt(gated_own, output_half) + nt(gated_rest, output_other)
    middle = token_values + attended
    gain_mid = feed_gain.astype(f32)
    normed_mid, inverse_mid = rms_forward(middle, gain_mid)
    mid_low = normed_mid.astype(bf16)
    mid_other = swap_tensor(mid_low)

    def feed_rows(mid_rows, cotangent_rows):
        both = nn(mid_rows, gate_up_full)
        gate_part = both[:, :feed_width]
        up_part = both[:, feed_width:]
        sigmoid_gate = jax.nn.sigmoid(gate_part)
        silu_gate = gate_part * sigmoid_gate
        hidden_low = (silu_gate * up_part).astype(bf16)
        grad_hidden = nn(cotangent_rows, feed_down_full)
        grad_gate_low = (
            grad_hidden * up_part * (sigmoid_gate + silu_gate * (1.0 - sigmoid_gate))
        ).astype(bf16)
        grad_up_low = (grad_hidden * silu_gate).astype(bf16)
        grad_both = jnp.concatenate([grad_gate_low, grad_up_low], axis=1)
        return hidden_low, grad_both, nt(grad_both, gate_up_full)

    hidden_other, grad_both_other, mid_back_other = feed_rows(mid_other, cotangent_other)
    mid_send, mid_here, cotangent_here = lax.optimization_barrier(
        (mid_back_other.astype(bf16), mid_low, cotangent)
    )
    mid_back = swap_tensor(mid_send)
    hidden_own, grad_both_own, mid_back_own = feed_rows(mid_here, cotangent_here)

    upstream = cotangent.astype(f32)
    grad_normed_mid = mid_back_own + mid_back.astype(f32)
    grad_mid_in, grad_feed_gain = rms_backward(middle, inverse_mid, gain_mid, grad_normed_mid)
    grad_middle = upstream + grad_mid_in
    grad_attended = grad_middle.astype(bf16)
    gated_back = swap_tensor(nn(grad_attended, output_other).astype(bf16))
    grad_gated = jnp.concatenate([nn(grad_attended, output_half).astype(bf16), gated_back], axis=0)

    mid_all = jnp.concatenate([mid_low, mid_other], axis=0)
    cotangent_all = jnp.concatenate([cotangent, cotangent_other], axis=0)
    hidden_all = jnp.concatenate([hidden_own, hidden_other], axis=0)
    grad_both_all = jnp.concatenate([grad_both_own, grad_both_other], axis=0)
    feed_grads = jnp.concatenate(
        [
            tn(mid_all, grad_both_all).astype(bf16),
            tn(cotangent_all, hidden_all).astype(bf16),
        ],
        axis=1,
    )
    fed_send = nt(hidden_other, feed_down_full).astype(bf16)
    output_chip = chip_sum(
        jnp.concatenate(
            [
                tn(grad_attended, gated_own).astype(bf16),
                tn(grad_attended, gated_rest).astype(bf16),
            ],
            axis=1,
        )
    )
    grad_gated, feed_grads, fed_send, output_chip = lax.optimization_barrier(
        (grad_gated, feed_grads, fed_send, output_chip)
    )
    feed_sum = lax.psum_scatter(feed_grads, "dp", scatter_dimension=0, tiled=True)
    fed_back = swap_tensor(fed_send)
    output_back = swap_tensor(output_chip[:, value_width:])
    grad_projected, grad_gain_rows, grad_up_rows, grad_bias_rows = mixer_backward(
        scal,
        projected,
        z,
        live,
        gain_head,
        sums,
        mixture,
        states,
        grad_gated,
        lane_pad(latent, 1).astype(bf16),
        lane_pad(up_local, 0).astype(bf16),
    )
    grad_joined = tn(normed_all, grad_projected).astype(bf16)
    grad_joined, output_back = lax.optimization_barrier((grad_joined, output_back))
    low_rank = decay_down.shape[1]
    grad_decay_down = grad_joined[:, projected_width : projected_width + low_rank].astype(f32)
    output_total = output_chip[:, :value_width].astype(f32) + output_back.astype(f32)
    joined_chip = jnp.concatenate(
        [chip_sum(grad_joined[:, :projected_width]), output_total.astype(bf16)], axis=1
    )
    joined_sums = [
        halving_stage(by_chip(piece), 0) for piece in jnp.split(joined_chip, 2, axis=1)
    ]

    joined_back = jnp.concatenate([joined_in, lane_pad(decay_down, 1)], axis=1)
    normed_part = nt(grad_projected, joined_back)
    grad_mixer_gain = jnp.sum(normed_part * normed_all.astype(f32), axis=0) / gain_in
    normed_part, fed_back = lax.optimization_barrier((normed_part.astype(bf16), fed_back))
    hidden_late, normed_part = lax.optimization_barrier((hidden_own, normed_part))
    fed = nt(hidden_late, feed_down_full) + fed_back.astype(f32)
    output = (middle + fed).astype(bf16)
    normed_back, joined_sums[1] = lax.optimization_barrier(
        (swap_tensor(normed_part[own:]), joined_sums[1])
    )
    grad_normed = normed_part[:own].astype(f32) + normed_back.astype(f32)
    grad_in_part = rms_backward(token_values, inverse_in, gain_in, grad_normed)[0]
    input_grad = grad_middle + grad_in_part

    up_full = lax.dynamic_update_slice_in_dim(
        jnp.zeros(decay_up.shape, f32), grad_up_rows[:low_rank], half_index * key_width, 1
    )
    bias_full = lax.dynamic_update_slice_in_dim(
        jnp.zeros(decay_bias.shape, f32), jnp.sum(grad_bias_rows, axis=0), half_index * key_width, 0
    )
    small = (
        grad_mixer_gain,
        grad_decay_down,
        up_full,
        bias_full,
        jnp.sum(grad_gain_rows, axis=0),
        grad_feed_gain,
    )
    flat = jnp.concatenate([part.reshape(-1, 128) for part in small], axis=0)
    flat, joined_sums[0] = lax.optimization_barrier((flat, joined_sums[0]))
    flat = butterfly_sum(flat)
    joined_sum = jnp.concatenate([halving_rest(held) for held in joined_sums], axis=1)
    small_sums = []
    row = 0
    for part in small:
        taken = part.size // 128
        small_sums.append(flat[row : row + taken].reshape(part.shape))
        row += taken
    return (
        output,
        input_grad,
        small_sums[0],
        joined_sum[:, :key_width],
        joined_sum[:, key_width : 2 * key_width],
        joined_sum[:, 2 * key_width : 2 * key_width + value_width],
        joined_sum[:, 2 * key_width + value_width : projected_width],
        joined_sum[:, projected_width:],
        small_sums[1],
        small_sums[2],
        small_sums[3],
        small_sums[4],
        small_sums[5],
        *unpack_thirds(feed_sum),
    )


def solution(mesh):
    rows = P(("dp", "tensor"), None)
    weight = P("dp", "tensor")
    return jax.shard_map(
        on_device,
        mesh=mesh,
        in_specs=(rows, rows, P(), P(), P(), P())
        + (weight,) * 5
        + (P(), P(), P(), P(), P())
        + (weight,) * 3,
        out_specs=(rows, rows, P()) + (weight,) * 5 + (P(),) * 5 + (weight,) * 3,
        check_vma=False,
    )
```

```python
import functools

import jax
import jax.numpy as jnp
import numpy as np
from jax import lax
from jax.experimental import pallas as pl
from jax.experimental.pallas import tpu as pltpu
from jax.sharding import PartitionSpec as P

KDIM = 128
VDIM = 256
SPAN = 64
LEVELS = 6
KINDS = LEVELS + 2
STEP_SPANS = 2
LANES = 128
LOWRANK = 16
DOWN_ROWS = slice(0, LOWRANK)
UP_ROWS = slice(LOWRANK, 2 * LOWRANK)
BIAS_ROWS = slice(2 * LOWRANK, 2 * LOWRANK + 8)
FEED_GAIN_ROW = 2 * LOWRANK + 8
MIXER_GAIN_ROW = FEED_GAIN_ROW + 1
PACKED_ROWS = FEED_GAIN_ROW + 8
UNPACK_FLOPS = 3 * 10**10

epsilon = 1e-06
head_epsilon = 1.0
gate_scale = 16.0
highest = lax.Precision.HIGHEST
f32 = jnp.float32
bf16 = jnp.bfloat16


def rms_forward(values, norm_gain, floor_value=epsilon):
    inverse = lax.rsqrt(jnp.mean(values * values, axis=-1, keepdims=True) + floor_value)
    return (values * inverse * norm_gain, inverse)


def rms_backward(values, inverse, norm_gain, upstream):
    scaled = upstream * norm_gain
    inner = jnp.mean(scaled * values, axis=-1, keepdims=True)
    grad_values = inverse * scaled - values * (inverse * inverse * inverse) * inner
    grad_gain = jnp.sum(upstream * values * inverse, axis=0)
    return (grad_values, grad_gain)


def group_layout(sequence_lengths, sequence_group, sequence_offset, which_group, places, span_count):
    live_record = (sequence_group == which_group) & (sequence_lengths > 0)
    start_row = sequence_offset * SPAN
    covered = (
        live_record[None, :]
        & (places >= start_row[None, :])
        & (places < (start_row + sequence_lengths)[None, :])
    )
    live_mask = jnp.any(covered, axis=1).astype(f32)
    span_ids = jnp.arange(span_count, dtype=jnp.int32)[:, None]
    restart = jnp.any(live_record[None, :] & (span_ids == sequence_offset[None, :]), axis=1)
    return (live_mask, restart.astype(jnp.int32))


def nn(left, right):
    return lax.dot_general(left, right, (((1,), (0,)), ((), ())), preferred_element_type=f32)


def nt(left, right):
    return lax.dot_general(left, right, (((1,), (1,)), ((), ())), preferred_element_type=f32)


def tn(left, right):
    return lax.dot_general(left, right, (((0,), (0,)), ((), ())), preferred_element_type=f32)


def decay_sums():
    rows = np.arange(SPAN)[:, None]
    cols = np.arange(SPAN)[None, :]
    blocks = [cols <= rows]
    for level in range(LEVELS):
        half = 1 << level
        edge = (rows // (2 * half)) * (2 * half) + half
        right = rows >= edge
        blocks.append(np.where(right, (cols >= edge) & (cols <= rows), (cols > rows) & (cols < edge)))
    blocks.append(cols > rows)
    return np.concatenate(blocks, axis=0).astype(np.float32)


def pair_levels():
    rows = lax.broadcasted_iota(jnp.int32, (SPAN, SPAN), 0)
    cols = lax.broadcasted_iota(jnp.int32, (SPAN, SPAN), 1)
    apart = rows ^ cols
    later = rows > cols
    masks = [later & (lax.shift_right_logical(apart, level) == 1) for level in range(LEVELS)]
    return masks, rows == cols


def span_factors(z_part, sums):
    decays = (jnp.minimum(z_part, 0.0) - jnp.log1p(jnp.exp(-jnp.abs(z_part)))) * (1.0 / gate_scale)
    high = decays.astype(bf16)
    low = (decays - high.astype(f32)).astype(bf16)
    return jnp.exp(nn(sums, jnp.concatenate([high, low], axis=0)))


def span_scores(queries, keys, factors, masks, diagonal):
    scores = jnp.where(diagonal, nt(queries.astype(bf16), keys.astype(bf16)), 0.0)
    query_levels = []
    key_levels = []
    for level in range(LEVELS):
        factor = factors[(level + 1) * SPAN : (level + 2) * SPAN]
        query_level = (queries * factor).astype(bf16)
        key_level = (keys * factor).astype(bf16)
        scores = jnp.where(masks[level], nt(query_level, key_level), scores)
        query_levels.append(query_level)
        key_levels.append(key_level)
    return scores, query_levels, key_levels


def forward_kernel(heads, scal, projected, z, live, gain, sums, gated, mixture, states, state):
    step = pl.program_id(0)
    key_width = heads * KDIM
    value_width = heads * VDIM

    @pl.when(step == 0)
    def _():
        state[...] = jnp.zeros_like(state)

    masks, diagonal = pair_levels()
    head_gain = gain[...]
    for part in range(STEP_SPANS):
        rows = slice(part * SPAN, (part + 1) * SPAN)
        factors_all = span_factors(z[rows, :], sums[...])
        keep = jnp.where(scal[1 + step * STEP_SPANS + part] == 0, 1.0, 0.0)
        for head in range(heads):
            keys_at = slice(head * KDIM, (head + 1) * KDIM)
            queries = projected[rows, keys_at].astype(f32)
            keys = projected[rows, key_width + head * KDIM : key_width + (head + 1) * KDIM].astype(f32)
            value_at = 2 * key_width + head * VDIM
            values = projected[rows, value_at : value_at + VDIM]
            gating = projected[rows, value_at + value_width : value_at + value_width + VDIM].astype(f32)
            factors = factors_all[:, keys_at]
            scores, _, _ = span_scores(queries, keys, factors, masks, diagonal)
            entering = state[head] * keep
            entering_low = entering.astype(bf16)
            states[part, head] = entering_low
            whole = factors[:SPAN]
            after = factors[(KINDS - 1) * SPAN :]
            mixed = nn(scores.astype(bf16), values) + nt(
                (queries * whole).astype(bf16), entering_low
            )
            state[head] = entering * whole[SPAN - 1 :] + tn(values, (keys * after).astype(bf16))
            value_cols = slice(head * VDIM, (head + 1) * VDIM)
            mixture[rows, value_cols] = mixed.astype(bf16)
            inverse = lax.rsqrt(jnp.mean(mixed * mixed, axis=-1, keepdims=True) + head_epsilon)
            silu = gating * jax.nn.sigmoid(gating)
            gated[rows, value_cols] = (mixed * inverse * head_gain * silu * live[rows, :]).astype(bf16)


def backward_kernel(
    heads,
    scal,
    projected,
    z,
    live,
    gain,
    sums,
    mixture,
    states,
    grad_gated,
    latent,
    up,
    normed,
    feed_gain_grad,
    grad_projected,
    packed,
    grad_up,
    grad_bias,
    grad_state,
):
    step = pl.program_id(0)
    natural = pl.num_programs(0) - 1 - step
    key_width = heads * KDIM
    value_width = heads * VDIM

    @pl.when(step == 0)
    def _():
        grad_state[...] = jnp.zeros_like(grad_state)
        packed[...] = jnp.zeros_like(packed)
        packed[FEED_GAIN_ROW : FEED_GAIN_ROW + 1, :] = feed_gain_grad[...]
        grad_up[...] = jnp.zeros_like(grad_up)
        grad_bias[...] = jnp.zeros_like(grad_bias)

    gain_at = slice(2 * key_width, 2 * key_width + VDIM)
    masks, diagonal = pair_levels()
    head_gain = gain[...]
    last_row = lax.broadcasted_iota(jnp.int32, (SPAN, KDIM), 0) == SPAN - 1
    for part in reversed(range(STEP_SPANS)):
        rows = slice(part * SPAN, (part + 1) * SPAN)
        z_part = z[rows, :]
        factors_all = span_factors(z_part, sums[...])
        keep = jnp.where(scal[1 + natural * STEP_SPANS + part] == 0, 1.0, 0.0)
        live_part = live[rows, :]
        exponents = []
        for head in range(heads):
            keys_at = slice(head * KDIM, (head + 1) * KDIM)
            key_cols = slice(key_width + head * KDIM, key_width + (head + 1) * KDIM)
            value_at = 2 * key_width + head * VDIM
            value_cols = slice(value_at, value_at + VDIM)
            gate_cols = slice(value_at + value_width, value_at + value_width + VDIM)
            mixed_cols = slice(head * VDIM, (head + 1) * VDIM)
            queries = projected[rows, keys_at].astype(f32)
            keys = projected[rows, key_cols].astype(f32)
            values = projected[rows, value_cols]
            gating = projected[rows, gate_cols].astype(f32)
            factors = factors_all[:, keys_at]
            scores, query_levels, key_levels = span_scores(queries, keys, factors, masks, diagonal)
            scores_low = scores.astype(bf16)
            whole = factors[:SPAN]
            after = factors[(KINDS - 1) * SPAN :]

            mixed = mixture[rows, mixed_cols].astype(f32)
            inverse = lax.rsqrt(jnp.mean(mixed * mixed, axis=-1, keepdims=True) + head_epsilon)
            unit = mixed * inverse
            sigmoid = jax.nn.sigmoid(gating)
            silu = gating * sigmoid
            upstream = grad_gated[rows, mixed_cols].astype(f32) * live_part
            grad_projected[rows, gate_cols] = (
                upstream * unit * head_gain * (sigmoid + silu * (1.0 - sigmoid))
            ).astype(bf16)
            normed_back = upstream * silu
            gain_part = normed_back * unit
            packed[BIAS_ROWS, gain_at] += jnp.sum(gain_part.reshape(SPAN // 8, 8, VDIM), axis=0)
            scaled = normed_back * head_gain
            inner = jnp.mean(scaled * unit, axis=-1, keepdims=True)
            grad_mixed = (inverse * (scaled - unit * inner)).astype(bf16)

            entering = states[part, head]
            leaving = grad_state[head]
            leaving_low = leaving.astype(bf16)
            grad_scores = nt(grad_mixed, values)
            after_keys = (keys * after).astype(bf16)
            whole_queries = (queries * whole).astype(bf16)
            grad_projected[rows, value_cols] = (
                tn(scores_low, grad_mixed) + nt(after_keys, leaving_low)
            ).astype(bf16)
            grad_queries = whole * nn(grad_mixed, entering)
            grad_keys = after * nn(values, leaving_low)
            fading = whole[SPAN - 1 :]
            last_sum = fading * jnp.sum(entering.astype(f32) * leaving, axis=0, keepdims=True)
            exponents_head = [queries * grad_queries + jnp.where(last_row, last_sum, 0.0)]
            last_exponent = keys * grad_keys
            for level in range(LEVELS):
                factor = factors[(level + 1) * SPAN : (level + 2) * SPAN]
                level_back = jnp.where(masks[level], grad_scores, 0.0).astype(bf16)
                query_part = factor * nn(level_back, key_levels[level])
                key_part = factor * tn(level_back, query_levels[level])
                grad_queries += query_part
                grad_keys += key_part
                exponents_head.append(queries * query_part + keys * key_part)
            exponents_head.append(last_exponent)
            same = jnp.sum(jnp.where(diagonal, grad_scores, 0.0), axis=1, keepdims=True)
            grad_projected[rows, keys_at] = (grad_queries + same * keys).astype(bf16)
            grad_projected[rows, key_cols] = (grad_keys + same * queries).astype(bf16)
            exponents.append(jnp.concatenate(exponents_head, axis=0).astype(bf16))
            grad_state[head] = keep * (leaving * fading + tn(grad_mixed, whole_queries))
        grad_decays = tn(sums[:, :SPAN], jnp.concatenate(exponents, axis=1))
        grad_z = grad_decays * jax.nn.sigmoid(-z_part) * (1.0 / gate_scale)
        grad_bias[...] += jnp.sum(grad_z.reshape(SPAN // 8, 8, key_width), axis=0)
        grad_z_low = grad_z.astype(bf16)
        grad_up[...] += tn(latent[rows, :LOWRANK], grad_z_low)
        latent_cols = slice(2 * key_width + 2 * value_width, grad_projected.shape[1])
        grad_latent = nt(grad_z_low, up[...]).astype(bf16)
        grad_projected[rows, latent_cols] = grad_latent
        packed[DOWN_ROWS, :] += tn(grad_latent[:, :LOWRANK], normed[rows, :])

    for half in range(2):

        @pl.when((step == pl.num_programs(0) - 1) & (scal[0] == half))
        def _(at=slice(half * key_width, (half + 1) * key_width)):
            packed[UP_ROWS, at] = grad_up[...]
            packed[BIAS_ROWS, at] = grad_bias[...]


def mixer_specs(length, projected_width, key_width, value_width, width, reverse):
    steps = length // (SPAN * STEP_SPANS)
    step_rows = SPAN * STEP_SPANS
    heads = key_width // KDIM

    def natural(step):
        return steps - 1 - step if reverse else step

    def by_rows(step, scal):
        return (lax.rem(natural(step) + scal[0] * (steps // 2), steps), 0)

    def whole(step, scal):
        return (0, 0)

    return dict(
        steps=steps,
        projected=pl.BlockSpec((step_rows, projected_width), by_rows),
        z=pl.BlockSpec((step_rows, key_width), by_rows),
        live=pl.BlockSpec((step_rows, 1), by_rows),
        gain=pl.BlockSpec((1, VDIM), whole),
        sums=pl.BlockSpec((KINDS * SPAN, 2 * SPAN), whole),
        values=pl.BlockSpec((step_rows, value_width), by_rows),
        states=pl.BlockSpec(
            (STEP_SPANS, heads, VDIM, KDIM), lambda step, scal: (natural(step), 0, 0, 0)
        ),
        normed=pl.BlockSpec((step_rows, width), by_rows),
        feed_gain=pl.BlockSpec((1, width), whole),
        packed=pl.BlockSpec((PACKED_ROWS, width), whole),
        latent=pl.BlockSpec((step_rows, LANES), by_rows),
        up=pl.BlockSpec((LANES, key_width), whole),
        extended=pl.BlockSpec((step_rows, projected_width + LANES), by_rows),
    )


def mixer_forward(scal, projected, z, live, gain, sums):
    length, projected_width = projected.shape
    key_width = z.shape[1]
    heads = key_width // KDIM
    value_width = heads * VDIM
    spans = length // SPAN
    specs = mixer_specs(length, projected_width, key_width, value_width, LANES, False)
    return pl.pallas_call(
        functools.partial(forward_kernel, heads),
        grid_spec=pltpu.PrefetchScalarGridSpec(
            num_scalar_prefetch=1,
            grid=(specs["steps"],),
            in_specs=[specs[name] for name in ("projected", "z", "live", "gain", "sums")],
            out_specs=[specs[name] for name in ("values", "values", "states")],
            scratch_shapes=[pltpu.VMEM((heads, VDIM, KDIM), f32)],
        ),
        out_shape=[
            jax.ShapeDtypeStruct((length, value_width), bf16),
            jax.ShapeDtypeStruct((length, value_width), bf16),
            jax.ShapeDtypeStruct((spans, heads, VDIM, KDIM), bf16),
        ],
        compiler_params=pltpu.CompilerParams(vmem_limit_bytes=40 * 1024 * 1024),
        cost_estimate=pl.CostEstimate(
            flops=10**10, bytes_accessed=15 * 10**6, transcendentals=4 * 10**6
        ),
        name="mixer_forward",
    )(scal, projected, z, live, gain, sums)


def mixer_backward(
    scal,
    projected,
    z,
    live,
    gain,
    sums,
    mixture,
    states,
    grad_gated,
    latent,
    up,
    normed,
    feed_gain_grad,
):
    length, projected_width = projected.shape
    key_width = z.shape[1]
    heads = key_width // KDIM
    value_width = heads * VDIM
    width = normed.shape[1]
    specs = mixer_specs(length, projected_width, key_width, value_width, width, True)
    names = ("projected", "z", "live", "gain", "sums", "values", "states", "values")
    names += ("latent", "up", "normed", "feed_gain")
    return pl.pallas_call(
        functools.partial(backward_kernel, heads),
        grid_spec=pltpu.PrefetchScalarGridSpec(
            num_scalar_prefetch=1,
            grid=(specs["steps"],),
            in_specs=[specs[name] for name in names],
            out_specs=[specs[name] for name in ("extended", "packed")],
            scratch_shapes=[
                pltpu.VMEM((LOWRANK, key_width), f32),
                pltpu.VMEM((8, key_width), f32),
                pltpu.VMEM((heads, VDIM, KDIM), f32),
            ],
        ),
        out_shape=[
            jax.ShapeDtypeStruct((length, projected_width + LANES), bf16),
            jax.ShapeDtypeStruct((PACKED_ROWS, width), f32),
        ],
        compiler_params=pltpu.CompilerParams(vmem_limit_bytes=40 * 1024 * 1024),
        cost_estimate=pl.CostEstimate(
            flops=25 * 10**9, bytes_accessed=20 * 10**6, transcendentals=4 * 10**6
        ),
        name="mixer_backward",
    )(
        scal,
        projected,
        z,
        live,
        gain,
        sums,
        mixture,
        states,
        grad_gated,
        latent,
        up,
        normed,
        feed_gain_grad,
    )


def unpack_kernel(packed, *parts):
    width = parts[0].shape[1]
    for index, part in enumerate(parts):
        part[...] = packed[:, index * width : (index + 1) * width].astype(f32)


def unpack_thirds(packed):
    rows, width = packed.shape[0], packed.shape[1] // 3
    return pl.pallas_call(
        unpack_kernel,
        out_shape=[jax.ShapeDtypeStruct((rows, width), f32)] * 3,
        compiler_params=pltpu.CompilerParams(vmem_limit_bytes=8 * 1024 * 1024),
        cost_estimate=pl.CostEstimate(
            flops=UNPACK_FLOPS, bytes_accessed=3 * 10**6, transcendentals=0
        ),
        name="unpack_thirds",
    )(packed)


def lane_pad(values, axis):
    widths = [(0, 0), (0, 0)]
    widths[axis] = (0, LANES - values.shape[axis])
    return jnp.pad(values, widths)


def swap_tensor(values):
    return lax.ppermute(values, "tensor", [(0, 1), (1, 0)])


def chip_sum(values):
    count = lax.axis_size("dp")
    parity = lax.axis_index("dp") % 2
    blocks = values.reshape(count // 2, 2, values.shape[0] // count, values.shape[1])
    kept = lax.dynamic_index_in_dim(blocks, parity, 1, keepdims=False)
    sent = lax.dynamic_index_in_dim(blocks, 1 - parity, 1, keepdims=False)
    arrived = lax.ppermute(sent, "dp", [(i, i ^ 1) for i in range(count)])
    total = (kept.astype(f32) + arrived.astype(f32)).astype(bf16)
    return total.reshape(values.shape[0] // 2, values.shape[1])


def halving_stages():
    return (lax.axis_size("dp") // 2).bit_length() - 1


def by_chip(values):
    stages = halving_stages()
    return values.reshape((2,) * stages + (values.shape[0] >> stages, values.shape[1]))


def halving_stage(held, stage):
    count = lax.axis_size("dp")
    stages = halving_stages()
    bit = 2 << stage
    side = (lax.axis_index("dp") // bit) % 2
    axis = stages - 1 - stage
    kept = lax.dynamic_index_in_dim(held, side, axis, keepdims=False)
    sent = lax.dynamic_index_in_dim(held, 1 - side, axis, keepdims=False)
    arrived = lax.ppermute(sent, "dp", [(i, i ^ bit) for i in range(count)])
    total = kept.astype(f32) + arrived.astype(f32)
    return total if stage == stages - 1 else total.astype(bf16)


def halving_rest(held):
    for stage in range(1, halving_stages()):
        held = halving_stage(held, stage)
    return held


def both_ways(side, mine, other, axis):
    first = jnp.where(side == 0, mine, other)
    second = jnp.where(side == 0, other, mine)
    return jnp.stack([first, second], axis=axis)


def swap_half(values):
    half = values.shape[0] // 2
    parity = lax.axis_index("dp") % 2
    return swap_tensor(lax.dynamic_slice_in_dim(values, parity * half, half, 0))


def join_halves(mine):
    count = lax.axis_size("dp")
    parity = lax.axis_index("dp") % 2
    other = lax.ppermute(mine, "dp", [(i, i ^ 1) for i in range(count)])
    return both_ways(parity, mine, other, 0).reshape(mine.shape[0] * 2, mine.shape[1])


def butterfly_sum(values):
    total = values + swap_tensor(values)
    count = lax.axis_size("dp")
    reach = 1
    while reach < count:
        total = total + lax.ppermute(total, "dp", [(i, i ^ reach) for i in range(count)])
        reach *= 2
    return total


def on_device(
    tokens,
    cotangent,
    sequence_lengths,
    sequence_group,
    sequence_offset,
    mixer_gain,
    query_weight,
    key_weight,
    value_weight,
    output_gate,
    output_weight,
    decay_down,
    decay_up,
    decay_bias,
    head_gain,
    feed_gain,
    feed_gate,
    feed_up,
    feed_down,
):
    which_group = lax.axis_index("dp")
    half_index = lax.axis_index("tensor")
    own = tokens.shape[0]
    group_rows = own * 2
    key_width = query_weight.shape[1]
    value_width = value_weight.shape[1]
    feed_width = feed_gate.shape[1]
    places = (jnp.arange(group_rows, dtype=jnp.int32) + half_index * own) % group_rows
    live_mask, restart = group_layout(
        sequence_lengths,
        sequence_group,
        sequence_offset,
        which_group,
        places[:, None],
        group_rows // SPAN,
    )
    live = live_mask[:, None]
    scal = jnp.concatenate([half_index.astype(jnp.int32)[None], restart])
    sums = jnp.asarray(np.tile(decay_sums(), (1, 2)), bf16)
    gain_head = head_gain.astype(f32)[None, :]

    joined = lax.all_gather(
        jnp.concatenate(
            [query_weight, key_weight, value_weight, output_gate, output_weight], axis=1
        ),
        "dp",
        axis=0,
        tiled=True,
    )
    feed_all = lax.all_gather(
        jnp.concatenate([feed_gate, feed_up, feed_down], axis=1), "dp", axis=0, tiled=True
    )
    gate_up_full = feed_all[:, : 2 * feed_width]
    feed_down_full = feed_all[:, 2 * feed_width :]
    gain_in = mixer_gain.astype(f32)
    token_values = tokens.astype(f32)
    normed_in, inverse_in = rms_forward(token_values, gain_in)
    normed_low = normed_in.astype(bf16)
    normed_other = swap_tensor(normed_low)
    cotangent_other = swap_tensor(cotangent)
    joined, cotangent_other = lax.optimization_barrier((joined, cotangent_other))
    projected_width = 2 * key_width + 2 * value_width
    joined_in = joined[:, :projected_width]
    output_half = joined[:, projected_width:]
    output_piece = swap_half(output_half)

    normed_all = jnp.concatenate([normed_low, normed_other], axis=0)
    projected = nn(normed_all, joined_in).astype(bf16)
    latent = nn(normed_all, decay_down)
    up_local = lax.dynamic_slice_in_dim(decay_up, half_index * key_width, key_width, 1).astype(f32)
    bias_local = lax.dynamic_slice_in_dim(decay_bias, half_index * key_width, key_width, 0)
    z = jnp.dot(latent, up_local, precision=highest) + bias_local.astype(f32)
    gated, mixture, states = mixer_forward(scal, projected, z, live, gain_head, sums)

    gated, output_piece = lax.optimization_barrier((gated, output_piece))
    output_other = join_halves(output_piece)
    gated_own = gated[:own]
    gated_rest = swap_tensor(gated[own:])
    attended = nt(gated_own, output_half) + nt(gated_rest, output_other)
    middle = token_values + attended
    gain_mid = feed_gain.astype(f32)
    normed_mid, inverse_mid = rms_forward(middle, gain_mid)
    mid_low = normed_mid.astype(bf16)
    mid_other = swap_tensor(mid_low)

    def feed_rows(mid_rows, cotangent_rows):
        both = nn(mid_rows, gate_up_full)
        gate_part = both[:, :feed_width]
        up_part = both[:, feed_width:]
        sigmoid_gate = jax.nn.sigmoid(gate_part)
        silu_gate = gate_part * sigmoid_gate
        hidden_low = (silu_gate * up_part).astype(bf16)
        grad_hidden = nn(cotangent_rows, feed_down_full)
        grad_gate_low = (
            grad_hidden * up_part * (sigmoid_gate + silu_gate * (1.0 - sigmoid_gate))
        ).astype(bf16)
        grad_up_low = (grad_hidden * silu_gate).astype(bf16)
        grad_both = jnp.concatenate([grad_gate_low, grad_up_low], axis=1)
        return hidden_low, grad_both, nt(grad_both, gate_up_full)

    hidden_other, grad_both_other, mid_back_other = feed_rows(mid_other, cotangent_other)
    mid_send, mid_here, cotangent_here = lax.optimization_barrier(
        (mid_back_other.astype(bf16), mid_low, cotangent)
    )
    mid_back = swap_tensor(mid_send)
    hidden_own, grad_both_own, mid_back_own = feed_rows(mid_here, cotangent_here)

    upstream = cotangent.astype(f32)
    grad_normed_mid = mid_back_own + mid_back.astype(f32)
    grad_mid_in, grad_feed_gain = rms_backward(middle, inverse_mid, gain_mid, grad_normed_mid)
    grad_middle = upstream + grad_mid_in
    grad_attended = grad_middle.astype(bf16)
    gated_send, attended_late, hidden_late = lax.optimization_barrier(
        (nn(grad_attended, output_other).astype(bf16), grad_attended, hidden_other)
    )
    gated_back = swap_tensor(gated_send)
    grad_gated = jnp.concatenate([nn(attended_late, output_half).astype(bf16), gated_back], axis=0)
    fed_send = nt(hidden_late, feed_down_full).astype(bf16)
    output_grads = tn(attended_late, jnp.concatenate([gated_own, gated_rest], axis=1)).astype(bf16)
    grad_gated, fed_send, output_grads = lax.optimization_barrier(
        (grad_gated, fed_send, output_grads)
    )
    fed_back = swap_tensor(fed_send)

    mid_all = jnp.concatenate([mid_low, mid_other], axis=0)
    cotangent_all = jnp.concatenate([cotangent, cotangent_other], axis=0)
    hidden_all = jnp.concatenate([hidden_own, hidden_other], axis=0)
    grad_both_all = jnp.concatenate([grad_both_own, grad_both_other], axis=0)
    feed_grads = jnp.concatenate(
        [
            tn(mid_all, grad_both_all).astype(bf16),
            tn(cotangent_all, hidden_all).astype(bf16),
        ],
        axis=1,
    )
    feed_sum = lax.psum_scatter(feed_grads, "dp", scatter_dimension=0, tiled=True)
    grad_projected, packed = mixer_backward(
        scal,
        projected,
        z,
        live,
        gain_head,
        sums,
        mixture,
        states,
        grad_gated,
        lane_pad(latent, 1).astype(bf16),
        lane_pad(up_local, 0).astype(bf16),
        normed_all,
        grad_feed_gain[None, :],
    )
    grad_joined = tn(normed_all, grad_projected).astype(bf16)
    grad_joined, output_grads, fed_back = lax.optimization_barrier(
        (grad_joined, output_grads, fed_back)
    )
    projected_chip, hidden_last = lax.optimization_barrier(
        (chip_sum(grad_joined[:, :projected_width]), hidden_own)
    )
    joined_sums = [
        halving_stage(by_chip(piece), 0) for piece in jnp.split(projected_chip, 2, axis=1)
    ]
    output_chip = chip_sum(output_grads)
    output_back, joined_sums[0] = lax.optimization_barrier(
        (swap_tensor(output_chip[:, value_width:]), joined_sums[0])
    )
    output_total = output_chip[:, :value_width].astype(f32) + output_back.astype(f32)
    joined_sums.append(halving_stage(by_chip(output_total.astype(bf16)), 0))

    joined_back = jnp.concatenate([joined_in, lane_pad(decay_down, 1)], axis=1)
    normed_part = nt(grad_projected, joined_back)
    grad_mixer_gain = jnp.sum(normed_part * normed_all.astype(f32), axis=0) / gain_in
    normed_part = normed_part.astype(bf16)
    fed = nt(hidden_last, feed_down_full) + fed_back.astype(f32)
    output = (middle + fed).astype(bf16)
    normed_back, joined_sums[1] = lax.optimization_barrier(
        (swap_tensor(normed_part[own:]), joined_sums[1])
    )
    grad_normed = normed_part[:own].astype(f32) + normed_back.astype(f32)
    grad_in_part = rms_backward(token_values, inverse_in, gain_in, grad_normed)[0]
    input_grad = grad_middle + grad_in_part

    flat = lax.dynamic_update_slice_in_dim(packed, grad_mixer_gain[None, :], MIXER_GAIN_ROW, 0)
    flat, joined_sums[0] = lax.optimization_barrier((flat, joined_sums[0]))
    flat = butterfly_sum(flat)
    joined_sum = jnp.concatenate([halving_rest(held) for held in joined_sums], axis=1)
    channels = 2 * key_width
    return (
        output,
        input_grad,
        flat[MIXER_GAIN_ROW],
        joined_sum[:, :key_width],
        joined_sum[:, key_width : 2 * key_width],
        joined_sum[:, 2 * key_width : 2 * key_width + value_width],
        joined_sum[:, 2 * key_width + value_width : projected_width],
        joined_sum[:, projected_width:],
        flat[DOWN_ROWS].T,
        flat[UP_ROWS, :channels],
        jnp.sum(flat[BIAS_ROWS, :channels], axis=0),
        jnp.sum(flat[BIAS_ROWS, channels : channels + VDIM], axis=0),
        flat[FEED_GAIN_ROW],
        *unpack_thirds(feed_sum),
    )


def solution(mesh):
    rows = P(("dp", "tensor"), None)
    weight = P("dp", "tensor")
    return jax.shard_map(
        on_device,
        mesh=mesh,
        in_specs=(rows, rows, P(), P(), P(), P())
        + (weight,) * 5
        + (P(), P(), P(), P(), P())
        + (weight,) * 3,
        out_specs=(rows, rows, P()) + (weight,) * 5 + (P(),) * 5 + (weight,) * 3,
        check_vma=False,
    )
```

```python
import functools

import jax
import jax.numpy as jnp
import numpy as np
from jax import lax
from jax.experimental import pallas as pl
from jax.experimental.pallas import tpu as pltpu
from jax.sharding import PartitionSpec as P

KDIM = 128
VDIM = 256
SPAN = 64
LEVELS = 6
KINDS = LEVELS + 2
STEP_SPANS = 4
LANES = 128
LOWRANK = 16
DOWN_ROWS = slice(0, LOWRANK)
UP_ROWS = slice(LOWRANK, 2 * LOWRANK)
BIAS_ROWS = slice(2 * LOWRANK, 2 * LOWRANK + 8)
FEED_GAIN_ROW = 2 * LOWRANK + 8
MIXER_GAIN_ROW = FEED_GAIN_ROW + 1
PACKED_ROWS = FEED_GAIN_ROW + 8
UNPACK_FLOPS = 3 * 10**10

epsilon = 1e-06
head_epsilon = 1.0
gate_scale = 16.0
highest = lax.Precision.HIGHEST
f32 = jnp.float32
bf16 = jnp.bfloat16


def rms_forward(values, norm_gain, floor_value=epsilon):
    inverse = lax.rsqrt(jnp.mean(values * values, axis=-1, keepdims=True) + floor_value)
    return (values * inverse * norm_gain, inverse)


def rms_backward(values, inverse, norm_gain, upstream):
    scaled = upstream * norm_gain
    inner = jnp.mean(scaled * values, axis=-1, keepdims=True)
    grad_values = inverse * scaled - values * (inverse * inverse * inverse) * inner
    grad_gain = jnp.sum(upstream * values * inverse, axis=0)
    return (grad_values, grad_gain)


def group_layout(sequence_lengths, sequence_group, sequence_offset, which_group, places, span_count):
    live_record = (sequence_group == which_group) & (sequence_lengths > 0)
    start_row = sequence_offset * SPAN
    covered = (
        live_record[None, :]
        & (places >= start_row[None, :])
        & (places < (start_row + sequence_lengths)[None, :])
    )
    live_mask = jnp.any(covered, axis=1).astype(f32)
    span_ids = jnp.arange(span_count, dtype=jnp.int32)[:, None]
    restart = jnp.any(live_record[None, :] & (span_ids == sequence_offset[None, :]), axis=1)
    return (live_mask, restart.astype(jnp.int32))


def nn(left, right):
    return lax.dot_general(left, right, (((1,), (0,)), ((), ())), preferred_element_type=f32)


def nt(left, right):
    return lax.dot_general(left, right, (((1,), (1,)), ((), ())), preferred_element_type=f32)


def tn(left, right):
    return lax.dot_general(left, right, (((0,), (0,)), ((), ())), preferred_element_type=f32)


def decay_sums():
    rows = np.arange(SPAN)[:, None]
    cols = np.arange(SPAN)[None, :]
    blocks = [cols <= rows]
    for level in range(LEVELS):
        half = 1 << level
        edge = (rows // (2 * half)) * (2 * half) + half
        right = rows >= edge
        blocks.append(np.where(right, (cols >= edge) & (cols <= rows), (cols > rows) & (cols < edge)))
    blocks.append(cols > rows)
    return np.concatenate(blocks, axis=0).astype(np.float32)


def pair_levels():
    rows = lax.broadcasted_iota(jnp.int32, (SPAN, SPAN), 0)
    cols = lax.broadcasted_iota(jnp.int32, (SPAN, SPAN), 1)
    apart = rows ^ cols
    later = rows > cols
    masks = [later & (lax.shift_right_logical(apart, level) == 1) for level in range(LEVELS)]
    return masks, rows == cols


def span_factors(z_part, sums):
    decays = (jnp.minimum(z_part, 0.0) - jnp.log1p(jnp.exp(-jnp.abs(z_part)))) * (1.0 / gate_scale)
    high = decays.astype(bf16)
    low = (decays - high.astype(f32)).astype(bf16)
    return jnp.exp(nn(sums, jnp.concatenate([high, low], axis=0)))


def span_scores(queries, keys, factors, masks, diagonal):
    scores = jnp.where(diagonal, nt(queries.astype(bf16), keys.astype(bf16)), 0.0)
    query_levels = []
    key_levels = []
    for level in range(LEVELS):
        factor = factors[(level + 1) * SPAN : (level + 2) * SPAN]
        query_level = (queries * factor).astype(bf16)
        key_level = (keys * factor).astype(bf16)
        scores = jnp.where(masks[level], nt(query_level, key_level), scores)
        query_levels.append(query_level)
        key_levels.append(key_level)
    return scores, query_levels, key_levels


def forward_kernel(heads, scal, projected, z, live, gain, sums, gated, mixture, states, state):
    step = pl.program_id(0)
    key_width = heads * KDIM
    value_width = heads * VDIM

    @pl.when(step == 0)
    def _():
        state[...] = jnp.zeros_like(state)

    masks, diagonal = pair_levels()
    head_gain = gain[...]
    for part in range(STEP_SPANS):
        rows = slice(part * SPAN, (part + 1) * SPAN)
        factors_all = span_factors(z[rows, :], sums[...])
        keep = jnp.where(scal[1 + step * STEP_SPANS + part] == 0, 1.0, 0.0)
        for head in range(heads):
            keys_at = slice(head * KDIM, (head + 1) * KDIM)
            queries = projected[rows, keys_at].astype(f32)
            keys = projected[rows, key_width + head * KDIM : key_width + (head + 1) * KDIM].astype(f32)
            value_at = 2 * key_width + head * VDIM
            values = projected[rows, value_at : value_at + VDIM]
            gating = projected[rows, value_at + value_width : value_at + value_width + VDIM].astype(f32)
            factors = factors_all[:, keys_at]
            scores, _, _ = span_scores(queries, keys, factors, masks, diagonal)
            entering = state[head] * keep
            entering_low = entering.astype(bf16)
            states[part, head] = entering_low
            whole = factors[:SPAN]
            after = factors[(KINDS - 1) * SPAN :]
            mixed = nn(scores.astype(bf16), values) + nt(
                (queries * whole).astype(bf16), entering_low
            )
            state[head] = entering * whole[SPAN - 1 :] + tn(values, (keys * after).astype(bf16))
            value_cols = slice(head * VDIM, (head + 1) * VDIM)
            mixture[rows, value_cols] = mixed.astype(bf16)
            inverse = lax.rsqrt(jnp.mean(mixed * mixed, axis=-1, keepdims=True) + head_epsilon)
            silu = gating * jax.nn.sigmoid(gating)
            gated[rows, value_cols] = (mixed * inverse * head_gain * silu * live[rows, :]).astype(bf16)


def backward_kernel(
    heads,
    scal,
    projected,
    z,
    live,
    gain,
    sums,
    mixture,
    states,
    grad_gated,
    latent,
    up,
    normed,
    feed_gain_grad,
    grad_projected,
    packed,
    grad_up,
    grad_bias,
    grad_state,
):
    step = pl.program_id(0)
    natural = pl.num_programs(0) - 1 - step
    key_width = heads * KDIM
    value_width = heads * VDIM

    @pl.when(step == 0)
    def _():
        grad_state[...] = jnp.zeros_like(grad_state)
        packed[...] = jnp.zeros_like(packed)
        packed[FEED_GAIN_ROW : FEED_GAIN_ROW + 1, :] = feed_gain_grad[...]
        grad_up[...] = jnp.zeros_like(grad_up)
        grad_bias[...] = jnp.zeros_like(grad_bias)

    gain_at = slice(2 * key_width, 2 * key_width + VDIM)
    masks, diagonal = pair_levels()
    head_gain = gain[...]
    last_row = lax.broadcasted_iota(jnp.int32, (SPAN, KDIM), 0) == SPAN - 1
    for part in reversed(range(STEP_SPANS)):
        rows = slice(part * SPAN, (part + 1) * SPAN)
        z_part = z[rows, :]
        factors_all = span_factors(z_part, sums[...])
        keep = jnp.where(scal[1 + natural * STEP_SPANS + part] == 0, 1.0, 0.0)
        live_part = live[rows, :]
        exponents = []
        for head in range(heads):
            keys_at = slice(head * KDIM, (head + 1) * KDIM)
            key_cols = slice(key_width + head * KDIM, key_width + (head + 1) * KDIM)
            value_at = 2 * key_width + head * VDIM
            value_cols = slice(value_at, value_at + VDIM)
            gate_cols = slice(value_at + value_width, value_at + value_width + VDIM)
            mixed_cols = slice(head * VDIM, (head + 1) * VDIM)
            queries = projected[rows, keys_at].astype(f32)
            keys = projected[rows, key_cols].astype(f32)
            values = projected[rows, value_cols]
            gating = projected[rows, gate_cols].astype(f32)
            factors = factors_all[:, keys_at]
            scores, query_levels, key_levels = span_scores(queries, keys, factors, masks, diagonal)
            scores_low = scores.astype(bf16)
            whole = factors[:SPAN]
            after = factors[(KINDS - 1) * SPAN :]

            mixed = mixture[rows, mixed_cols].astype(f32)
            inverse = lax.rsqrt(jnp.mean(mixed * mixed, axis=-1, keepdims=True) + head_epsilon)
            unit = mixed * inverse
            sigmoid = jax.nn.sigmoid(gating)
            silu = gating * sigmoid
            upstream = grad_gated[rows, mixed_cols].astype(f32) * live_part
            grad_projected[rows, gate_cols] = (
                upstream * unit * head_gain * (sigmoid + silu * (1.0 - sigmoid))
            ).astype(bf16)
            normed_back = upstream * silu
            gain_part = normed_back * unit
            packed[BIAS_ROWS, gain_at] += jnp.sum(gain_part.reshape(SPAN // 8, 8, VDIM), axis=0)
            scaled = normed_back * head_gain
            inner = jnp.mean(scaled * unit, axis=-1, keepdims=True)
            grad_mixed = (inverse * (scaled - unit * inner)).astype(bf16)

            entering = states[part, head]
            leaving = grad_state[head]
            leaving_low = leaving.astype(bf16)
            grad_scores = nt(grad_mixed, values)
            after_keys = (keys * after).astype(bf16)
            whole_queries = (queries * whole).astype(bf16)
            grad_projected[rows, value_cols] = (
                tn(scores_low, grad_mixed) + nt(after_keys, leaving_low)
            ).astype(bf16)
            grad_queries = whole * nn(grad_mixed, entering)
            grad_keys = after * nn(values, leaving_low)
            fading = whole[SPAN - 1 :]
            last_sum = fading * jnp.sum(entering.astype(f32) * leaving, axis=0, keepdims=True)
            exponents_head = [queries * grad_queries + jnp.where(last_row, last_sum, 0.0)]
            last_exponent = keys * grad_keys
            for level in range(LEVELS):
                factor = factors[(level + 1) * SPAN : (level + 2) * SPAN]
                level_back = jnp.where(masks[level], grad_scores, 0.0).astype(bf16)
                query_part = factor * nn(level_back, key_levels[level])
                key_part = factor * tn(level_back, query_levels[level])
                grad_queries += query_part
                grad_keys += key_part
                exponents_head.append(queries * query_part + keys * key_part)
            exponents_head.append(last_exponent)
            same = jnp.sum(jnp.where(diagonal, grad_scores, 0.0), axis=1, keepdims=True)
            grad_projected[rows, keys_at] = (grad_queries + same * keys).astype(bf16)
            grad_projected[rows, key_cols] = (grad_keys + same * queries).astype(bf16)
            exponents.append(jnp.concatenate(exponents_head, axis=0).astype(bf16))
            grad_state[head] = keep * (leaving * fading + tn(grad_mixed, whole_queries))
        grad_decays = tn(sums[:, :SPAN], jnp.concatenate(exponents, axis=1))
        grad_z = grad_decays * jax.nn.sigmoid(-z_part) * (1.0 / gate_scale)
        grad_bias[...] += jnp.sum(grad_z.reshape(SPAN // 8, 8, key_width), axis=0)
        grad_z_low = grad_z.astype(bf16)
        grad_up[...] += tn(latent[rows, :LOWRANK], grad_z_low)
        latent_cols = slice(2 * key_width + 2 * value_width, grad_projected.shape[1])
        grad_projected[rows, latent_cols] = nt(grad_z_low, up[...]).astype(bf16)

    latent_at = 2 * key_width + 2 * value_width
    packed[DOWN_ROWS, :] += tn(grad_projected[:, latent_at : latent_at + LOWRANK], normed[...])

    for half in range(2):

        @pl.when((step == pl.num_programs(0) - 1) & (scal[0] == half))
        def _(at=slice(half * key_width, (half + 1) * key_width)):
            packed[UP_ROWS, at] = grad_up[...]
            packed[BIAS_ROWS, at] = grad_bias[...]


def mixer_specs(length, projected_width, key_width, value_width, width, reverse):
    steps = length // (SPAN * STEP_SPANS)
    step_rows = SPAN * STEP_SPANS
    heads = key_width // KDIM

    def natural(step):
        return steps - 1 - step if reverse else step

    def by_rows(step, scal):
        return (lax.rem(natural(step) + scal[0] * (steps // 2), steps), 0)

    def whole(step, scal):
        return (0, 0)

    return dict(
        steps=steps,
        projected=pl.BlockSpec((step_rows, projected_width), by_rows),
        z=pl.BlockSpec((step_rows, key_width), by_rows),
        live=pl.BlockSpec((step_rows, 1), by_rows),
        gain=pl.BlockSpec((1, VDIM), whole),
        sums=pl.BlockSpec((KINDS * SPAN, 2 * SPAN), whole),
        values=pl.BlockSpec((step_rows, value_width), by_rows),
        states=pl.BlockSpec(
            (STEP_SPANS, heads, VDIM, KDIM), lambda step, scal: (natural(step), 0, 0, 0)
        ),
        normed=pl.BlockSpec((step_rows, width), by_rows),
        feed_gain=pl.BlockSpec((1, width), whole),
        packed=pl.BlockSpec((PACKED_ROWS, width), whole),
        latent=pl.BlockSpec((step_rows, LANES), by_rows),
        up=pl.BlockSpec((LANES, key_width), whole),
        extended=pl.BlockSpec((step_rows, projected_width + LANES), by_rows),
    )


def mixer_forward(scal, projected, z, live, gain, sums):
    length, projected_width = projected.shape
    key_width = z.shape[1]
    heads = key_width // KDIM
    value_width = heads * VDIM
    spans = length // SPAN
    specs = mixer_specs(length, projected_width, key_width, value_width, LANES, False)
    return pl.pallas_call(
        functools.partial(forward_kernel, heads),
        grid_spec=pltpu.PrefetchScalarGridSpec(
            num_scalar_prefetch=1,
            grid=(specs["steps"],),
            in_specs=[specs[name] for name in ("projected", "z", "live", "gain", "sums")],
            out_specs=[specs[name] for name in ("values", "values", "states")],
            scratch_shapes=[pltpu.VMEM((heads, VDIM, KDIM), f32)],
        ),
        out_shape=[
            jax.ShapeDtypeStruct((length, value_width), bf16),
            jax.ShapeDtypeStruct((length, value_width), bf16),
            jax.ShapeDtypeStruct((spans, heads, VDIM, KDIM), bf16),
        ],
        compiler_params=pltpu.CompilerParams(vmem_limit_bytes=40 * 1024 * 1024),
        cost_estimate=pl.CostEstimate(
            flops=10**10, bytes_accessed=15 * 10**6, transcendentals=4 * 10**6
        ),
        name="mixer_forward",
    )(scal, projected, z, live, gain, sums)


def mixer_backward(
    scal,
    projected,
    z,
    live,
    gain,
    sums,
    mixture,
    states,
    grad_gated,
    latent,
    up,
    normed,
    feed_gain_grad,
):
    length, projected_width = projected.shape
    key_width = z.shape[1]
    heads = key_width // KDIM
    value_width = heads * VDIM
    width = normed.shape[1]
    specs = mixer_specs(length, projected_width, key_width, value_width, width, True)
    names = ("projected", "z", "live", "gain", "sums", "values", "states", "values")
    names += ("latent", "up", "normed", "feed_gain")
    return pl.pallas_call(
        functools.partial(backward_kernel, heads),
        grid_spec=pltpu.PrefetchScalarGridSpec(
            num_scalar_prefetch=1,
            grid=(specs["steps"],),
            in_specs=[specs[name] for name in names],
            out_specs=[specs[name] for name in ("extended", "packed")],
            scratch_shapes=[
                pltpu.VMEM((LOWRANK, key_width), f32),
                pltpu.VMEM((8, key_width), f32),
                pltpu.VMEM((heads, VDIM, KDIM), f32),
            ],
        ),
        out_shape=[
            jax.ShapeDtypeStruct((length, projected_width + LANES), bf16),
            jax.ShapeDtypeStruct((PACKED_ROWS, width), f32),
        ],
        compiler_params=pltpu.CompilerParams(vmem_limit_bytes=40 * 1024 * 1024),
        cost_estimate=pl.CostEstimate(
            flops=25 * 10**9, bytes_accessed=20 * 10**6, transcendentals=4 * 10**6
        ),
        name="mixer_backward",
    )(
        scal,
        projected,
        z,
        live,
        gain,
        sums,
        mixture,
        states,
        grad_gated,
        latent,
        up,
        normed,
        feed_gain_grad,
    )


def unpack_kernel(packed, *parts):
    width = parts[0].shape[1]
    for index, part in enumerate(parts):
        part[...] = packed[:, index * width : (index + 1) * width].astype(f32)


def unpack_thirds(packed):
    rows, width = packed.shape[0], packed.shape[1] // 3
    return pl.pallas_call(
        unpack_kernel,
        out_shape=[jax.ShapeDtypeStruct((rows, width), f32)] * 3,
        compiler_params=pltpu.CompilerParams(vmem_limit_bytes=8 * 1024 * 1024),
        cost_estimate=pl.CostEstimate(
            flops=UNPACK_FLOPS, bytes_accessed=3 * 10**6, transcendentals=0
        ),
        name="unpack_thirds",
    )(packed)


def lane_pad(values, axis):
    widths = [(0, 0), (0, 0)]
    widths[axis] = (0, LANES - values.shape[axis])
    return jnp.pad(values, widths)


def swap_tensor(values):
    return lax.ppermute(values, "tensor", [(0, 1), (1, 0)])


def chip_sum(values):
    count = lax.axis_size("dp")
    parity = lax.axis_index("dp") % 2
    blocks = values.reshape(count // 2, 2, values.shape[0] // count, values.shape[1])
    kept = lax.dynamic_index_in_dim(blocks, parity, 1, keepdims=False)
    sent = lax.dynamic_index_in_dim(blocks, 1 - parity, 1, keepdims=False)
    arrived = lax.ppermute(sent, "dp", [(i, i ^ 1) for i in range(count)])
    total = (kept.astype(f32) + arrived.astype(f32)).astype(bf16)
    return total.reshape(values.shape[0] // 2, values.shape[1])


def halving_stages():
    return (lax.axis_size("dp") // 2).bit_length() - 1


def by_chip(values):
    stages = halving_stages()
    return values.reshape((2,) * stages + (values.shape[0] >> stages, values.shape[1]))


def halving_stage(held, stage):
    count = lax.axis_size("dp")
    stages = halving_stages()
    bit = 2 << stage
    side = (lax.axis_index("dp") // bit) % 2
    axis = stages - 1 - stage
    kept = lax.dynamic_index_in_dim(held, side, axis, keepdims=False)
    sent = lax.dynamic_index_in_dim(held, 1 - side, axis, keepdims=False)
    arrived = lax.ppermute(sent, "dp", [(i, i ^ bit) for i in range(count)])
    total = kept.astype(f32) + arrived.astype(f32)
    return total if stage == stages - 1 else total.astype(bf16)


def halving_rest(held, first):
    for stage in range(first, halving_stages()):
        held = halving_stage(held, stage)
    return held


def both_ways(side, mine, other, axis):
    first = jnp.where(side == 0, mine, other)
    second = jnp.where(side == 0, other, mine)
    return jnp.stack([first, second], axis=axis)


def swap_half(values):
    half = values.shape[0] // 2
    parity = lax.axis_index("dp") % 2
    return swap_tensor(lax.dynamic_slice_in_dim(values, parity * half, half, 0))


def join_halves(mine):
    count = lax.axis_size("dp")
    parity = lax.axis_index("dp") % 2
    other = lax.ppermute(mine, "dp", [(i, i ^ 1) for i in range(count)])
    return both_ways(parity, mine, other, 0).reshape(mine.shape[0] * 2, mine.shape[1])


def butterfly_sum(values):
    count = lax.axis_size("dp")
    reaches = [1 << bit for bit in range(count.bit_length() - 1)]
    total = values
    for reach in reaches[:1] + reaches[2:] + reaches[1:2]:
        low = total.astype(bf16)
        arrived = lax.ppermute(low, "dp", [(i, i ^ reach) for i in range(count)])
        total = low.astype(f32) + arrived.astype(f32)
    low = total.astype(bf16)
    return low.astype(f32) + swap_tensor(low).astype(f32)


def on_device(
    tokens,
    cotangent,
    sequence_lengths,
    sequence_group,
    sequence_offset,
    mixer_gain,
    query_weight,
    key_weight,
    value_weight,
    output_gate,
    output_weight,
    decay_down,
    decay_up,
    decay_bias,
    head_gain,
    feed_gain,
    feed_gate,
    feed_up,
    feed_down,
):
    which_group = lax.axis_index("dp")
    half_index = lax.axis_index("tensor")
    own = tokens.shape[0]
    group_rows = own * 2
    key_width = query_weight.shape[1]
    value_width = value_weight.shape[1]
    feed_width = feed_gate.shape[1]
    places = (jnp.arange(group_rows, dtype=jnp.int32) + half_index * own) % group_rows
    live_mask, restart = group_layout(
        sequence_lengths,
        sequence_group,
        sequence_offset,
        which_group,
        places[:, None],
        group_rows // SPAN,
    )
    live = live_mask[:, None]
    scal = jnp.concatenate([half_index.astype(jnp.int32)[None], restart])
    sums = jnp.asarray(np.tile(decay_sums(), (1, 2)), bf16)
    gain_head = head_gain.astype(f32)[None, :]

    joined = lax.all_gather(
        jnp.concatenate(
            [query_weight, key_weight, value_weight, output_gate, output_weight], axis=1
        ),
        "dp",
        axis=0,
        tiled=True,
    )
    feed_all = lax.all_gather(
        jnp.concatenate([feed_gate, feed_up, feed_down], axis=1), "dp", axis=0, tiled=True
    )
    gate_up_full = feed_all[:, : 2 * feed_width]
    feed_down_full = feed_all[:, 2 * feed_width :]
    gain_in = mixer_gain.astype(f32)
    token_values = tokens.astype(f32)
    normed_in, inverse_in = rms_forward(token_values, gain_in)
    normed_low = normed_in.astype(bf16)
    normed_other = swap_tensor(normed_low)
    cotangent_other = swap_tensor(cotangent)
    joined, cotangent_other = lax.optimization_barrier((joined, cotangent_other))
    projected_width = 2 * key_width + 2 * value_width
    joined_in = joined[:, :projected_width]
    output_half = joined[:, projected_width:]
    output_piece = swap_half(output_half)

    normed_all = jnp.concatenate([normed_low, normed_other], axis=0)
    projected = nn(normed_all, joined_in).astype(bf16)
    latent = nn(normed_all, decay_down)
    up_local = lax.dynamic_slice_in_dim(decay_up, half_index * key_width, key_width, 1).astype(f32)
    bias_local = lax.dynamic_slice_in_dim(decay_bias, half_index * key_width, key_width, 0)
    z = jnp.dot(latent, up_local, precision=highest) + bias_local.astype(f32)
    gated, mixture, states = mixer_forward(scal, projected, z, live, gain_head, sums)

    gated, output_piece = lax.optimization_barrier((gated, output_piece))
    output_other = join_halves(output_piece)
    gated_own = gated[:own]
    gated_rest = swap_tensor(gated[own:])
    attended = nt(gated_own, output_half) + nt(gated_rest, output_other)
    middle = token_values + attended
    gain_mid = feed_gain.astype(f32)
    normed_mid, inverse_mid = rms_forward(middle, gain_mid)
    mid_low = normed_mid.astype(bf16)
    mid_other = swap_tensor(mid_low)

    def feed_rows(mid_rows, cotangent_rows):
        both = nn(mid_rows, gate_up_full)
        gate_part = both[:, :feed_width]
        up_part = both[:, feed_width:]
        sigmoid_gate = jax.nn.sigmoid(gate_part)
        silu_gate = gate_part * sigmoid_gate
        hidden_low = (silu_gate * up_part).astype(bf16)
        grad_hidden = nn(cotangent_rows, feed_down_full)
        grad_gate_low = (
            grad_hidden * up_part * (sigmoid_gate + silu_gate * (1.0 - sigmoid_gate))
        ).astype(bf16)
        grad_up_low = (grad_hidden * silu_gate).astype(bf16)
        grad_both = jnp.concatenate([grad_gate_low, grad_up_low], axis=1)
        return hidden_low, grad_both, nt(grad_both, gate_up_full)

    hidden_other, grad_both_other, mid_back_other = feed_rows(mid_other, cotangent_other)
    mid_send, mid_here, cotangent_here = lax.optimization_barrier(
        (mid_back_other.astype(bf16), mid_low, cotangent)
    )
    mid_back = swap_tensor(mid_send)
    hidden_own, grad_both_own, mid_back_own = feed_rows(mid_here, cotangent_here)

    upstream = cotangent.astype(f32)
    grad_normed_mid = mid_back_own + mid_back.astype(f32)
    grad_mid_in, grad_feed_gain = rms_backward(middle, inverse_mid, gain_mid, grad_normed_mid)
    grad_middle = upstream + grad_mid_in
    grad_attended = grad_middle.astype(bf16)
    gated_send, attended_late, hidden_late = lax.optimization_barrier(
        (nn(grad_attended, output_other).astype(bf16), grad_attended, hidden_other)
    )
    gated_back = swap_tensor(gated_send)
    grad_gated = jnp.concatenate([nn(attended_late, output_half).astype(bf16), gated_back], axis=0)
    fed_send = nt(hidden_late, feed_down_full).astype(bf16)
    output_grads = tn(attended_late, jnp.concatenate([gated_own, gated_rest], axis=1)).astype(bf16)
    grad_gated, fed_send, output_grads = lax.optimization_barrier(
        (grad_gated, fed_send, output_grads)
    )
    fed_back = swap_tensor(fed_send)

    mid_all = jnp.concatenate([mid_low, mid_other], axis=0)
    cotangent_all = jnp.concatenate([cotangent, cotangent_other], axis=0)
    hidden_all = jnp.concatenate([hidden_own, hidden_other], axis=0)
    grad_both_all = jnp.concatenate([grad_both_own, grad_both_other], axis=0)
    feed_grads = jnp.concatenate(
        [
            tn(mid_all, grad_both_all).astype(bf16),
            tn(cotangent_all, hidden_all).astype(bf16),
        ],
        axis=1,
    )
    feed_sum = lax.psum_scatter(feed_grads, "dp", scatter_dimension=0, tiled=True)
    grad_projected, packed = mixer_backward(
        scal,
        projected,
        z,
        live,
        gain_head,
        sums,
        mixture,
        states,
        grad_gated,
        lane_pad(latent, 1).astype(bf16),
        lane_pad(up_local, 0).astype(bf16),
        normed_all,
        grad_feed_gain[None, :],
    )
    grad_joined = tn(normed_all, grad_projected).astype(bf16)
    grad_joined, output_grads, fed_back = lax.optimization_barrier(
        (grad_joined, output_grads, fed_back)
    )
    projected_chip, hidden_last = lax.optimization_barrier(
        (chip_sum(grad_joined[:, :projected_width]), hidden_own)
    )
    joined_sums = [
        halving_stage(by_chip(piece), 0) for piece in jnp.split(projected_chip, 2, axis=1)
    ]
    output_chip = chip_sum(output_grads)
    output_back = swap_tensor(output_chip[:, value_width:])
    joined_back = jnp.concatenate([joined_in, lane_pad(decay_down, 1)], axis=1)
    normed_part = nt(grad_projected, joined_back)
    grad_mixer_gain = jnp.sum(normed_part * normed_all.astype(f32), axis=0) / gain_in
    normed_part, _ = lax.optimization_barrier((normed_part.astype(bf16), output_back))
    fed = nt(hidden_last, feed_down_full) + fed_back.astype(f32)
    output = (middle + fed).astype(bf16)
    output_total = output_chip[:, :value_width].astype(f32) + output_back.astype(f32)
    joined_sums.append(halving_stage(by_chip(output_total.astype(bf16)), 0))
    packed, _ = lax.optimization_barrier((packed, joined_sums[0]))
    joined_sums = [halving_stage(held, 1) for held in joined_sums]
    normed_back, _ = lax.optimization_barrier((swap_tensor(normed_part[own:]), joined_sums[1]))
    grad_normed = normed_part[:own].astype(f32) + normed_back.astype(f32)
    grad_in_part = rms_backward(token_values, inverse_in, gain_in, grad_normed)[0]
    input_grad = grad_middle + grad_in_part

    flat = lax.dynamic_update_slice_in_dim(packed, grad_mixer_gain[None, :], MIXER_GAIN_ROW, 0)
    flat = butterfly_sum(flat)
    joined_sum = jnp.concatenate([halving_rest(held, 2) for held in joined_sums], axis=1)
    channels = 2 * key_width
    return (
        output,
        input_grad,
        flat[MIXER_GAIN_ROW],
        joined_sum[:, :key_width],
        joined_sum[:, key_width : 2 * key_width],
        joined_sum[:, 2 * key_width : 2 * key_width + value_width],
        joined_sum[:, 2 * key_width + value_width : projected_width],
        joined_sum[:, projected_width:],
        flat[DOWN_ROWS].T,
        flat[UP_ROWS, :channels],
        jnp.sum(flat[BIAS_ROWS, :channels], axis=0),
        jnp.sum(flat[BIAS_ROWS, channels : channels + VDIM], axis=0),
        flat[FEED_GAIN_ROW],
        *unpack_thirds(feed_sum),
    )


def solution(mesh):
    rows = P(("dp", "tensor"), None)
    weight = P("dp", "tensor")
    return jax.shard_map(
        on_device,
        mesh=mesh,
        in_specs=(rows, rows, P(), P(), P(), P())
        + (weight,) * 5
        + (P(), P(), P(), P(), P())
        + (weight,) * 3,
        out_specs=(rows, rows, P()) + (weight,) * 5 + (P(),) * 5 + (weight,) * 3,
        check_vma=False,
    )
```

```python
import functools

import jax
import jax.numpy as jnp
import numpy as np
from jax import lax
from jax.experimental import pallas as pl
from jax.experimental.pallas import tpu as pltpu
from jax.sharding import PartitionSpec as P

KDIM = 128
VDIM = 256
SPAN = 64
LEVELS = 6
KINDS = LEVELS + 2
STEP_SPANS = 4
LANES = 128
LOWRANK = 16
DOWN_ROWS = slice(0, LOWRANK)
UP_ROWS = slice(LOWRANK, 2 * LOWRANK)
BIAS_ROWS = slice(2 * LOWRANK, 2 * LOWRANK + 8)
FEED_GAIN_ROW = 2 * LOWRANK + 8
MIXER_GAIN_ROW = FEED_GAIN_ROW + 1
PACKED_ROWS = FEED_GAIN_ROW + 8
UNPACK_FLOPS = 3 * 10**10

epsilon = 1e-06
head_epsilon = 1.0
gate_scale = 16.0
highest = lax.Precision.HIGHEST
f32 = jnp.float32
bf16 = jnp.bfloat16


def rms_forward(values, norm_gain, floor_value=epsilon):
    inverse = lax.rsqrt(jnp.mean(values * values, axis=-1, keepdims=True) + floor_value)
    return (values * inverse * norm_gain, inverse)


def rms_backward(values, inverse, norm_gain, upstream):
    scaled = upstream * norm_gain
    inner = jnp.mean(scaled * values, axis=-1, keepdims=True)
    grad_values = inverse * scaled - values * (inverse * inverse * inverse) * inner
    grad_gain = jnp.sum(upstream * values * inverse, axis=0)
    return (grad_values, grad_gain)


def group_layout(sequence_lengths, sequence_group, sequence_offset, which_group, places, span_count):
    live_record = (sequence_group == which_group) & (sequence_lengths > 0)
    start_row = sequence_offset * SPAN
    covered = (
        live_record[None, :]
        & (places >= start_row[None, :])
        & (places < (start_row + sequence_lengths)[None, :])
    )
    live_mask = jnp.any(covered, axis=1).astype(f32)
    span_ids = jnp.arange(span_count, dtype=jnp.int32)[:, None]
    restart = jnp.any(live_record[None, :] & (span_ids == sequence_offset[None, :]), axis=1)
    return (live_mask, restart.astype(jnp.int32))


def nn(left, right):
    return lax.dot_general(left, right, (((1,), (0,)), ((), ())), preferred_element_type=f32)


def nt(left, right):
    return lax.dot_general(left, right, (((1,), (1,)), ((), ())), preferred_element_type=f32)


def tn(left, right):
    return lax.dot_general(left, right, (((0,), (0,)), ((), ())), preferred_element_type=f32)


def decay_sums():
    rows = np.arange(SPAN)[:, None]
    cols = np.arange(SPAN)[None, :]
    blocks = [cols <= rows]
    for level in range(LEVELS):
        half = 1 << level
        edge = (rows // (2 * half)) * (2 * half) + half
        right = rows >= edge
        blocks.append(np.where(right, (cols >= edge) & (cols <= rows), (cols > rows) & (cols < edge)))
    blocks.append(cols > rows)
    return np.concatenate(blocks, axis=0).astype(np.float32)


def pair_levels():
    rows = lax.broadcasted_iota(jnp.int32, (SPAN, SPAN), 0)
    cols = lax.broadcasted_iota(jnp.int32, (SPAN, SPAN), 1)
    apart = rows ^ cols
    later = rows > cols
    masks = [later & (lax.shift_right_logical(apart, level) == 1) for level in range(LEVELS)]
    return masks, rows == cols


def span_factors(z_part, sums):
    decays = (jnp.minimum(z_part, 0.0) - jnp.log1p(jnp.exp(-jnp.abs(z_part)))) * (1.0 / gate_scale)
    high = decays.astype(bf16)
    low = (decays - high.astype(f32)).astype(bf16)
    return jnp.exp(nn(sums, jnp.concatenate([high, low], axis=0)))


def span_scores(queries, keys, factors, masks, diagonal):
    scores = jnp.where(diagonal, nt(queries.astype(bf16), keys.astype(bf16)), 0.0)
    query_levels = []
    key_levels = []
    for level in range(LEVELS):
        factor = factors[(level + 1) * SPAN : (level + 2) * SPAN]
        query_level = (queries * factor).astype(bf16)
        key_level = (keys * factor).astype(bf16)
        scores = jnp.where(masks[level], nt(query_level, key_level), scores)
        query_levels.append(query_level)
        key_levels.append(key_level)
    return scores, query_levels, key_levels


def forward_kernel(heads, scal, projected, z, live, gain, sums, gated, mixture, states, state):
    step = pl.program_id(0)
    key_width = heads * KDIM
    value_width = heads * VDIM

    @pl.when(step == 0)
    def _():
        state[...] = jnp.zeros_like(state)

    masks, diagonal = pair_levels()
    head_gain = gain[...]
    for part in range(STEP_SPANS):
        rows = slice(part * SPAN, (part + 1) * SPAN)
        factors_all = span_factors(z[rows, :], sums[...])
        keep = jnp.where(scal[1 + step * STEP_SPANS + part] == 0, 1.0, 0.0)
        for head in range(heads):
            keys_at = slice(head * KDIM, (head + 1) * KDIM)
            queries = projected[rows, keys_at].astype(f32)
            keys = projected[rows, key_width + head * KDIM : key_width + (head + 1) * KDIM].astype(f32)
            value_at = 2 * key_width + head * VDIM
            values = projected[rows, value_at : value_at + VDIM]
            gating = projected[rows, value_at + value_width : value_at + value_width + VDIM].astype(f32)
            factors = factors_all[:, keys_at]
            scores, _, _ = span_scores(queries, keys, factors, masks, diagonal)
            entering = state[head] * keep
            entering_low = entering.astype(bf16)
            states[part, head] = entering_low
            whole = factors[:SPAN]
            after = factors[(KINDS - 1) * SPAN :]
            mixed = nn(scores.astype(bf16), values) + nt(
                (queries * whole).astype(bf16), entering_low
            )
            state[head] = entering * whole[SPAN - 1 :] + tn(values, (keys * after).astype(bf16))
            value_cols = slice(head * VDIM, (head + 1) * VDIM)
            mixture[rows, value_cols] = mixed.astype(bf16)
            inverse = lax.rsqrt(jnp.mean(mixed * mixed, axis=-1, keepdims=True) + head_epsilon)
            silu = gating * jax.nn.sigmoid(gating)
            gated[rows, value_cols] = (mixed * inverse * head_gain * silu * live[rows, :]).astype(bf16)


def backward_kernel(
    heads,
    scal,
    projected,
    z,
    live,
    gain,
    sums,
    mixture,
    states,
    grad_gated,
    latent,
    up,
    normed,
    feed_gain_grad,
    grad_projected,
    packed,
    grad_up,
    grad_bias,
    grad_state,
):
    step = pl.program_id(0)
    natural = pl.num_programs(0) - 1 - step
    key_width = heads * KDIM
    value_width = heads * VDIM

    @pl.when(step == 0)
    def _():
        grad_state[...] = jnp.zeros_like(grad_state)
        packed[...] = jnp.zeros_like(packed)
        packed[FEED_GAIN_ROW : FEED_GAIN_ROW + 1, :] = feed_gain_grad[...]
        grad_up[...] = jnp.zeros_like(grad_up)
        grad_bias[...] = jnp.zeros_like(grad_bias)

    gain_at = slice(2 * key_width, 2 * key_width + VDIM)
    masks, diagonal = pair_levels()
    head_gain = gain[...]
    last_row = lax.broadcasted_iota(jnp.int32, (SPAN, KDIM), 0) == SPAN - 1
    for part in reversed(range(STEP_SPANS)):
        rows = slice(part * SPAN, (part + 1) * SPAN)
        z_part = z[rows, :]
        factors_all = span_factors(z_part, sums[...])
        keep = jnp.where(scal[1 + natural * STEP_SPANS + part] == 0, 1.0, 0.0)
        live_part = live[rows, :]
        exponents = []
        for head in range(heads):
            keys_at = slice(head * KDIM, (head + 1) * KDIM)
            key_cols = slice(key_width + head * KDIM, key_width + (head + 1) * KDIM)
            value_at = 2 * key_width + head * VDIM
            value_cols = slice(value_at, value_at + VDIM)
            gate_cols = slice(value_at + value_width, value_at + value_width + VDIM)
            mixed_cols = slice(head * VDIM, (head + 1) * VDIM)
            queries = projected[rows, keys_at].astype(f32)
            keys = projected[rows, key_cols].astype(f32)
            values = projected[rows, value_cols]
            gating = projected[rows, gate_cols].astype(f32)
            factors = factors_all[:, keys_at]
            scores, query_levels, key_levels = span_scores(queries, keys, factors, masks, diagonal)
            scores_low = scores.astype(bf16)
            whole = factors[:SPAN]
            after = factors[(KINDS - 1) * SPAN :]

            mixed = mixture[rows, mixed_cols].astype(f32)
            inverse = lax.rsqrt(jnp.mean(mixed * mixed, axis=-1, keepdims=True) + head_epsilon)
            unit = mixed * inverse
            sigmoid = jax.nn.sigmoid(gating)
            silu = gating * sigmoid
            upstream = grad_gated[rows, mixed_cols].astype(f32) * live_part
            grad_projected[rows, gate_cols] = (
                upstream * unit * head_gain * (sigmoid + silu * (1.0 - sigmoid))
            ).astype(bf16)
            normed_back = upstream * silu
            gain_part = normed_back * unit
            packed[BIAS_ROWS, gain_at] += jnp.sum(gain_part.reshape(SPAN // 8, 8, VDIM), axis=0)
            scaled = normed_back * head_gain
            inner = jnp.mean(scaled * unit, axis=-1, keepdims=True)
            grad_mixed = (inverse * (scaled - unit * inner)).astype(bf16)

            entering = states[part, head]
            leaving = grad_state[head]
            leaving_low = leaving.astype(bf16)
            grad_scores = nt(grad_mixed, values)
            after_keys = (keys * after).astype(bf16)
            whole_queries = (queries * whole).astype(bf16)
            grad_projected[rows, value_cols] = (
                tn(scores_low, grad_mixed) + nt(after_keys, leaving_low)
            ).astype(bf16)
            grad_queries = whole * nn(grad_mixed, entering)
            grad_keys = after * nn(values, leaving_low)
            fading = whole[SPAN - 1 :]
            last_sum = fading * jnp.sum(entering.astype(f32) * leaving, axis=0, keepdims=True)
            exponents_head = [queries * grad_queries + jnp.where(last_row, last_sum, 0.0)]
            last_exponent = keys * grad_keys
            for level in range(LEVELS):
                factor = factors[(level + 1) * SPAN : (level + 2) * SPAN]
                level_back = jnp.where(masks[level], grad_scores, 0.0).astype(bf16)
                query_part = factor * nn(level_back, key_levels[level])
                key_part = factor * tn(level_back, query_levels[level])
                grad_queries += query_part
                grad_keys += key_part
                exponents_head.append(queries * query_part + keys * key_part)
            exponents_head.append(last_exponent)
            same = jnp.sum(jnp.where(diagonal, grad_scores, 0.0), axis=1, keepdims=True)
            grad_projected[rows, keys_at] = (grad_queries + same * keys).astype(bf16)
            grad_projected[rows, key_cols] = (grad_keys + same * queries).astype(bf16)
            exponents.append(jnp.concatenate(exponents_head, axis=0).astype(bf16))
            grad_state[head] = keep * (leaving * fading + tn(grad_mixed, whole_queries))
        grad_decays = tn(sums[:, :SPAN], jnp.concatenate(exponents, axis=1))
        grad_z = grad_decays * jax.nn.sigmoid(-z_part) * (1.0 / gate_scale)
        grad_bias[...] += jnp.sum(grad_z.reshape(SPAN // 8, 8, key_width), axis=0)
        grad_z_low = grad_z.astype(bf16)
        grad_up[...] += tn(latent[rows, :LOWRANK], grad_z_low)
        latent_cols = slice(2 * key_width + 2 * value_width, grad_projected.shape[1])
        grad_projected[rows, latent_cols] = nt(grad_z_low, up[...]).astype(bf16)

    latent_at = 2 * key_width + 2 * value_width
    packed[DOWN_ROWS, :] += tn(grad_projected[:, latent_at : latent_at + LOWRANK], normed[...])

    for half in range(2):

        @pl.when((step == pl.num_programs(0) - 1) & (scal[0] == half))
        def _(at=slice(half * key_width, (half + 1) * key_width)):
            packed[UP_ROWS, at] = grad_up[...]
            packed[BIAS_ROWS, at] = grad_bias[...]


def mixer_specs(length, projected_width, key_width, value_width, width, reverse):
    steps = length // (SPAN * STEP_SPANS)
    step_rows = SPAN * STEP_SPANS
    heads = key_width // KDIM

    def natural(step):
        return steps - 1 - step if reverse else step

    def by_rows(step, scal):
        return (lax.rem(natural(step) + scal[0] * (steps // 2), steps), 0)

    def whole(step, scal):
        return (0, 0)

    return dict(
        steps=steps,
        projected=pl.BlockSpec((step_rows, projected_width), by_rows),
        z=pl.BlockSpec((step_rows, key_width), by_rows),
        live=pl.BlockSpec((step_rows, 1), by_rows),
        gain=pl.BlockSpec((1, VDIM), whole),
        sums=pl.BlockSpec((KINDS * SPAN, 2 * SPAN), whole),
        values=pl.BlockSpec((step_rows, value_width), by_rows),
        states=pl.BlockSpec(
            (STEP_SPANS, heads, VDIM, KDIM), lambda step, scal: (natural(step), 0, 0, 0)
        ),
        normed=pl.BlockSpec((step_rows, width), by_rows),
        feed_gain=pl.BlockSpec((1, width), whole),
        packed=pl.BlockSpec((PACKED_ROWS, width), whole),
        latent=pl.BlockSpec((step_rows, LANES), by_rows),
        up=pl.BlockSpec((LANES, key_width), whole),
        extended=pl.BlockSpec((step_rows, projected_width + LANES), by_rows),
    )


def mixer_forward(scal, projected, z, live, gain, sums):
    length, projected_width = projected.shape
    key_width = z.shape[1]
    heads = key_width // KDIM
    value_width = heads * VDIM
    spans = length // SPAN
    specs = mixer_specs(length, projected_width, key_width, value_width, LANES, False)
    return pl.pallas_call(
        functools.partial(forward_kernel, heads),
        grid_spec=pltpu.PrefetchScalarGridSpec(
            num_scalar_prefetch=1,
            grid=(specs["steps"],),
            in_specs=[specs[name] for name in ("projected", "z", "live", "gain", "sums")],
            out_specs=[specs[name] for name in ("values", "values", "states")],
            scratch_shapes=[pltpu.VMEM((heads, VDIM, KDIM), f32)],
        ),
        out_shape=[
            jax.ShapeDtypeStruct((length, value_width), bf16),
            jax.ShapeDtypeStruct((length, value_width), bf16),
            jax.ShapeDtypeStruct((spans, heads, VDIM, KDIM), bf16),
        ],
        compiler_params=pltpu.CompilerParams(vmem_limit_bytes=40 * 1024 * 1024),
        cost_estimate=pl.CostEstimate(
            flops=10**10, bytes_accessed=15 * 10**6, transcendentals=4 * 10**6
        ),
        name="mixer_forward",
    )(scal, projected, z, live, gain, sums)


def mixer_backward(
    scal,
    projected,
    z,
    live,
    gain,
    sums,
    mixture,
    states,
    grad_gated,
    latent,
    up,
    normed,
    feed_gain_grad,
):
    length, projected_width = projected.shape
    key_width = z.shape[1]
    heads = key_width // KDIM
    value_width = heads * VDIM
    width = normed.shape[1]
    specs = mixer_specs(length, projected_width, key_width, value_width, width, True)
    names = ("projected", "z", "live", "gain", "sums", "values", "states", "values")
    names += ("latent", "up", "normed", "feed_gain")
    return pl.pallas_call(
        functools.partial(backward_kernel, heads),
        grid_spec=pltpu.PrefetchScalarGridSpec(
            num_scalar_prefetch=1,
            grid=(specs["steps"],),
            in_specs=[specs[name] for name in names],
            out_specs=[specs[name] for name in ("extended", "packed")],
            scratch_shapes=[
                pltpu.VMEM((LOWRANK, key_width), f32),
                pltpu.VMEM((8, key_width), f32),
                pltpu.VMEM((heads, VDIM, KDIM), f32),
            ],
        ),
        out_shape=[
            jax.ShapeDtypeStruct((length, projected_width + LANES), bf16),
            jax.ShapeDtypeStruct((PACKED_ROWS, width), f32),
        ],
        compiler_params=pltpu.CompilerParams(vmem_limit_bytes=40 * 1024 * 1024),
        cost_estimate=pl.CostEstimate(
            flops=25 * 10**9, bytes_accessed=20 * 10**6, transcendentals=4 * 10**6
        ),
        name="mixer_backward",
    )(
        scal,
        projected,
        z,
        live,
        gain,
        sums,
        mixture,
        states,
        grad_gated,
        latent,
        up,
        normed,
        feed_gain_grad,
    )


def unpack_kernel(packed, *parts):
    width = parts[0].shape[1]
    for index, part in enumerate(parts):
        part[...] = packed[:, index * width : (index + 1) * width].astype(f32)


def unpack_thirds(packed):
    rows, width = packed.shape[0], packed.shape[1] // 3
    return pl.pallas_call(
        unpack_kernel,
        out_shape=[jax.ShapeDtypeStruct((rows, width), f32)] * 3,
        compiler_params=pltpu.CompilerParams(vmem_limit_bytes=8 * 1024 * 1024),
        cost_estimate=pl.CostEstimate(
            flops=UNPACK_FLOPS, bytes_accessed=3 * 10**6, transcendentals=0
        ),
        name="unpack_thirds",
    )(packed)


def lane_pad(values, axis):
    widths = [(0, 0), (0, 0)]
    widths[axis] = (0, LANES - values.shape[axis])
    return jnp.pad(values, widths)


def swap_tensor(values):
    return lax.ppermute(values, "tensor", [(0, 1), (1, 0)])


def chip_sum(values):
    count = lax.axis_size("dp")
    parity = lax.axis_index("dp") % 2
    blocks = values.reshape(count // 2, 2, values.shape[0] // count, values.shape[1])
    kept = lax.dynamic_index_in_dim(blocks, parity, 1, keepdims=False)
    sent = lax.dynamic_index_in_dim(blocks, 1 - parity, 1, keepdims=False)
    arrived = lax.ppermute(sent, "dp", [(i, i ^ 1) for i in range(count)])
    total = (kept.astype(f32) + arrived.astype(f32)).astype(bf16)
    return total.reshape(values.shape[0] // 2, values.shape[1])


def halving_stages():
    return (lax.axis_size("dp") // 2).bit_length() - 1


def by_chip(values):
    stages = halving_stages()
    return values.reshape((2,) * stages + (values.shape[0] >> stages, values.shape[1]))


def halving_stage(held, stage):
    count = lax.axis_size("dp")
    stages = halving_stages()
    bit = 2 << stage
    side = (lax.axis_index("dp") // bit) % 2
    axis = stages - 1 - stage
    kept = lax.dynamic_index_in_dim(held, side, axis, keepdims=False)
    sent = lax.dynamic_index_in_dim(held, 1 - side, axis, keepdims=False)
    arrived = lax.ppermute(sent, "dp", [(i, i ^ bit) for i in range(count)])
    total = kept.astype(f32) + arrived.astype(f32)
    return total if stage == stages - 1 else total.astype(bf16)


def halving_rest(held, first):
    for stage in range(first, halving_stages()):
        held = halving_stage(held, stage)
    return held


def both_ways(side, mine, other, axis):
    first = jnp.where(side == 0, mine, other)
    second = jnp.where(side == 0, other, mine)
    return jnp.stack([first, second], axis=axis)


def swap_half(values):
    half = values.shape[0] // 2
    parity = lax.axis_index("dp") % 2
    return swap_tensor(lax.dynamic_slice_in_dim(values, parity * half, half, 0))


def join_halves(mine):
    count = lax.axis_size("dp")
    parity = lax.axis_index("dp") % 2
    other = lax.ppermute(mine, "dp", [(i, i ^ 1) for i in range(count)])
    return both_ways(parity, mine, other, 0).reshape(mine.shape[0] * 2, mine.shape[1])


def butterfly_sum(values):
    count = lax.axis_size("dp")
    reaches = [1 << bit for bit in range(count.bit_length() - 1)]
    total = values
    for reach in reaches[:1] + reaches[2:] + reaches[1:2]:
        low = total.astype(bf16)
        arrived = lax.ppermute(low, "dp", [(i, i ^ reach) for i in range(count)])
        total = low.astype(f32) + arrived.astype(f32)
    low = total.astype(bf16)
    return low.astype(f32) + swap_tensor(low).astype(f32)


def on_device(
    tokens,
    cotangent,
    sequence_lengths,
    sequence_group,
    sequence_offset,
    mixer_gain,
    query_weight,
    key_weight,
    value_weight,
    output_gate,
    output_weight,
    decay_down,
    decay_up,
    decay_bias,
    head_gain,
    feed_gain,
    feed_gate,
    feed_up,
    feed_down,
):
    which_group = lax.axis_index("dp")
    half_index = lax.axis_index("tensor")
    own = tokens.shape[0]
    group_rows = own * 2
    key_width = query_weight.shape[1]
    value_width = value_weight.shape[1]
    feed_width = feed_gate.shape[1]
    places = (jnp.arange(group_rows, dtype=jnp.int32) + half_index * own) % group_rows
    live_mask, restart = group_layout(
        sequence_lengths,
        sequence_group,
        sequence_offset,
        which_group,
        places[:, None],
        group_rows // SPAN,
    )
    live = live_mask[:, None]
    scal = jnp.concatenate([half_index.astype(jnp.int32)[None], restart])
    sums = jnp.asarray(np.tile(decay_sums(), (1, 2)), bf16)
    gain_head = head_gain.astype(f32)[None, :]

    joined = lax.all_gather(
        jnp.concatenate(
            [query_weight, key_weight, value_weight, output_gate, output_weight], axis=1
        ),
        "dp",
        axis=0,
        tiled=True,
    )
    feed_all = lax.all_gather(
        jnp.concatenate([feed_gate, feed_up, feed_down], axis=1), "dp", axis=0, tiled=True
    )
    gate_up_full = feed_all[:, : 2 * feed_width]
    feed_down_full = feed_all[:, 2 * feed_width :]
    gain_in = mixer_gain.astype(f32)
    token_values = tokens.astype(f32)
    normed_in, inverse_in = rms_forward(token_values, gain_in)
    normed_low = normed_in.astype(bf16)
    normed_other = swap_tensor(normed_low)
    cotangent_other = swap_tensor(cotangent)
    joined, cotangent_other = lax.optimization_barrier((joined, cotangent_other))
    projected_width = 2 * key_width + 2 * value_width
    joined_in = joined[:, :projected_width]
    output_half = joined[:, projected_width:]
    output_piece = swap_half(output_half)

    normed_all = jnp.concatenate([normed_low, normed_other], axis=0)
    projected = nn(normed_all, joined_in).astype(bf16)
    latent = nn(normed_all, decay_down)
    up_local = lax.dynamic_slice_in_dim(decay_up, half_index * key_width, key_width, 1).astype(f32)
    bias_local = lax.dynamic_slice_in_dim(decay_bias, half_index * key_width, key_width, 0)
    z = jnp.dot(latent, up_local, precision=highest) + bias_local.astype(f32)
    gated, mixture, states = mixer_forward(scal, projected, z, live, gain_head, sums)

    gated, output_piece = lax.optimization_barrier((gated, output_piece))
    output_other = join_halves(output_piece)
    gated_own = gated[:own]
    gated_rest = swap_tensor(gated[own:])
    attended = nt(gated_own, output_half) + nt(gated_rest, output_other)
    middle = token_values + attended
    gain_mid = feed_gain.astype(f32)
    normed_mid, inverse_mid = rms_forward(middle, gain_mid)
    mid_low = normed_mid.astype(bf16)
    mid_other = swap_tensor(mid_low)

    def feed_rows(mid_rows, cotangent_rows):
        both = nn(mid_rows, gate_up_full)
        gate_part = both[:, :feed_width]
        up_part = both[:, feed_width:]
        sigmoid_gate = jax.nn.sigmoid(gate_part)
        silu_gate = gate_part * sigmoid_gate
        hidden_low = (silu_gate * up_part).astype(bf16)
        grad_hidden = nn(cotangent_rows, feed_down_full)
        grad_gate_low = (
            grad_hidden * up_part * (sigmoid_gate + silu_gate * (1.0 - sigmoid_gate))
        ).astype(bf16)
        grad_up_low = (grad_hidden * silu_gate).astype(bf16)
        grad_both = jnp.concatenate([grad_gate_low, grad_up_low], axis=1)
        return hidden_low, grad_both, nt(grad_both, gate_up_full)

    hidden_other, grad_both_other, mid_back_other = feed_rows(mid_other, cotangent_other)
    mid_send, mid_here, cotangent_here = lax.optimization_barrier(
        (mid_back_other.astype(bf16), mid_low, cotangent)
    )
    mid_back = swap_tensor(mid_send)
    hidden_own, grad_both_own, mid_back_own = feed_rows(mid_here, cotangent_here)

    upstream = cotangent.astype(f32)
    grad_normed_mid = mid_back_own + mid_back.astype(f32)
    grad_mid_in, grad_feed_gain = rms_backward(middle, inverse_mid, gain_mid, grad_normed_mid)
    grad_middle = upstream + grad_mid_in
    grad_attended = grad_middle.astype(bf16)
    gated_send, attended_late, hidden_late = lax.optimization_barrier(
        (nn(grad_attended, output_other).astype(bf16), grad_attended, hidden_other)
    )
    gated_back = swap_tensor(gated_send)
    grad_gated = jnp.concatenate([nn(attended_late, output_half).astype(bf16), gated_back], axis=0)
    fed_send = nt(hidden_late, feed_down_full).astype(bf16)
    output_grads = tn(attended_late, jnp.concatenate([gated_own, gated_rest], axis=1)).astype(bf16)
    grad_gated, fed_send, output_grads = lax.optimization_barrier(
        (grad_gated, fed_send, output_grads)
    )
    fed_back = swap_tensor(fed_send)

    mid_all = jnp.concatenate([mid_low, mid_other], axis=0)
    cotangent_all = jnp.concatenate([cotangent, cotangent_other], axis=0)
    hidden_all = jnp.concatenate([hidden_own, hidden_other], axis=0)
    grad_both_all = jnp.concatenate([grad_both_own, grad_both_other], axis=0)
    feed_grads = jnp.concatenate(
        [
            tn(mid_all, grad_both_all).astype(bf16),
            tn(cotangent_all, hidden_all).astype(bf16),
        ],
        axis=1,
    )
    feed_sum = lax.psum_scatter(feed_grads, "dp", scatter_dimension=0, tiled=True)
    grad_projected, packed = mixer_backward(
        scal,
        projected,
        z,
        live,
        gain_head,
        sums,
        mixture,
        states,
        grad_gated,
        lane_pad(latent, 1).astype(bf16),
        lane_pad(up_local, 0).astype(bf16),
        normed_all,
        grad_feed_gain[None, :],
    )
    grad_joined = tn(normed_all, grad_projected).astype(bf16)
    grad_joined, output_grads, fed_back = lax.optimization_barrier(
        (grad_joined, output_grads, fed_back)
    )
    projected_chip, hidden_last, packed = lax.optimization_barrier(
        (chip_sum(grad_joined[:, :projected_width]), hidden_own, packed)
    )
    joined_sums = [
        halving_stage(by_chip(piece), 0) for piece in jnp.split(projected_chip, 2, axis=1)
    ]
    output_chip = chip_sum(output_grads)
    output_back = swap_tensor(output_chip[:, value_width:])
    joined_back = jnp.concatenate([joined_in, lane_pad(decay_down, 1)], axis=1)
    normed_part = nt(grad_projected, joined_back)
    grad_mixer_gain = jnp.sum(normed_part * normed_all.astype(f32), axis=0) / gain_in
    normed_part = normed_part.astype(bf16)
    fed = nt(hidden_last, feed_down_full) + fed_back.astype(f32)
    output = (middle + fed).astype(bf16)
    output_back, _ = lax.optimization_barrier((output_back, joined_sums[0]))
    output_total = output_chip[:, :value_width].astype(f32) + output_back.astype(f32)
    joined_sums.append(halving_stage(by_chip(output_total.astype(bf16)), 0))
    joined_sums = [halving_stage(held, 1) for held in joined_sums]
    normed_back, _ = lax.optimization_barrier((swap_tensor(normed_part[own:]), joined_sums[1]))
    grad_normed = normed_part[:own].astype(f32) + normed_back.astype(f32)
    grad_in_part = rms_backward(token_values, inverse_in, gain_in, grad_normed)[0]
    input_grad = grad_middle + grad_in_part

    flat = lax.dynamic_update_slice_in_dim(packed, grad_mixer_gain[None, :], MIXER_GAIN_ROW, 0)
    flat = butterfly_sum(flat)
    joined_sum = jnp.concatenate([halving_rest(held, 2) for held in joined_sums], axis=1)
    channels = 2 * key_width
    return (
        output,
        input_grad,
        flat[MIXER_GAIN_ROW],
        joined_sum[:, :key_width],
        joined_sum[:, key_width : 2 * key_width],
        joined_sum[:, 2 * key_width : 2 * key_width + value_width],
        joined_sum[:, 2 * key_width + value_width : projected_width],
        joined_sum[:, projected_width:],
        flat[DOWN_ROWS].T,
        flat[UP_ROWS, :channels],
        jnp.sum(flat[BIAS_ROWS, :channels], axis=0),
        jnp.sum(flat[BIAS_ROWS, channels : channels + VDIM], axis=0),
        flat[FEED_GAIN_ROW],
        *unpack_thirds(feed_sum),
    )


def solution(mesh):
    rows = P(("dp", "tensor"), None)
    weight = P("dp", "tensor")
    return jax.shard_map(
        on_device,
        mesh=mesh,
        in_specs=(rows, rows, P(), P(), P(), P())
        + (weight,) * 5
        + (P(), P(), P(), P(), P())
        + (weight,) * 3,
        out_specs=(rows, rows, P()) + (weight,) * 5 + (P(),) * 5 + (weight,) * 3,
        check_vma=False,
    )
```
